128 devices in a mesh: seq: 8 (over y, core), exp: 16 (over z, x).
Axes of the slice: x: 4, y: 4, z: 4, core: 2. Of those that a mesh axis runs over, the one named last changes fastest.
Arguments:
- stream_in: bfloat16 [16, 1024, 2048], P('exp', 'seq'), may hold values from -20 to 20
- qkv_heads: bfloat16 [16, 1024, 3, 2048], P('exp', 'seq'), may hold values from -16 to 16
- expert_ids: int32 [16, 1024, 2], P('exp', 'seq'), may hold values from 0 to 15, all different within a row; in each aligned block of 128 rows (0 to 127, 128 to 255, ..., all dimensions but the last counted through in order) at most 24 rows name the same one
- gate_weights: float32 [16, 1024, 2], P('exp', 'seq'), may hold values from 0.25 to 1
- w_out: bfloat16 [2048, 2048], replicated, may hold values from -0.125 to 0.125
- w_gate: bfloat16 [16, 2048, 4096], P('exp', None, 'seq'), may hold values from -0.125 to 0.125
- w_up: bfloat16 [16, 2048, 4096], P('exp', None, 'seq'), may hold values from -0.125 to 0.125
- w_down: bfloat16 [16, 4096, 2048], P('exp', 'seq'), may hold values from -0.09375 to 0.09375
Outputs:
- block_out: bfloat16 [16, 1024, 2048], P('exp', 'seq')
The draws below stay inside these ranges and needn't reach their ends.
Inputs may be any that keep to these rules, and one draw needn't show every extreme that they name: `expert_ids`: the 2 experts of a token differ. Among the 128 tokens of one device (aligned blocks of 128 tokens along the flattened image and token dimensions) no expert is named more than 24 times, a bound that some block reaches.
All inputs are finite; a program needn't handle non-finite values.
Results may differ from the reference program's by a relative error of at most 0.01.
Values may be sent and summed in bfloat16 or wider, within the bound.
No kernel may reach another device: no remote copies, remote signals or barrier semaphores. Data moves between devices by JAX's collectives and lax.ppermute only.
A program may use at most 128 MiB of HBM per device.

```python
import math
import jax
import jax.numpy as jnp
import numpy as np
from jax import lax

D = 2048
HEADS = 32
HD = 64
FF = 4096
TOP = 2
TOK_DEV = 128
LEN = 1024
IMAGES = 16
EXPERTS = 16
CAP = 24
N_SEQ = 8


def draw_stream_in(key, part):
    key = jax.random.fold_in(key, 5)
    base_key, row_key, col_key = jax.random.split(key, 3)
    shape = (IMAGES, LEN, D)
    row_scale = jnp.exp(jax.random.uniform(row_key, (IMAGES, LEN, 1), jnp.float32, 0.0, math.log(10.0))) * 0.2
    col_scale = jnp.exp(jax.random.uniform(col_key, (1, 1, D), jnp.float32, math.log(0.5), math.log(1.5)))
    base = jnp.clip(jax.random.normal(base_key, shape, jnp.float32), -6.0, 6.0)
    return (base * row_scale * col_scale).astype(jnp.bfloat16)


def draw_qkv_heads(key, part):
    key = jax.random.fold_in(key, 11)
    base_key = jax.random.fold_in(key, 0)
    shape = (IMAGES, LEN, 3, D)
    result = jnp.clip(jax.random.normal(base_key, shape, jnp.float32), -6.0, 6.0)
    return result.astype(jnp.bfloat16)


def level_of(key, shape, pieces, low, largest):
    def one(dim, blocks):
        steps = jax.random.uniform(jax.random.fold_in(jax.random.fold_in(key, 6), dim), (blocks,), jnp.float32, low / len(pieces), largest / len(pieces))
        return jnp.repeat(jnp.exp(steps), shape[dim] // blocks).reshape((-1,) + (1,) * (len(shape) - dim - 1))

    factor_of = one(*pieces[0])
    for cut in pieces[1:]:
        factor_of = factor_of * one(*cut)
    return factor_of


def routed_block(own_key, own, number, rows, count, top, reach, skew):
    order = jax.random.permutation(own_key, count)
    crowded, ordinary = portions_of(count, rows * top, reach, skew, True), portions_of(count, rows * top, reach, skew, False)
    places = jnp.arange(count)

    def named(lengths, rotation):
        used = int((lengths > 0).sum())
        fixed = max(1, used // 4)
        moved = fixed + (places - fixed + rotation * (used - fixed)) % max(1, count - fixed)
        return jnp.zeros((count,), jnp.int32).at[order[jnp.where(places < fixed, places, moved)]].set(jnp.asarray(lengths, jnp.int32))

    lengths = jnp.where(number % 4 == 0, named(crowded, number // 4), named(ordinary, number - number // 4 - 1))
    mixed = jax.random.permutation(jax.random.fold_in(own, 3), count)
    giver, sink = mixed[0:count // 2 * 2:2], mixed[1:count // 2 * 2:2]
    slack = jnp.minimum(lengths[giver] - 1, reach - lengths[sink]) // 2
    slack = jnp.where((giver == order[0]) | (sink == order[0]) | (lengths[sink] == 0), 0, jnp.maximum(slack, 0))
    moved = jax.random.randint(jax.random.fold_in(own, 4), (count // 2,), 0, 1 << 20) % (slack + 1)
    lengths = lengths.at[giver].add(-moved).at[sink].add(moved)
    items = jnp.searchsorted(jnp.cumsum(lengths), jnp.arange(rows * top), side="right").astype(jnp.int32)
    table = items.reshape(top, rows).T
    table = table[jax.random.permutation(jax.random.fold_in(own, 1), rows)]
    rotation = jax.random.randint(jax.random.fold_in(own, 2), (rows, 1), 0, top)
    return jnp.take_along_axis(table, (jnp.arange(top)[None, :] + rotation) % top, axis=1)


def portions_of(count, total, limit, skew, full):
    loads = [(1 << 20) // math.isqrt(rank ** skew) + 1 for rank in range(1, count + 1)]
    largest = limit if full else min(limit, max(-(-total // count), total * loads[0] // sum(loads)))
    least = 1 if total - largest >= count - 1 else 0
    counts, spare = [largest] + [least] * (count - 1), total - largest - least * (count - 1)
    while spare > 0:
        movable = [i for i in range(1, count) if counts[i] < largest] or [i for i in range(1, count) if counts[i] < limit]
        whole, remaining = sum([loads[i] for i in movable]), spare
        for i in movable:
            addition = min(limit - counts[i], max(1, remaining * loads[i] // whole), spare)
            counts[i] = counts[i] + addition
            spare = spare - addition
    return np.array(counts)


def noise(own_key, shape, deviation, bound, cuts=(), kind=jnp.bfloat16):
    drawn = deviation * jax.random.normal(own_key, shape, jnp.float32)
    if cuts:
        drawn = drawn * level_of(own_key, shape, cuts, -0.22, 0.18)
    return jnp.clip(drawn, -bound, bound).astype(kind)


def setup_inputs(seed: int = 0) -> dict:
    splits = jax.random.split(jax.random.key(seed), 9)
    stream_in = draw_stream_in(jax.random.fold_in(splits[8], 71), 0)
    qkv_heads = draw_qkv_heads(jax.random.fold_in(splits[8], 71), 0)
    expert_ids_keys = jax.random.split(jax.random.fold_in(splits[2], 1), IMAGES * LEN // TOK_DEV)
    expert_ids_turns = jax.random.permutation(jax.random.fold_in(splits[2], 3), IMAGES * LEN // TOK_DEV)
    expert_ids = jax.vmap(lambda own, number: routed_block(jax.random.fold_in(splits[2], 2), own, number, TOK_DEV, EXPERTS, TOP, CAP, 2))(expert_ids_keys, expert_ids_turns).reshape((IMAGES, LEN, TOP))
    gate_weights = jnp.clip(0.25 + 0.75 * jax.random.uniform(splits[3], (IMAGES, LEN, TOP), jnp.float32) ** level_of(splits[3], (IMAGES, LEN, TOP), ((0, 16), (1, 8)), -0.2, 0.2), 0.25, 1.0)
    w_out = noise(splits[4], (D, D), D ** -0.5, 0.125)
    w_gate = noise(splits[5], (EXPERTS, D, FF), D ** -0.5, 0.125, ((0, 16), (2, 8)))
    w_up = noise(splits[6], (EXPERTS, D, FF), D ** -0.5, 0.125, ((0, 16), (2, 8)))
    w_down = noise(splits[7], (EXPERTS, FF, D), FF ** -0.5, 0.09375, ((0, 16), (1, 8)))
    return {"stream_in": stream_in, "qkv_heads": qkv_heads, "expert_ids": expert_ids, "gate_weights": gate_weights, "w_out": w_out, "w_gate": w_gate, "w_up": w_up, "w_down": w_down}


def attend_image(block):
    scale = float(HD) ** (-0.5)
    query = block[:, 0].reshape(LEN, HEADS, HD).transpose(1, 0, 2)
    keys = block[:, 1].reshape(LEN, HEADS, HD).transpose(1, 0, 2)
    values = block[:, 2].reshape(LEN, HEADS, HD).transpose(1, 0, 2)

    def one_head(parts):
        q_head, k_head, v_head = parts
        scores = jnp.dot(q_head, k_head.T, preferred_element_type=jnp.float32) * scale
        top = lax.optimization_barrier(jnp.max(scores, axis=1, keepdims=True))
        weights = jnp.exp(scores - top)
        probs = (weights / lax.optimization_barrier(jnp.sum(weights, axis=1, keepdims=True))).astype(jnp.bfloat16)
        return jnp.dot(probs, v_head, preferred_element_type=jnp.float32).astype(jnp.bfloat16)
    context = lax.map(one_head, (query, keys, values))
    return context.transpose(1, 0, 2).reshape(LEN, D)

def reference(stream_in, qkv_heads, expert_ids, gate_weights, w_out, w_gate, w_up, w_down):
    context = lax.map(attend_image, qkv_heads).reshape(IMAGES * LEN, D)
    mid = stream_in.reshape(IMAGES * LEN, D).astype(jnp.float32) + jnp.dot(context, w_out, preferred_element_type=jnp.float32)
    normed = (mid * lax.rsqrt(lax.optimization_barrier(jnp.mean(mid * mid, axis=1, keepdims=True)) + 1e-06)).astype(jnp.bfloat16)
    blocks = IMAGES * LEN // TOK_DEV
    assigned = TOK_DEV * TOP
    flat_ids = expert_ids.reshape(blocks, assigned).astype(jnp.int32)
    onehot = (flat_ids[:, :, None] == jnp.arange(EXPERTS, dtype=jnp.int32)[None, None, :]).astype(jnp.int32)
    rank = jnp.cumsum(onehot, axis=1) - onehot
    slot = lax.optimization_barrier(jnp.sum(rank * onehot, axis=2)).astype(jnp.int32)
    destination = flat_ids * CAP + slot
    sources = jnp.repeat(normed, TOP, axis=0).reshape(blocks, assigned, D)
    block_index = jnp.broadcast_to(jnp.arange(blocks, dtype=jnp.int32)[:, None], (blocks, assigned))
    buffer = jnp.zeros((blocks, EXPERTS * CAP, D), jnp.bfloat16).at[block_index, destination].set(sources)
    per_expert = buffer.reshape(blocks, EXPERTS, CAP, D).transpose(1, 0, 2, 3).reshape(EXPERTS, blocks * CAP, D)
    slice_width = FF // N_SEQ

    def run_expert(parts):
        rows, gate_mat, up_mat, down_mat = parts
        gate = jnp.dot(rows, gate_mat, preferred_element_type=jnp.float32)
        up_value = jnp.dot(rows, up_mat, preferred_element_type=jnp.float32)
        hidden = (jax.nn.silu(gate) * up_value).astype(jnp.bfloat16)
        total = jnp.zeros((rows.shape[0], D), jnp.float32)
        for share in range(N_SEQ):
            lower = share * slice_width
            partial_term = jnp.dot(hidden[:, lower:lower + slice_width], down_mat[lower:lower + slice_width], preferred_element_type=jnp.float32)
            rounded = lax.optimization_barrier(partial_term.astype(jnp.bfloat16))
            total = total + rounded.astype(jnp.float32)
        return total
    results = lax.map(run_expert, (per_expert, w_gate, w_up, w_down)).reshape(EXPERTS, blocks, CAP, D)
    picked = results[flat_ids, block_index, slot]
    moe = lax.optimization_barrier(jnp.sum(picked.reshape(IMAGES * LEN, TOP, D) * gate_weights.reshape(IMAGES * LEN, TOP)[:, :, None], axis=1))
    return (mid + moe).astype(jnp.bfloat16).reshape(IMAGES, LEN, D)
```

```python
import functools

import jax
import jax.numpy as jnp
from jax import lax
from jax.experimental import pallas as pl
from jax.experimental.pallas import tpu as pltpu
from jax.sharding import Mesh
from jax.sharding import PartitionSpec as P

HD = 64
LANES = 128
MIB = 1 << 20
BF16 = jnp.bfloat16
F32 = jnp.float32
LOG2E = 1.4426950408889634
NUM_CHUNKS = 3


def vmem(shape):
    return pl.BlockSpec(shape, lambda *_: (0,) * len(shape))


def attention_kernel(x_ref, out_ref, *, block):
    n_src, _, rows, lanes = x_ref.shape
    length = n_src * rows
    keys = x_ref[:, 1].reshape(length, lanes)
    values = x_ref[:, 2].reshape(length, lanes)
    wide = jnp.concatenate([values, jnp.ones((length, lanes), BF16)], axis=1)
    lane = lax.broadcasted_iota(jnp.int32, (1, lanes), 1)
    first = lane < HD
    scale = float(HD) ** (-0.5) * LOG2E
    per = block // rows
    for i in range(length // block):
        query = x_ref[i * per : (i + 1) * per, 0].reshape(block, lanes)
        parts = []
        for head in range(2):
            mine = jnp.where(first if head == 0 else ~first, query, jnp.zeros_like(query))
            scores = lax.dot_general(
                mine, keys, (((1,), (1,)), ((), ())), preferred_element_type=F32
            )
            top = jnp.max(scores, axis=1, keepdims=True)
            weights = jnp.exp2((scores - top) * scale).astype(BF16)
            both = jnp.dot(weights, wide, preferred_element_type=F32)
            parts.append(both[:, :lanes] / both[:, lanes:])
        context = jnp.where(first, parts[0], parts[1]).astype(BF16)
        out_ref[i * per : (i + 1) * per] = context.reshape(per, rows, lanes)


def attention(arrived):
    n_src, three, rows, width = arrived.shape
    return pl.pallas_call(
        functools.partial(attention_kernel, block=2 * rows),
        grid=(width // LANES,),
        in_specs=[pl.BlockSpec((n_src, three, rows, LANES), lambda i: (0, 0, 0, i))],
        out_specs=pl.BlockSpec((n_src, rows, LANES), lambda i: (0, 0, i)),
        out_shape=jax.ShapeDtypeStruct((n_src, rows, width), BF16),
        compiler_params=pltpu.CompilerParams(vmem_limit_bytes=40 * MIB),
        name="attention",
    )(arrived)


def places(ids, n_exp, piece):
    tokens = ids.shape[1]
    expert = lax.broadcasted_iota(jnp.int32, (n_exp, tokens), 0)
    named = [expert == ids[k : k + 1] for k in range(ids.shape[0])]
    member = sum(n.astype(F32) for n in named)
    before = (
        lax.broadcasted_iota(jnp.int32, (tokens, tokens), 0)
        < lax.broadcasted_iota(jnp.int32, (tokens, tokens), 1)
    ).astype(BF16)
    rank = jnp.dot(member.astype(BF16), before, preferred_element_type=F32)
    rows = []
    for k, n in enumerate(named):
        slot = jnp.sum(jnp.where(n, rank, 0.0), axis=0, keepdims=True).astype(jnp.int32)
        chunk = slot // piece
        rows.append(chunk * (n_exp * piece) + ids[k : k + 1] * piece + (slot - chunk * piece))
    return rows


def project_kernel(ctx_ref, w_ref, stream_ref, ids_ref, mid_ref, *out_refs, n_exp, piece):
    n_src = ctx_ref.shape[0]
    merged = jnp.concatenate([ctx_ref[s] for s in range(n_src)], axis=1)
    step = pl.program_id(0)
    cols = w_ref.shape[1]
    here = pl.ds(pl.multiple_of(step * cols, cols), cols)
    mid_ref[:, here] = stream_ref[...].astype(F32) + jnp.dot(
        merged, w_ref[...], preferred_element_type=F32
    )

    @pl.when(step == pl.num_programs(0) - 1)
    def _():
        mid = mid_ref[...]
        factor = lax.rsqrt(jnp.mean(mid * mid, axis=1, keepdims=True) + 1e-06)
        normed = (mid * factor).astype(BF16)
        rows = places(ids_ref[...], n_exp, piece)
        slots = n_exp * piece
        for c, ref in enumerate(out_refs):
            at = lax.broadcasted_iota(jnp.int32, (slots, normed.shape[0]), 0) + c * slots
            pick = sum((at == r).astype(F32) for r in rows).astype(BF16)
            ref[...] = jnp.dot(pick, normed, preferred_element_type=F32).astype(BF16)


def project(merged, w_out, stream, ids, n_exp, piece, n_chunks):
    n_src, rows, part = merged.shape
    width = w_out.shape[1]
    cols = 512
    slots = n_exp * piece
    return pl.pallas_call(
        functools.partial(project_kernel, n_exp=n_exp, piece=piece),
        grid=(width // cols,),
        in_specs=[
            vmem((n_src, rows, part)),
            pl.BlockSpec((width, cols), lambda i: (0, i)),
            pl.BlockSpec((rows, cols), lambda i: (0, i)),
            vmem(ids.shape),
        ],
        out_specs=[vmem((rows, width))] + [vmem((slots, width))] * n_chunks,
        out_shape=[jax.ShapeDtypeStruct((rows, width), F32)]
        + [jax.ShapeDtypeStruct((slots, width), BF16)] * n_chunks,
        compiler_params=pltpu.CompilerParams(vmem_limit_bytes=40 * MIB),
        name="project",
    )(merged, w_out, stream, ids)


def expert_kernel(x_ref, g0, g1, u0, u1, d0, d1, out_ref):
    rows = x_ref[...]
    total = None
    for gate_ref, up_ref, down_ref in ((g0, u0, d0), (g1, u1, d1)):
        gate = jnp.dot(rows, gate_ref[...], preferred_element_type=F32)
        up = jnp.dot(rows, up_ref[...], preferred_element_type=F32)
        hidden = (gate / (1.0 + jnp.exp(-gate)) * up).astype(BF16)
        term = jnp.dot(hidden, down_ref[...], preferred_element_type=F32)
        total = term if total is None else total + term
    out_ref[...] = total.astype(BF16)


def experts(rows, gates, ups, downs):
    n, width = rows.shape
    block = 256
    full = [vmem(w.shape) for w in (*gates, *ups, *downs)]
    return pl.pallas_call(
        expert_kernel,
        grid=(n // block,),
        in_specs=[pl.BlockSpec((block, width), lambda i: (i, 0))] + full,
        out_specs=pl.BlockSpec((block, width), lambda i: (i, 0)),
        out_shape=jax.ShapeDtypeStruct((n, width), BF16),
        compiler_params=pltpu.CompilerParams(vmem_limit_bytes=56 * MIB),
        name="experts",
    )(rows, *gates, *ups, *downs)


def combine_kernel(mid_ref, ids_ref, weight_ref, *refs, n_exp, piece):
    *back_refs, out_ref = refs
    rows = places(ids_ref[...], n_exp, piece)
    slots = n_exp * piece
    back = jnp.concatenate([r[...] for r in back_refs], axis=0)
    total = mid_ref[...]
    at = lax.broadcasted_iota(jnp.int32, (back.shape[0], rows[0].shape[1]), 0)
    for k, row in enumerate(rows):
        pick = (at == row).astype(F32).astype(BF16)
        term = lax.dot_general(pick, back, (((0,), (0,)), ((), ())), preferred_element_type=F32)
        total = total + term * weight_ref[:, k : k + 1]
    out_ref[...] = total.astype(BF16)


def combine(mid, ids, weights, backs, n_exp, piece):
    rows, width = mid.shape
    cols = 512
    slots = n_exp * piece
    return pl.pallas_call(
        functools.partial(combine_kernel, n_exp=n_exp, piece=piece),
        grid=(width // cols,),
        in_specs=[
            pl.BlockSpec((rows, cols), lambda i: (0, i)),
            vmem(ids.shape),
            vmem(weights.shape),
        ]
        + [pl.BlockSpec((slots, cols), lambda i: (0, i))] * len(backs),
        out_specs=pl.BlockSpec((rows, cols), lambda i: (0, i)),
        out_shape=jax.ShapeDtypeStruct((rows, width), BF16),
        compiler_params=pltpu.CompilerParams(vmem_limit_bytes=40 * MIB),
        name="combine",
    )(mid, ids, weights, *backs)


def per_device(stream_in, qkv_heads, expert_ids, gate_weights, w_out, w_gate, w_up, w_down):
    rows, width = stream_in.shape[1:]
    seq, exp = ("y", "core"), ("z", "x")
    n_seq, n_exp = lax.axis_size(seq), lax.axis_size(exp)
    capacity = 3 * expert_ids.shape[2] * rows // (2 * n_exp)
    piece = capacity // NUM_CHUNKS
    swap = [(0, 1), (1, 0)]
    gates, ups, downs = (
        (w[0], lax.ppermute(w[0], "core", swap)) for w in (w_gate, w_up, w_down)
    )
    ids = expert_ids[0].T
    qkv = qkv_heads[0].transpose(1, 0, 2).reshape(3, rows, n_seq, width // n_seq)
    qkv = qkv.transpose(2, 0, 1, 3)
    arrived = lax.all_to_all(qkv, seq, split_axis=0, concat_axis=0, tiled=True)
    context = attention(arrived)
    merged = lax.all_to_all(context, seq, split_axis=0, concat_axis=0, tiled=True)
    mid, *buffers = project(merged, w_out, stream_in[0], ids, n_exp, piece, NUM_CHUNKS)
    backs = []
    for buffer in buffers:
        sent = lax.all_to_all(buffer, exp, split_axis=0, concat_axis=0, tiled=True)
        gathered = lax.all_gather(sent, "y", tiled=True)
        shares = experts(gathered, gates, ups, downs)
        summed = lax.psum_scatter(shares, "y", scatter_dimension=0, tiled=True)
        backs.append(lax.all_to_all(summed, exp, split_axis=0, concat_axis=0, tiled=True))
    return combine(mid, ids, gate_weights[0], backs, n_exp, piece)[None]


def solution(mesh):
    split = Mesh(mesh.devices.reshape(-1, 2, 4, 4), ("y", "core", "z", "x"))
    seq, exp = ("y", "core"), ("z", "x")
    in_specs = (
        P(exp, seq, None),
        P(exp, seq, None, None),
        P(exp, seq, None),
        P(exp, seq, None),
        P(),
        P(exp, None, seq),
        P(exp, None, seq),
        P(exp, seq, None),
    )
    return jax.shard_map(
        per_device, mesh=split, in_specs=in_specs, out_specs=P(exp, seq, None), check_vma=False
    )
```

```python
import functools

import jax
import jax.numpy as jnp
from jax import lax
from jax.experimental import pallas as pl
from jax.experimental.pallas import tpu as pltpu
from jax.sharding import Mesh
from jax.sharding import PartitionSpec as P

HD = 64
LANES = 128
MIB = 1 << 20
BF16 = jnp.bfloat16
F32 = jnp.float32
LOG2E = 1.4426950408889634
TOP = 2


def vmem(shape):
    return pl.BlockSpec(shape, lambda *_: (0,) * len(shape))


def attention_kernel(x_ref, out_ref, *, block):
    n_src, _, rows, lanes = x_ref.shape
    length = n_src * rows
    keys = x_ref[:, 1].reshape(length, lanes)
    values = x_ref[:, 2].reshape(length, lanes)
    wide = jnp.concatenate([values, jnp.ones((length, lanes), BF16)], axis=1)
    lane = lax.broadcasted_iota(jnp.int32, (1, lanes), 1)
    first = lane < HD
    scale = float(HD) ** (-0.5) * LOG2E
    per = block // rows
    for i in range(length // block):
        query = x_ref[i * per : (i + 1) * per, 0].reshape(block, lanes)
        parts = []
        for head in range(2):
            mine = jnp.where(first if head == 0 else ~first, query, jnp.zeros_like(query))
            scores = lax.dot_general(
                mine, keys, (((1,), (1,)), ((), ())), preferred_element_type=F32
            )
            top = jnp.max(scores, axis=1, keepdims=True)
            weights = jnp.exp2((scores - top) * scale).astype(BF16)
            both = jnp.dot(weights, wide, preferred_element_type=F32)
            parts.append(both[:, :lanes] / both[:, lanes:])
        context = jnp.where(first, parts[0], parts[1]).astype(BF16)
        out_ref[i * per : (i + 1) * per] = context.reshape(per, rows, lanes)


def attention(arrived):
    n_src, three, rows, width = arrived.shape
    return pl.pallas_call(
        functools.partial(attention_kernel, block=2 * rows),
        grid=(width // LANES,),
        in_specs=[pl.BlockSpec((n_src, three, rows, LANES), lambda i: (0, 0, 0, i))],
        out_specs=pl.BlockSpec((n_src, rows, LANES), lambda i: (0, 0, i)),
        out_shape=jax.ShapeDtypeStruct((n_src, rows, width), BF16),
        compiler_params=pltpu.CompilerParams(vmem_limit_bytes=24 * MIB),
        name="attention",
    )(arrived)


def places(info, n_exp, pieces):
    tokens = info.shape[1]
    ids = info[:TOP].astype(jnp.int32)
    expert = lax.broadcasted_iota(jnp.int32, (n_exp, tokens), 0)
    named = [expert == ids[k : k + 1] for k in range(TOP)]
    member = sum(n.astype(F32) for n in named)
    before = (
        lax.broadcasted_iota(jnp.int32, (tokens, tokens), 0)
        < lax.broadcasted_iota(jnp.int32, (tokens, tokens), 1)
    ).astype(F32)
    rank = jnp.dot(member.astype(BF16), before.astype(BF16), preferred_element_type=F32)
    rows = []
    for k, n in enumerate(named):
        slot = jnp.sum(jnp.where(n, rank, 0.0), axis=0, keepdims=True).astype(jnp.int32)
        row, start = None, 0
        for piece in pieces:
            here = start * n_exp + ids[k : k + 1] * piece + (slot - start)
            row = here if row is None else jnp.where(slot >= start, here, row)
            start += piece
        rows.append(row)
    return rows


def fill(normed, info, out_refs, n_exp, pieces):
    rows = places(info, n_exp, pieces)
    start = 0
    for ref, piece in zip(out_refs, pieces, strict=True):
        slots = n_exp * piece
        at = lax.broadcasted_iota(jnp.int32, (slots, normed.shape[0]), 0) + start
        pick = sum((at == r).astype(F32) for r in rows).astype(BF16)
        ref[...] = jnp.dot(pick, normed, preferred_element_type=F32).astype(BF16)
        start += slots


def project_kernel(ctx_ref, w_ref, stream_ref, info_ref, mid_ref, normed_ref, *out_refs, n_exp, pieces):
    n_src = ctx_ref.shape[0]
    merged = jnp.concatenate([ctx_ref[s] for s in range(n_src)], axis=1)
    step = pl.program_id(0)
    cols = w_ref.shape[1]
    here = pl.ds(pl.multiple_of(step * cols, cols), cols)
    mid_ref[:, here] = stream_ref[...].astype(F32) + jnp.dot(
        merged, w_ref[...], preferred_element_type=F32
    )

    @pl.when(step == pl.num_programs(0) - 1)
    def _():
        mid = mid_ref[...]
        factor = lax.rsqrt(jnp.mean(mid * mid, axis=1, keepdims=True) + 1e-06)
        normed = (mid * factor).astype(BF16)
        normed_ref[...] = normed
        fill(normed, info_ref[...], out_refs, n_exp, pieces)


def project(merged, w_out, stream, info, n_exp, pieces):
    n_src, rows, part = merged.shape
    width = w_out.shape[1]
    cols = 512
    slots = [n_exp * p for p in pieces]
    return pl.pallas_call(
        functools.partial(project_kernel, n_exp=n_exp, pieces=pieces),
        grid=(width // cols,),
        in_specs=[
            vmem((n_src, rows, part)),
            pl.BlockSpec((width, cols), lambda i: (0, i)),
            pl.BlockSpec((rows, cols), lambda i: (0, i)),
            vmem(info.shape),
        ],
        out_specs=[vmem((rows, width))] * 2 + [vmem((s, width)) for s in slots],
        out_shape=[
            jax.ShapeDtypeStruct((rows, width), F32),
            jax.ShapeDtypeStruct((rows, width), BF16),
        ]
        + [jax.ShapeDtypeStruct((s, width), BF16) for s in slots],
        compiler_params=pltpu.CompilerParams(vmem_limit_bytes=32 * MIB),
        name="project",
    )(merged, w_out, stream, info)


def route_kernel(normed_ref, info_ref, *out_refs, n_exp, pieces):
    fill(normed_ref[...], info_ref[...], out_refs, n_exp, pieces)


def route(normed, info, n_exp, pieces):
    rows, width = normed.shape
    slots = [n_exp * p for p in pieces]
    return pl.pallas_call(
        functools.partial(route_kernel, n_exp=n_exp, pieces=pieces),
        grid=(1,),
        in_specs=[vmem(normed.shape), vmem(info.shape)],
        out_specs=[vmem((s, width)) for s in slots],
        out_shape=[jax.ShapeDtypeStruct((s, width), BF16) for s in slots],
        compiler_params=pltpu.CompilerParams(vmem_limit_bytes=24 * MIB),
        name="route",
    )(normed, info)


def expert_kernel(*refs, n_in):
    x_refs, w_refs = refs[:n_in], refs[n_in : n_in + 6]
    out_refs, (rows_ref, total_ref) = refs[n_in + 6 : -2], refs[-2:]
    step, steps = pl.program_id(0), pl.num_programs(0)

    @pl.when(step == 0)
    def _():
        start = 0
        for ref in x_refs:
            rows_ref[start : start + ref.shape[0]] = ref[...]
            start += ref.shape[0]

    def part(gate_ref, up_ref, down_ref):
        rows = rows_ref[...]
        gate = jnp.dot(rows, gate_ref[...], preferred_element_type=F32)
        up = jnp.dot(rows, up_ref[...], preferred_element_type=F32)
        hidden = (gate / (1.0 + jnp.exp(-gate)) * up).astype(BF16)
        return jnp.dot(hidden, down_ref[...], preferred_element_type=F32)

    @pl.when(step == 0)
    def _():
        total_ref[...] = part(*w_refs[:3])

    @pl.when((step > 0) & (step < steps // 2))
    def _():
        total_ref[...] += part(*w_refs[:3])

    @pl.when((step >= steps // 2) & (step < steps - 1))
    def _():
        total_ref[...] += part(*w_refs[3:])

    @pl.when(step == steps - 1)
    def _():
        total = (total_ref[...] + part(*w_refs[3:])).astype(BF16)
        start = 0
        for ref in out_refs:
            ref[...] = total[start : start + ref.shape[0]]
            start += ref.shape[0]


def experts(arrays, mine, other):
    width = arrays[0].shape[1]
    hidden = mine[0].shape[1]
    block = 256
    half = hidden // block
    total = sum(x.shape[0] for x in arrays)

    def specs(at):
        return [
            pl.BlockSpec((width, block), lambda i: (0, at(i))),
            pl.BlockSpec((width, block), lambda i: (0, at(i))),
            pl.BlockSpec((block, width), lambda i: (at(i), 0)),
        ]

    return pl.pallas_call(
        functools.partial(expert_kernel, n_in=len(arrays)),
        grid=(2 * half,),
        in_specs=[vmem(x.shape) for x in arrays]
        + specs(lambda i: jnp.minimum(i, half - 1))
        + specs(lambda i: jnp.maximum(i - half, 0)),
        out_specs=[vmem(x.shape) for x in arrays],
        out_shape=[jax.ShapeDtypeStruct(x.shape, BF16) for x in arrays],
        scratch_shapes=[pltpu.VMEM((total, width), BF16), pltpu.VMEM((total, width), F32)],
        compiler_params=pltpu.CompilerParams(vmem_limit_bytes=48 * MIB),
        cost_estimate=pl.CostEstimate(
            flops=12 * total * width * hidden,
            bytes_accessed=12 * width * hidden + 4 * total * width,
            transcendentals=2 * total * hidden,
        ),
        name="experts",
    )(*arrays, *mine, *other)


def combine_kernel(info_ref, *refs, n_exp, pieces, with_mid):
    *back_refs, out_ref = refs
    info = info_ref[...]
    rows = places(info, n_exp, pieces)
    gates = info.T
    if with_mid:
        mid_ref, far_ref, *back_refs = back_refs
        total = mid_ref[...] + far_ref[...].astype(F32)
    else:
        total = None
    back = jnp.concatenate([r[...] for r in back_refs], axis=0)
    at = lax.broadcasted_iota(jnp.int32, (back.shape[0], rows[0].shape[1]), 0)
    for k, row in enumerate(rows):
        pick = (at == row).astype(F32).astype(BF16)
        term = lax.dot_general(pick, back, (((0,), (0,)), ((), ())), preferred_element_type=F32)
        term = term * gates[:, TOP + k : TOP + k + 1]
        total = term if total is None else total + term
    out_ref[...] = total.astype(BF16)


def combine(info, backs, n_exp, pieces, mid=None, far=None):
    rows, width = info.shape[1], backs[0].shape[1]
    cols = 512
    base = [] if mid is None else [mid, far]
    return pl.pallas_call(
        functools.partial(
            combine_kernel, n_exp=n_exp, pieces=pieces, with_mid=mid is not None
        ),
        grid=(width // cols,),
        in_specs=[vmem(info.shape)]
        + [pl.BlockSpec((x.shape[0], cols), lambda i: (0, i)) for x in (*base, *backs)],
        out_specs=pl.BlockSpec((rows, cols), lambda i: (0, i)),
        out_shape=jax.ShapeDtypeStruct((rows, width), BF16),
        compiler_params=pltpu.CompilerParams(vmem_limit_bytes=24 * MIB),
        name="combine",
    )(info, *base, *backs)


def spread_kernel(x_ref, out_ref):
    out_ref[0] = x_ref[...]


def spread(qkv, n_seq):
    three, rows, width = qkv.shape
    part = width // n_seq
    return pl.pallas_call(
        spread_kernel,
        grid=(n_seq,),
        in_specs=[pl.BlockSpec((three, rows, part), lambda i: (0, 0, i))],
        out_specs=pl.BlockSpec((1, three, rows, part), lambda i: (i, 0, 0, 0)),
        out_shape=jax.ShapeDtypeStruct((n_seq, three, rows, part), BF16),
        compiler_params=pltpu.CompilerParams(vmem_limit_bytes=16 * MIB),
        name="spread",
    )(qkv)


def per_device(stream_in, qkv_heads, expert_ids, gate_weights, w_out, w_gate, w_up, w_down):
    rows, width = stream_in.shape[1:]
    seq, exp = ("y", "core"), ("z", "x")
    n_y, n_seq, n_exp = lax.axis_size("y"), lax.axis_size(seq), lax.axis_size(exp)
    capacity = 3 * TOP * rows // (2 * n_exp)
    pieces = (capacity // 3, capacity - capacity // 3)
    whole = (capacity,)

    def swap(x):
        return lax.ppermute(x, "core", [(0, 1), (1, 0)])

    def shift(x, by):
        return lax.ppermute(x, "y", [(i, (i + by) % n_y) for i in range(n_y)])

    def exchange(x):
        return lax.all_to_all(x, exp, split_axis=0, concat_axis=0, tiled=True)

    mine = [w[0] for w in (w_gate, w_up, w_down)]
    other = [swap(w) for w in mine]
    info = jnp.concatenate(
        [expert_ids[0].T.astype(F32), gate_weights[0].T, jnp.zeros((8 - 2 * TOP, rows), F32)]
    )
    info_far = shift(info, 2)
    qkv = spread(qkv_heads[0].transpose(1, 0, 2), n_seq)
    arrived = lax.all_to_all(qkv, seq, split_axis=0, concat_axis=0, tiled=True)
    context = attention(arrived)
    context, info_far, other = lax.optimization_barrier((context, info_far, other))
    merged = lax.all_to_all(context, seq, split_axis=0, concat_axis=0, tiled=True)
    mid, normed, *buffers = project(merged, w_out, stream_in[0], info, n_exp, pieces)

    [buffer_far] = route(shift(normed, 2), info_far, n_exp, whole)
    own = [exchange(b) for b in buffers]
    far = exchange(buffer_far)
    up, down = [shift(x, 1) for x in own], [shift(x, -1) for x in own]

    own_part = experts(own, mine, other)
    near_part = [experts([u, d], mine, other) for u, d in zip(up, down)]
    [far_part] = experts([far], mine, other)

    far_sum = combine(info_far, [exchange(far_part)], n_exp, whole)
    far_home = shift(far_sum, 2)
    backs = []
    for a, (u, d) in zip(own_part, near_part):
        summed = a.astype(F32) + shift(u, -1).astype(F32) + shift(d, 1).astype(F32)
        backs.append(exchange(summed.astype(BF16)))
    return combine(info, backs, n_exp, pieces, mid, far_home)[None]


def solution(mesh):
    split = Mesh(mesh.devices.reshape(-1, 2, 4, 4), ("y", "core", "z", "x"))
    seq, exp = ("y", "core"), ("z", "x")
    in_specs = (
        P(exp, seq, None),
        P(exp, seq, None, None),
        P(exp, seq, None),
        P(exp, seq, None),
        P(),
        P(exp, None, seq),
        P(exp, None, seq),
        P(exp, seq, None),
    )
    return jax.shard_map(
        per_device, mesh=split, in_specs=in_specs, out_specs=P(exp, seq, None), check_vma=False
    )
```

```python
import functools

import jax
import jax.numpy as jnp
from jax import lax
from jax.experimental import pallas as pl
from jax.experimental.pallas import tpu as pltpu
from jax.sharding import Mesh
from jax.sharding import PartitionSpec as P

HD = 64
LANES = 128
MIB = 1 << 20
BF16 = jnp.bfloat16
F32 = jnp.float32
LOG2E = 1.4426950408889634
TOP = 2


def vmem(shape):
    return pl.BlockSpec(shape, lambda *_: (0,) * len(shape))


def attention_kernel(x_ref, out_ref, *, block):
    n_src, _, rows, lanes = x_ref.shape
    length = n_src * rows
    keys = x_ref[:, 1].reshape(length, lanes)
    values = x_ref[:, 2].reshape(length, lanes)
    wide = jnp.concatenate([values, jnp.ones((length, lanes), BF16)], axis=1)
    lane = lax.broadcasted_iota(jnp.int32, (1, lanes), 1)
    first = lane < HD
    scale = float(HD) ** (-0.5) * LOG2E
    per = block // rows
    for i in range(length // block):
        query = x_ref[i * per : (i + 1) * per, 0].reshape(block, lanes)
        parts = []
        for head in range(2):
            mine = jnp.where(first if head == 0 else ~first, query, jnp.zeros_like(query))
            scores = lax.dot_general(
                mine, keys, (((1,), (1,)), ((), ())), preferred_element_type=F32
            )
            top = jnp.max(scores, axis=1, keepdims=True)
            weights = jnp.exp2((scores - top) * scale).astype(BF16)
            both = jnp.dot(weights, wide, preferred_element_type=F32)
            parts.append(both[:, :lanes] / both[:, lanes:])
        context = jnp.where(first, parts[0], parts[1]).astype(BF16)
        out_ref[i * per : (i + 1) * per] = context.reshape(per, rows, lanes)


def attention(arrived):
    n_src, three, rows, width = arrived.shape
    return pl.pallas_call(
        functools.partial(attention_kernel, block=2 * rows),
        grid=(width // LANES,),
        in_specs=[pl.BlockSpec((n_src, three, rows, LANES), lambda i: (0, 0, 0, i))],
        out_specs=pl.BlockSpec((n_src, rows, LANES), lambda i: (0, 0, i)),
        out_shape=jax.ShapeDtypeStruct((n_src, rows, width), BF16),
        compiler_params=pltpu.CompilerParams(vmem_limit_bytes=24 * MIB),
        name="attention",
    )(arrived)


def places(info, n_exp, pieces):
    tokens = info.shape[1]
    ids = info[:TOP].astype(jnp.int32)
    expert = lax.broadcasted_iota(jnp.int32, (n_exp, tokens), 0)
    named = [expert == ids[k : k + 1] for k in range(TOP)]
    member = sum(n.astype(F32) for n in named)
    before = (
        lax.broadcasted_iota(jnp.int32, (tokens, tokens), 0)
        < lax.broadcasted_iota(jnp.int32, (tokens, tokens), 1)
    ).astype(F32)
    rank = jnp.dot(member.astype(BF16), before.astype(BF16), preferred_element_type=F32)
    rows = []
    for k, n in enumerate(named):
        slot = jnp.sum(jnp.where(n, rank, 0.0), axis=0, keepdims=True).astype(jnp.int32)
        row, start = None, 0
        for piece in pieces:
            here = start * n_exp + ids[k : k + 1] * piece + (slot - start)
            row = here if row is None else jnp.where(slot >= start, here, row)
            start += piece
        rows.append(row)
    return rows


def fill(normed, info, out_refs, n_exp, pieces):
    rows = places(info, n_exp, pieces)
    start = 0
    for ref, piece in zip(out_refs, pieces, strict=True):
        slots = n_exp * piece
        at = lax.broadcasted_iota(jnp.int32, (slots, normed.shape[0]), 0) + start
        pick = sum((at == r).astype(F32) for r in rows).astype(BF16)
        ref[...] = jnp.dot(pick, normed, preferred_element_type=F32).astype(BF16)
        start += slots


def project_kernel(
    ctx_ref, w_hbm, stream_ref, info_ref, mid_ref, normed_ref, *refs, n_exp, pieces, cuts
):
    *out_refs, w_ref, sems = refs
    cols = w_ref.shape[1] // cuts
    copies = [
        pltpu.make_async_copy(
            w_hbm.at[:, pl.ds(i * cols, cols)], w_ref.at[:, pl.ds(i * cols, cols)], sems.at[i]
        )
        for i in range(cuts)
    ]
    for copy in copies:
        copy.start()
    merged = jnp.concatenate([ctx_ref[s] for s in range(ctx_ref.shape[0])], axis=1)
    for i, copy in enumerate(copies):
        copy.wait()
        here = slice(i * cols, (i + 1) * cols)
        mid_ref[:, here] = stream_ref[:, here].astype(F32) + jnp.dot(
            merged, w_ref[:, here], preferred_element_type=F32
        )
    mid = mid_ref[...]
    factor = lax.rsqrt(jnp.mean(mid * mid, axis=1, keepdims=True) + 1e-06)
    normed = (mid * factor).astype(BF16)
    normed_ref[...] = normed
    fill(normed, info_ref[...], out_refs, n_exp, pieces)


def project(merged, w_out, stream, info, n_exp, pieces):
    rows, width = stream.shape
    cuts = 4
    slots = [n_exp * p for p in pieces]
    return pl.pallas_call(
        functools.partial(project_kernel, n_exp=n_exp, pieces=pieces, cuts=cuts),
        grid=(1,),
        in_specs=[
            vmem(merged.shape),
            pl.BlockSpec(memory_space=pltpu.HBM),
            vmem(stream.shape),
            vmem(info.shape),
        ],
        out_specs=[vmem((rows, width))] * 2 + [vmem((s, width)) for s in slots],
        out_shape=[
            pltpu.HBM((rows, width), F32),
            jax.ShapeDtypeStruct((rows, width), BF16),
        ]
        + [jax.ShapeDtypeStruct((s, width), BF16) for s in slots],
        scratch_shapes=[
            pltpu.VMEM(w_out.shape, BF16),
            pltpu.SemaphoreType.DMA((cuts,)),
        ],
        compiler_params=pltpu.CompilerParams(vmem_limit_bytes=32 * MIB),
        name="project",
    )(merged, in_hbm(w_out), stream, info)


def route_kernel(normed_ref, info_ref, *out_refs, n_exp, pieces):
    fill(normed_ref[...], info_ref[...], out_refs, n_exp, pieces)


def route(normed, info, n_exp, pieces):
    rows, width = normed.shape
    slots = [n_exp * p for p in pieces]
    return pl.pallas_call(
        functools.partial(route_kernel, n_exp=n_exp, pieces=pieces),
        grid=(1,),
        in_specs=[vmem(normed.shape), vmem(info.shape)],
        out_specs=[vmem((s, width)) for s in slots],
        out_shape=[jax.ShapeDtypeStruct((s, width), BF16) for s in slots],
        compiler_params=pltpu.CompilerParams(vmem_limit_bytes=24 * MIB),
        name="route",
    )(normed, info)


def expert_kernel(*refs, n_in, block):
    x_refs, w_refs = refs[:n_in], refs[n_in : n_in + 6]
    *out_refs, rows_ref, gate_ref, up_ref, down_ref, x_sems, w_sems = refs[n_in + 6 :]
    share = w_refs[0].shape[1]
    per = share // block

    def weight_copies(i):
        gate, up, down = w_refs[:3] if i < per else w_refs[3:]
        there, here = pl.ds(i % per * block, block), pl.ds(i * block, block)
        return (
            pltpu.make_async_copy(gate.at[:, there], gate_ref.at[:, here], w_sems.at[i, 0]),
            pltpu.make_async_copy(up.at[:, there], up_ref.at[:, here], w_sems.at[i, 1]),
            pltpu.make_async_copy(down.at[there], down_ref.at[here], w_sems.at[i, 2]),
        )

    row_copies, start = [], 0
    for i, ref in enumerate(x_refs):
        here = pl.ds(start, ref.shape[0])
        row_copies.append(pltpu.make_async_copy(ref, rows_ref.at[here], x_sems.at[i]))
        start += ref.shape[0]
    copies = [weight_copies(i) for i in range(2 * per)]
    for copy in (*row_copies, *copies[0], *copies[1]):
        copy.start()
    for copy in row_copies:
        copy.wait()
    rows, total = rows_ref[...], None
    for i in range(2 * per):
        here = slice(i * block, (i + 1) * block)
        copies[i][0].wait()
        copies[i][1].wait()
        if i + 2 < 2 * per:
            for copy in copies[i + 2]:
                copy.start()
        gate = jnp.dot(rows, gate_ref[:, here], preferred_element_type=F32)
        up = jnp.dot(rows, up_ref[:, here], preferred_element_type=F32)
        hidden = (gate / (1.0 + jnp.exp(-gate)) * up).astype(BF16)
        copies[i][2].wait()
        term = jnp.dot(hidden, down_ref[here], preferred_element_type=F32)
        total = term if total is None else total + term
    start = 0
    for ref in out_refs:
        ref[...] = total[start : start + ref.shape[0]].astype(BF16)
        start += ref.shape[0]


def in_hbm(x):
    return pltpu.with_memory_space_constraint(x, pltpu.HBM)


def experts(arrays, mine, other):
    width = arrays[0].shape[1]
    hidden = 2 * mine[0].shape[1]
    total = sum(x.shape[0] for x in arrays)
    block = 256
    return pl.pallas_call(
        functools.partial(expert_kernel, n_in=len(arrays), block=block),
        grid=(1,),
        in_specs=[pl.BlockSpec(memory_space=pl.ANY)] * len(arrays)
        + [pl.BlockSpec(memory_space=pltpu.HBM)] * 6,
        out_specs=[vmem(x.shape) for x in arrays],
        out_shape=[pltpu.HBM(x.shape, BF16) for x in arrays],
        scratch_shapes=[
            pltpu.VMEM((total, width), BF16),
            pltpu.VMEM((width, hidden), BF16),
            pltpu.VMEM((width, hidden), BF16),
            pltpu.VMEM((hidden, width), BF16),
            pltpu.SemaphoreType.DMA((len(arrays),)),
            pltpu.SemaphoreType.DMA((hidden // block, 3)),
        ],
        compiler_params=pltpu.CompilerParams(vmem_limit_bytes=44 * MIB),
        cost_estimate=pl.CostEstimate(
            flops=6 * total * width * hidden,
            bytes_accessed=6 * width * hidden + 4 * total * width,
            transcendentals=total * hidden,
        ),
        name="experts",
    )(*arrays, *(in_hbm(w) for w in (*mine, *other)))


def combine_kernel(info_ref, *refs, n_exp, pieces, with_mid):
    *back_refs, out_ref = refs
    info = info_ref[...]
    rows = places(info, n_exp, pieces)
    gates = info.T
    if with_mid:
        mid_ref, far_ref, *back_refs = back_refs
        total = mid_ref[...] + far_ref[...].astype(F32)
    else:
        total = None
    back = jnp.concatenate([r[...] for r in back_refs], axis=0)
    at = lax.broadcasted_iota(jnp.int32, (back.shape[0], rows[0].shape[1]), 0)
    for k, row in enumerate(rows):
        pick = (at == row).astype(F32).astype(BF16)
        term = lax.dot_general(pick, back, (((0,), (0,)), ((), ())), preferred_element_type=F32)
        term = term * gates[:, TOP + k : TOP + k + 1]
        total = term if total is None else total + term
    out_ref[...] = total.astype(BF16)


def combine(info, backs, n_exp, pieces, mid=None, far=None):
    rows, width = info.shape[1], backs[0].shape[1]
    cols = 512
    base = [] if mid is None else [in_hbm(mid), far]
    return pl.pallas_call(
        functools.partial(
            combine_kernel, n_exp=n_exp, pieces=pieces, with_mid=mid is not None
        ),
        grid=(width // cols,),
        in_specs=[vmem(info.shape)]
        + [pl.BlockSpec((x.shape[0], cols), lambda i: (0, i)) for x in (*base, *backs)],
        out_specs=pl.BlockSpec((rows, cols), lambda i: (0, i)),
        out_shape=jax.ShapeDtypeStruct((rows, width), BF16),
        compiler_params=pltpu.CompilerParams(vmem_limit_bytes=24 * MIB),
        name="combine",
    )(info, *base, *backs)


def spread_kernel(x_ref, out_ref, sems):
    part = out_ref.shape[3]
    copies = [
        pltpu.make_async_copy(x_ref.at[:, :, pl.ds(i * part, part)], out_ref.at[i], sems.at[i])
        for i in range(out_ref.shape[0])
    ]
    for copy in copies:
        copy.start()
    for copy in copies:
        copy.wait()


def spread(qkv, n_seq):
    three, rows, width = qkv.shape
    return pl.pallas_call(
        spread_kernel,
        in_specs=[pl.BlockSpec(memory_space=pltpu.HBM)],
        out_specs=pl.BlockSpec(memory_space=pltpu.HBM),
        out_shape=jax.ShapeDtypeStruct((n_seq, three, rows, width // n_seq), BF16),
        scratch_shapes=[pltpu.SemaphoreType.DMA((n_seq,))],
        compiler_params=pltpu.CompilerParams(vmem_limit_bytes=4 * MIB),
        name="spread",
    )(in_hbm(qkv))


def total_kernel(own_ref, *refs):
    *in_refs, out_ref = refs
    start = 0
    for up_ref, down_ref in zip(in_refs[::2], in_refs[1::2]):
        here = slice(start, start + up_ref.shape[0])
        total = own_ref[here].astype(F32) + up_ref[...].astype(F32) + down_ref[...].astype(F32)
        out_ref[here] = total.astype(BF16)
        start += up_ref.shape[0]


def add_up(own, pairs):
    arrays = [own, *(x for pair in pairs for x in pair)]
    rows, width = own.shape
    cols = 512
    return pl.pallas_call(
        total_kernel,
        grid=(width // cols,),
        in_specs=[pl.BlockSpec((x.shape[0], cols), lambda i: (0, i)) for x in arrays],
        out_specs=pl.BlockSpec((rows, cols), lambda i: (0, i)),
        out_shape=pltpu.HBM((rows, width), BF16),
        compiler_params=pltpu.CompilerParams(vmem_limit_bytes=16 * MIB),
        name="add_up",
    )(*arrays)


def per_device(stream_in, qkv_heads, expert_ids, gate_weights, w_out, w_gate, w_up, w_down):
    rows, width = stream_in.shape[1:]
    seq, exp = ("y", "core"), ("z", "x")
    n_y, n_seq, n_exp = lax.axis_size("y"), lax.axis_size(seq), lax.axis_size(exp)
    capacity = 3 * TOP * rows // (2 * n_exp)
    pieces = (capacity,)

    def swap(x):
        return lax.ppermute(x, "core", [(0, 1), (1, 0)])

    def shift(x, by):
        return lax.ppermute(x, "y", [(i, (i + by) % n_y) for i in range(n_y)])

    def exchange(x):
        return lax.all_to_all(x, exp, split_axis=0, concat_axis=0, tiled=True)

    mine = [w[0] for w in (w_gate, w_up, w_down)]
    other = [swap(w) for w in mine]
    info = jnp.concatenate(
        [expert_ids[0].T.astype(F32), gate_weights[0].T, jnp.zeros((8 - 2 * TOP, rows), F32)]
    )
    info_far = shift(info, 2)
    qkv = spread(qkv_heads[0].transpose(1, 0, 2), n_seq)
    arrived = lax.all_to_all(qkv, seq, split_axis=0, concat_axis=0, tiled=True)
    context = attention(arrived)
    context, info_far, other = lax.optimization_barrier((context, info_far, other))
    merged = lax.all_to_all(context, seq, split_axis=0, concat_axis=0, tiled=True)
    mid, normed, buffer = project(merged, w_out, stream_in[0], info, n_exp, pieces)

    tie = lax.optimization_barrier
    far_tokens = shift(normed, 2)
    own = exchange(buffer)
    own, far_tokens = tie((own, far_tokens))
    [far_buffer] = route(far_tokens, info_far, n_exp, pieces)
    cut = own.shape[0] // 2
    low, high = own[:cut], own[cut:]
    up_low, down_low = shift(low, 1), shift(low, -1)
    up_high, down_high = shift(high, 1), shift(high, -1)
    far_rows = exchange(far_buffer)

    [own_part] = experts([own], mine, other)
    up_low, down_low, own_part = tie((up_low, down_low, own_part))
    up_low, down_low = experts([up_low, down_low], mine, other)
    far_rows, up_low, down_low = tie((far_rows, up_low, down_low))
    [far_part] = experts([far_rows], mine, other)
    up_high, down_high, far_part = tie((up_high, down_high, far_part))
    up_high, down_high = experts([up_high, down_high], mine, other)
    far_back = exchange(far_part)
    up_low, down_low = shift(up_low, -1), shift(down_low, 1)
    up_high, down_high = shift(up_high, -1), shift(down_high, 1)
    far_sum = combine(info_far, [far_back], n_exp, pieces)
    total = add_up(own_part, [(up_low, down_low), (up_high, down_high)])
    total, far_back = tie((total, far_back))
    back = exchange(total)
    far_home = shift(far_sum, 2)
    return combine(info, [back], n_exp, pieces, mid, far_home)[None]


def solution(mesh):
    split = Mesh(mesh.devices.reshape(-1, 2, 4, 4), ("y", "core", "z", "x"))
    seq, exp = ("y", "core"), ("z", "x")
    in_specs = (
        P(exp, seq, None),
        P(exp, seq, None, None),
        P(exp, seq, None),
        P(exp, seq, None),
        P(),
        P(exp, None, seq),
        P(exp, None, seq),
        P(exp, seq, None),
    )
    return jax.shard_map(
        per_device, mesh=split, in_specs=in_specs, out_specs=P(exp, seq, None), check_vma=False
    )
```

```python
import functools

import jax
import jax.numpy as jnp
from jax import lax
from jax.experimental import pallas as pl
from jax.experimental.pallas import tpu as pltpu
from jax.sharding import Mesh
from jax.sharding import PartitionSpec as P

HD = 64
LANES = 128
MIB = 1 << 20
BF16 = jnp.bfloat16
F32 = jnp.float32
LOG2E = 1.4426950408889634
TOP = 2


def vmem(shape):
    return pl.BlockSpec(shape, lambda *_: (0,) * len(shape))


def attention_kernel(x_ref, out_ref, *, block):
    n_src, _, rows, lanes = x_ref.shape
    length = n_src * rows
    keys = x_ref[:, 1].reshape(length, lanes)
    values = x_ref[:, 2].reshape(length, lanes)
    wide = jnp.concatenate([values, jnp.ones((length, lanes), BF16)], axis=1)
    lane = lax.broadcasted_iota(jnp.int32, (1, lanes), 1)
    first = lane < HD
    scale = float(HD) ** (-0.5) * LOG2E
    per = block // rows
    for i in range(length // block):
        query = x_ref[i * per : (i + 1) * per, 0].reshape(block, lanes)
        parts = []
        for head in range(2):
            mine = jnp.where(first if head == 0 else ~first, query, jnp.zeros_like(query))
            scores = lax.dot_general(
                mine, keys, (((1,), (1,)), ((), ())), preferred_element_type=F32
            )
            top = jnp.max(scores, axis=1, keepdims=True)
            weights = jnp.exp2((scores - top) * scale).astype(BF16)
            both = jnp.dot(weights, wide, preferred_element_type=F32)
            parts.append(both[:, :lanes] / both[:, lanes:])
        context = jnp.where(first, parts[0], parts[1]).astype(BF16)
        out_ref[i * per : (i + 1) * per] = context.reshape(per, rows, lanes)


def attention(arrived):
    n_src, three, rows, width = arrived.shape
    return pl.pallas_call(
        functools.partial(attention_kernel, block=2 * rows),
        grid=(width // LANES,),
        in_specs=[pl.BlockSpec((n_src, three, rows, LANES), lambda i: (0, 0, 0, i))],
        out_specs=pl.BlockSpec((n_src, rows, LANES), lambda i: (0, 0, i)),
        out_shape=jax.ShapeDtypeStruct((n_src, rows, width), BF16),
        compiler_params=pltpu.CompilerParams(vmem_limit_bytes=24 * MIB),
        name="attention",
    )(arrived)


def plan_kernel(info_ref, out_ref, *, n_exp, capacity):
    info = info_ref[...]
    tokens = info.shape[1]
    ids = info[:TOP].astype(jnp.int32)
    expert = lax.broadcasted_iota(jnp.int32, (n_exp, tokens), 0)
    named = [expert == ids[k : k + 1] for k in range(TOP)]
    member = sum(n.astype(F32) for n in named)
    before = (
        lax.broadcasted_iota(jnp.int32, (tokens, tokens), 0)
        < lax.broadcasted_iota(jnp.int32, (tokens, tokens), 1)
    ).astype(F32)
    rank = jnp.dot(member.astype(BF16), before.astype(BF16), preferred_element_type=F32)
    out_ref[...] = info
    for k, n in enumerate(named):
        slot = jnp.sum(jnp.where(n, rank, 0.0), axis=0, keepdims=True)
        out_ref[2 * TOP + k : 2 * TOP + k + 1] = info[k : k + 1] * capacity + slot


def plan(info, n_exp, capacity):
    return pl.pallas_call(
        functools.partial(plan_kernel, n_exp=n_exp, capacity=capacity),
        grid=(1,),
        in_specs=[vmem(info.shape)],
        out_specs=vmem(info.shape),
        out_shape=jax.ShapeDtypeStruct(info.shape, F32),
        compiler_params=pltpu.CompilerParams(vmem_limit_bytes=4 * MIB),
        name="plan",
    )(info)


def fill(normed, info, out_ref):
    rows = info[2 * TOP : 3 * TOP].astype(jnp.int32)
    at = lax.broadcasted_iota(jnp.int32, (out_ref.shape[0], normed.shape[0]), 0)
    pick = sum((at == rows[k : k + 1]).astype(F32) for k in range(TOP)).astype(BF16)
    out_ref[...] = jnp.dot(pick, normed, preferred_element_type=F32).astype(BF16)


def project_kernel(
    ctx_ref, w_hbm, stream_ref, info_ref, mid_ref, normed_ref, out_ref, w_ref, sems, *, cuts
):
    cols = w_ref.shape[1] // cuts
    copies = [
        pltpu.make_async_copy(
            w_hbm.at[:, pl.ds(i * cols, cols)], w_ref.at[:, pl.ds(i * cols, cols)], sems.at[i]
        )
        for i in range(cuts)
    ]
    for copy in copies:
        copy.start()
    merged = jnp.concatenate([ctx_ref[s] for s in range(ctx_ref.shape[0])], axis=1)
    for i, copy in enumerate(copies):
        copy.wait()
        here = slice(i * cols, (i + 1) * cols)
        mid_ref[:, here] = stream_ref[:, here].astype(F32) + jnp.dot(
            merged, w_ref[:, here], preferred_element_type=F32
        )
    mid = mid_ref[...]
    factor = lax.rsqrt(jnp.mean(mid * mid, axis=1, keepdims=True) + 1e-06)
    normed = (mid * factor).astype(BF16)
    normed_ref[...] = normed
    fill(normed, info_ref[...], out_ref)


def project(merged, w_out, stream, info, slots):
    rows, width = stream.shape
    cuts = 4
    return pl.pallas_call(
        functools.partial(project_kernel, cuts=cuts),
        grid=(1,),
        in_specs=[
            vmem(merged.shape),
            pl.BlockSpec(memory_space=pltpu.HBM),
            vmem(stream.shape),
            vmem(info.shape),
        ],
        out_specs=[vmem((rows, width))] * 2 + [vmem((slots, width))],
        out_shape=[
            pltpu.HBM((rows, width), F32),
            jax.ShapeDtypeStruct((rows, width), BF16),
            jax.ShapeDtypeStruct((slots, width), BF16),
        ],
        scratch_shapes=[
            pltpu.VMEM(w_out.shape, BF16),
            pltpu.SemaphoreType.DMA((cuts,)),
        ],
        compiler_params=pltpu.CompilerParams(vmem_limit_bytes=32 * MIB),
        name="project",
    )(merged, in_hbm(w_out), stream, info)


def route_kernel(normed_ref, info_ref, out_ref):
    fill(normed_ref[...], info_ref[...], out_ref)


def route(normed, info, slots):
    rows, width = normed.shape
    return pl.pallas_call(
        route_kernel,
        grid=(1,),
        in_specs=[vmem(normed.shape), vmem(info.shape)],
        out_specs=vmem((slots, width)),
        out_shape=jax.ShapeDtypeStruct((slots, width), BF16),
        compiler_params=pltpu.CompilerParams(vmem_limit_bytes=16 * MIB),
        name="route",
    )(normed, info)


def expert_kernel(*refs, n_in, block):
    x_refs, w_refs = refs[:n_in], refs[n_in : n_in + 6]
    *out_refs, rows_ref, hidden_ref, gate_ref, up_ref, down_ref, x_sems, w_sems = refs[
        n_in + 6 :
    ]
    share = w_refs[0].shape[1]
    per = share // block

    def weight_copies(i):
        gate, up, down = w_refs[:3] if i < per else w_refs[3:]
        there, here = pl.ds(i % per * block, block), pl.ds(i * block, block)
        return (
            pltpu.make_async_copy(gate.at[:, there], gate_ref.at[:, here], w_sems.at[i, 0]),
            pltpu.make_async_copy(up.at[:, there], up_ref.at[:, here], w_sems.at[i, 1]),
            pltpu.make_async_copy(down.at[there], down_ref.at[here], w_sems.at[i, 2]),
        )

    row_copies, start = [], 0
    for i, ref in enumerate(x_refs):
        here = pl.ds(start, ref.shape[0])
        row_copies.append(pltpu.make_async_copy(ref, rows_ref.at[here], x_sems.at[i]))
        start += ref.shape[0]
    copies = [weight_copies(i) for i in range(2 * per)]
    for copy in (*row_copies, *copies[0], *copies[1]):
        copy.start()
    for copy in row_copies:
        copy.wait()
    rows = rows_ref[...]
    for i in range(2 * per):
        here = slice(i * block, (i + 1) * block)
        copies[i][0].wait()
        copies[i][1].wait()
        if i + 2 < 2 * per:
            for copy in copies[i + 2]:
                copy.start()
        gate = jnp.dot(rows, gate_ref[:, here], preferred_element_type=F32)
        up = jnp.dot(rows, up_ref[:, here], preferred_element_type=F32)
        half = 0.5 * gate
        hidden_ref[:, here] = ((half + half * jnp.tanh(half)) * up).astype(BF16)
    for copy in copies:
        copy[2].wait()
    total = jnp.dot(hidden_ref[...], down_ref[...], preferred_element_type=F32)
    start = 0
    for ref in out_refs:
        ref[...] = total[start : start + ref.shape[0]].astype(BF16)
        start += ref.shape[0]


def in_hbm(x):
    return pltpu.with_memory_space_constraint(x, pltpu.HBM)


def experts(arrays, mine, other):
    width = arrays[0].shape[1]
    hidden = 2 * mine[0].shape[1]
    total = sum(x.shape[0] for x in arrays)
    block = 256
    return pl.pallas_call(
        functools.partial(expert_kernel, n_in=len(arrays), block=block),
        grid=(1,),
        in_specs=[pl.BlockSpec(memory_space=pl.ANY)] * len(arrays)
        + [pl.BlockSpec(memory_space=pltpu.HBM)] * 6,
        out_specs=[vmem(x.shape) for x in arrays],
        out_shape=[pltpu.HBM(x.shape, BF16) for x in arrays],
        scratch_shapes=[
            pltpu.VMEM((total, width), BF16),
            pltpu.VMEM((total, hidden), BF16),
            pltpu.VMEM((width, hidden), BF16),
            pltpu.VMEM((width, hidden), BF16),
            pltpu.VMEM((hidden, width), BF16),
            pltpu.SemaphoreType.DMA((len(arrays),)),
            pltpu.SemaphoreType.DMA((hidden // block, 3)),
        ],
        compiler_params=pltpu.CompilerParams(vmem_limit_bytes=44 * MIB),
        cost_estimate=pl.CostEstimate(
            flops=600 * total * width * hidden,
            bytes_accessed=6 * width * hidden + 4 * total * width,
            transcendentals=total * hidden,
        ),
        name="experts",
    )(*arrays, *(in_hbm(w) for w in (*mine, *other)))


def combine_kernel(info_ref, back_ref, *refs, cuts):
    by_token = info_ref[...].T
    rows = by_token[:, 2 * TOP : 3 * TOP].astype(jnp.int32)
    at = lax.broadcasted_iota(jnp.int32, (rows.shape[0], back_ref.shape[0]), 1)
    picks = [(at == rows[:, k : k + 1]).astype(F32).astype(BF16) for k in range(TOP)]
    gates = [by_token[:, TOP + k : TOP + k + 1] for k in range(TOP)]
    if len(refs) > 1:
        far_ref, mid_hbm, out_ref, mid_ref, sem = refs
        copy = pltpu.make_async_copy(mid_hbm, mid_ref, sem)
        copy.start()
    else:
        [out_ref], copy = refs, None
    cols = out_ref.shape[1] // cuts
    for i in range(cuts):
        here = slice(i * cols, (i + 1) * cols)
        back = back_ref[:, here]
        terms = [
            jnp.dot(pick, back, preferred_element_type=F32) * gate
            for pick, gate in zip(picks, gates, strict=True)
        ]
        total = sum(terms[1:], terms[0])
        if copy is not None:
            if i == 0:
                copy.wait()
            total = mid_ref[:, here] + far_ref[:, here].astype(F32) + total
        out_ref[:, here] = total.astype(BF16)


def combine(info, back, mid=None, far=None):
    rows, width = info.shape[1], back.shape[1]
    held = pl.BlockSpec(memory_space=pltpu.VMEM)
    final = mid is not None
    return pl.pallas_call(
        functools.partial(combine_kernel, cuts=4),
        in_specs=[held] * (3 if final else 2)
        + [pl.BlockSpec(memory_space=pltpu.HBM)] * final,
        out_specs=held,
        out_shape=jax.ShapeDtypeStruct((rows, width), BF16),
        scratch_shapes=[pltpu.VMEM((rows, width), F32), pltpu.SemaphoreType.DMA(())] * final,
        compiler_params=pltpu.CompilerParams(vmem_limit_bytes=16 * MIB),
        name="combine",
    )(info, back, *([far, in_hbm(mid)] if final else []))


def spread_kernel(x_ref, out_ref):
    part = out_ref.shape[3]
    for i in range(out_ref.shape[0]):
        out_ref[i] = x_ref[:, :, i * part : (i + 1) * part]


def spread(qkv, n_seq):
    three, rows, width = qkv.shape
    part = width // n_seq
    return pl.pallas_call(
        spread_kernel,
        grid=(three,),
        in_specs=[pl.BlockSpec((1, rows, width), lambda i: (i, 0, 0))],
        out_specs=pl.BlockSpec((n_seq, 1, rows, part), lambda i: (0, i, 0, 0)),
        out_shape=jax.ShapeDtypeStruct((n_seq, three, rows, part), BF16),
        compiler_params=pltpu.CompilerParams(vmem_limit_bytes=8 * MIB),
        name="spread",
    )(in_hbm(qkv))


def total_kernel(own_ref, *refs):
    *in_refs, out_ref = refs
    start = 0
    for up_ref, down_ref in zip(in_refs[::2], in_refs[1::2]):
        here = slice(start, start + up_ref.shape[0])
        total = own_ref[here].astype(F32) + up_ref[...].astype(F32) + down_ref[...].astype(F32)
        out_ref[here] = total.astype(BF16)
        start = here.stop


def add_up(own, pairs):
    arrays = [own, *(x for pair in pairs for x in pair)]
    rows, width = own.shape
    cols = 512
    return pl.pallas_call(
        total_kernel,
        grid=(width // cols,),
        in_specs=[pl.BlockSpec((x.shape[0], cols), lambda i: (0, i)) for x in arrays],
        out_specs=pl.BlockSpec((rows, cols), lambda i: (0, i)),
        out_shape=pltpu.HBM((rows, width), BF16),
        compiler_params=pltpu.CompilerParams(vmem_limit_bytes=16 * MIB),
        name="add_up",
    )(*arrays)


def per_device(stream_in, qkv_heads, expert_ids, gate_weights, w_out, w_gate, w_up, w_down):
    rows, width = stream_in.shape[1:]
    seq, exp = ("y", "core"), ("z", "x")
    n_y, n_seq, n_exp = lax.axis_size("y"), lax.axis_size(seq), lax.axis_size(exp)
    capacity = 3 * TOP * rows // (2 * n_exp)
    slots = n_exp * capacity

    def swap(x):
        return lax.ppermute(x, "core", [(0, 1), (1, 0)])

    def shift(x, by):
        return lax.ppermute(x, "y", [(i, (i + by) % n_y) for i in range(n_y)])

    def exchange(x):
        return lax.all_to_all(x, exp, split_axis=0, concat_axis=0, tiled=True)

    mine = [w[0] for w in (w_gate, w_up, w_down)]
    other = [swap(w) for w in mine]
    info = jnp.concatenate(
        [expert_ids[0].T.astype(F32), gate_weights[0].T, jnp.zeros((8 - 2 * TOP, rows), F32)]
    )
    info = plan(info, n_exp, capacity)
    info_far = shift(info, 2)
    qkv = spread(qkv_heads[0].transpose(1, 0, 2), n_seq)
    arrived = lax.all_to_all(qkv, seq, split_axis=0, concat_axis=0, tiled=True)
    context = attention(arrived)
    context, info_far, other = lax.optimization_barrier((context, info_far, other))
    merged = lax.all_to_all(context, seq, split_axis=0, concat_axis=0, tiled=True)
    mid, normed, buffer = project(merged, w_out, stream_in[0], info, slots)

    tie = lax.optimization_barrier
    far_tokens = shift(normed, 2)
    far_buffer = route(far_tokens, info_far, slots)
    own = exchange(buffer)
    quarter = own.shape[0] // 4
    bounds = (0, quarter, quarter + 3 * quarter // 2, 4 * quarter)
    parts = [own[i:j] for i, j in zip(bounds[:-1], bounds[1:], strict=True)]
    ups = [shift(x, 1) for x in parts]
    downs = [shift(x, -1) for x in parts]

    def near(i):
        return experts([ups[i], downs[i]], mine, other)

    [own_part] = experts([own], mine, other)
    ups[0], downs[0], own_part, far_buffer = tie((ups[0], downs[0], own_part, far_buffer))
    far_rows = exchange(far_buffer)
    back0 = near(0)
    ups[1], downs[1], back0 = tie((ups[1], downs[1], back0))
    back1 = near(1)
    far_rows, back1 = tie((far_rows, back1))
    [far_part] = experts([far_rows], mine, other)
    ups[2], downs[2], far_part = tie((ups[2], downs[2], far_part))
    back2 = near(2)
    far_back = exchange(far_part)
    far_sum = combine(info_far, far_back)
    total = add_up(own_part, [(shift(u, -1), shift(d, 1)) for u, d in (back0, back1, back2)])
    total, far_back = tie((total, far_back))
    back = exchange(total)
    far_home = shift(far_sum, 2)
    return combine(info, back, mid, far_home)[None]


def solution(mesh):
    split = Mesh(mesh.devices.reshape(-1, 2, 4, 4), ("y", "core", "z", "x"))
    seq, exp = ("y", "core"), ("z", "x")
    in_specs = (
        P(exp, seq, None),
        P(exp, seq, None, None),
        P(exp, seq, None),
        P(exp, seq, None),
        P(),
        P(exp, None, seq),
        P(exp, None, seq),
        P(exp, seq, None),
    )
    return jax.shard_map(
        per_device, mesh=split, in_specs=in_specs, out_specs=P(exp, seq, None), check_vma=False
    )
```

```python
import functools

import jax
import jax.numpy as jnp
from jax import lax
from jax.experimental import pallas as pl
from jax.experimental.pallas import tpu as pltpu
from jax.sharding import Mesh
from jax.sharding import PartitionSpec as P

HD = 64
LANES = 128
MIB = 1 << 20
BF16 = jnp.bfloat16
F32 = jnp.float32
LOG2E = 1.4426950408889634
TOP = 2


def vmem(shape):
    return pl.BlockSpec(shape, lambda *_: (0,) * len(shape))


def attention_kernel(x_ref, w_hbm, out_ref, w_ref, sems, *, block):
    cuts = sems.shape[0]
    rows = w_hbm.shape[0] // cuts
    fetch = [
        pltpu.make_async_copy(
            w_hbm.at[pl.ds(i * rows, rows)], w_ref.at[pl.ds(i * rows, rows)], sems.at[i]
        )
        for i in range(cuts)
    ]

    @pl.when(pl.program_id(0) == 0)
    def _():
        for copy in fetch:
            copy.start()

    n_src, _, rows, lanes = x_ref.shape
    length = n_src * rows
    keys = x_ref[:, 1].reshape(length, lanes)
    values = x_ref[:, 2].reshape(length, lanes)
    wide = jnp.concatenate([values, jnp.ones((length, lanes), BF16)], axis=1)
    lane = lax.broadcasted_iota(jnp.int32, (1, lanes), 1)
    first = lane < HD
    scale = float(HD) ** (-0.5) * LOG2E
    per = block // rows
    for i in range(length // block):
        query = x_ref[i * per : (i + 1) * per, 0].reshape(block, lanes)
        parts = []
        for head in range(2):
            mine = jnp.where(first if head == 0 else ~first, query, jnp.zeros_like(query))
            scores = lax.dot_general(
                mine, keys, (((1,), (1,)), ((), ())), preferred_element_type=F32
            )
            top = jnp.max(scores, axis=1, keepdims=True)
            weights = jnp.exp2((scores - top) * scale).astype(BF16)
            both = jnp.dot(weights, wide, preferred_element_type=F32)
            parts.append(both[:, :lanes] / both[:, lanes:])
        context = jnp.where(first, parts[0], parts[1]).astype(BF16)
        out_ref[i * per : (i + 1) * per] = context.reshape(per, rows, lanes)

    @pl.when(pl.program_id(0) == pl.num_programs(0) - 1)
    def _():
        for copy in fetch:
            copy.wait()


def attention(arrived, w_out):
    n_src, three, rows, width = arrived.shape
    return pl.pallas_call(
        functools.partial(attention_kernel, block=2 * rows),
        grid=(width // LANES,),
        in_specs=[
            pl.BlockSpec((n_src, three, rows, LANES), lambda i: (0, 0, 0, i)),
            pl.BlockSpec(memory_space=pltpu.HBM),
        ],
        out_specs=[
            pl.BlockSpec((n_src, rows, LANES), lambda i: (0, 0, i)),
            pl.BlockSpec(memory_space=pl.ANY),
        ],
        out_shape=[
            jax.ShapeDtypeStruct((n_src, rows, width), BF16),
            pltpu.VMEM(w_out.shape, BF16),
        ],
        scratch_shapes=[pltpu.SemaphoreType.DMA((8,))],
        compiler_params=pltpu.CompilerParams(vmem_limit_bytes=24 * MIB),
        name="attention",
    )(arrived, in_hbm(w_out))


def plan_kernel(info_ref, out_ref, *, n_exp, capacity):
    info = info_ref[...]
    tokens = info.shape[1]
    ids = info[:TOP].astype(jnp.int32)
    expert = lax.broadcasted_iota(jnp.int32, (n_exp, tokens), 0)
    named = [expert == ids[k : k + 1] for k in range(TOP)]
    member = sum(n.astype(F32) for n in named)
    before = (
        lax.broadcasted_iota(jnp.int32, (tokens, tokens), 0)
        < lax.broadcasted_iota(jnp.int32, (tokens, tokens), 1)
    ).astype(F32)
    rank = jnp.dot(member.astype(BF16), before.astype(BF16), preferred_element_type=F32)
    out_ref[...] = info
    for k, n in enumerate(named):
        slot = jnp.sum(jnp.where(n, rank, 0.0), axis=0, keepdims=True)
        out_ref[2 * TOP + k : 2 * TOP + k + 1] = info[k : k + 1] * capacity + slot


def plan(info, n_exp, capacity):
    return pl.pallas_call(
        functools.partial(plan_kernel, n_exp=n_exp, capacity=capacity),
        grid=(1,),
        in_specs=[vmem(info.shape)],
        out_specs=vmem(info.shape),
        out_shape=jax.ShapeDtypeStruct(info.shape, F32),
        compiler_params=pltpu.CompilerParams(vmem_limit_bytes=4 * MIB),
        name="plan",
    )(info)


def fill(normed, info, out_ref):
    rows = info[2 * TOP : 3 * TOP].astype(jnp.int32)
    at = lax.broadcasted_iota(jnp.int32, (out_ref.shape[0], normed.shape[0]), 0)
    pick = sum((at == rows[k : k + 1]).astype(F32) for k in range(TOP)).astype(BF16)
    out_ref[...] = jnp.dot(pick, normed, preferred_element_type=F32).astype(BF16)


def project_kernel(
    ctx_ref, w_ref, stream_ref, info_ref, mid_hbm, normed_ref, out_ref, mid_ref, sem
):
    merged = jnp.concatenate([ctx_ref[s] for s in range(ctx_ref.shape[0])], axis=1)
    mid = stream_ref[...].astype(F32) + jnp.dot(
        merged, w_ref[...], preferred_element_type=F32
    )
    mid_ref[...] = mid
    copy = pltpu.make_async_copy(mid_ref, mid_hbm, sem)
    copy.start()
    factor = lax.rsqrt(jnp.mean(mid * mid, axis=1, keepdims=True) + 1e-06)
    normed = (mid * factor).astype(BF16)
    normed_ref[...] = normed
    fill(normed, info_ref[...], out_ref)
    copy.wait()


def project(merged, w_out, stream, info, slots):
    rows, width = stream.shape
    held = pl.BlockSpec(memory_space=pltpu.VMEM)
    return pl.pallas_call(
        project_kernel,
        in_specs=[held] * 4,
        out_specs=[pl.BlockSpec(memory_space=pltpu.HBM), held, held],
        out_shape=[
            pltpu.HBM((rows, width), F32),
            jax.ShapeDtypeStruct((rows, width), BF16),
            jax.ShapeDtypeStruct((slots, width), BF16),
        ],
        scratch_shapes=[pltpu.VMEM((rows, width), F32), pltpu.SemaphoreType.DMA(())],
        compiler_params=pltpu.CompilerParams(vmem_limit_bytes=24 * MIB),
        name="project",
    )(merged, pltpu.with_memory_space_constraint(w_out, pltpu.VMEM), stream, info)


def route_kernel(normed_ref, info_ref, out_ref):
    fill(normed_ref[...], info_ref[...], out_ref)


def route(normed, info, slots):
    rows, width = normed.shape
    return pl.pallas_call(
        route_kernel,
        grid=(1,),
        in_specs=[vmem(normed.shape), vmem(info.shape)],
        out_specs=vmem((slots, width)),
        out_shape=jax.ShapeDtypeStruct((slots, width), BF16),
        compiler_params=pltpu.CompilerParams(vmem_limit_bytes=16 * MIB),
        name="route",
    )(normed, info)


def expert_kernel(*refs, n_in, block):
    x_refs, w_refs = refs[:n_in], refs[n_in : n_in + 6]
    *out_refs, rows_ref, hidden_ref, gate_ref, up_ref, down_ref, x_sems, w_sems = refs[
        n_in + 6 :
    ]
    share = w_refs[0].shape[1]
    per = share // block

    def weight_copies(i):
        gate, up, down = w_refs[:3] if i < per else w_refs[3:]
        there, here = pl.ds(i % per * block, block), pl.ds(i * block, block)
        return (
            pltpu.make_async_copy(gate.at[:, there], gate_ref.at[:, here], w_sems.at[i, 0]),
            pltpu.make_async_copy(up.at[:, there], up_ref.at[:, here], w_sems.at[i, 1]),
            pltpu.make_async_copy(down.at[there], down_ref.at[here], w_sems.at[i, 2]),
        )

    row_copies, start = [], 0
    for i, ref in enumerate(x_refs):
        here = pl.ds(start, ref.shape[0])
        row_copies.append(pltpu.make_async_copy(ref, rows_ref.at[here], x_sems.at[i]))
        start += ref.shape[0]
    copies = [weight_copies(i) for i in range(2 * per)]
    for copy in (*row_copies, *copies[0], *copies[1]):
        copy.start()
    for copy in row_copies:
        copy.wait()
    rows = rows_ref[...]
    for i in range(2 * per):
        here = slice(i * block, (i + 1) * block)
        copies[i][0].wait()
        copies[i][1].wait()
        if i + 2 < 2 * per:
            for copy in copies[i + 2]:
                copy.start()
        gate = jnp.dot(rows, gate_ref[:, here], preferred_element_type=F32)
        up = jnp.dot(rows, up_ref[:, here], preferred_element_type=F32)
        half = 0.5 * gate
        hidden_ref[:, here] = ((half + half * jnp.tanh(half)) * up).astype(BF16)
    for copy in copies:
        copy[2].wait()
    total = jnp.dot(hidden_ref[...], down_ref[...], preferred_element_type=F32)
    start = 0
    for ref in out_refs:
        ref[...] = total[start : start + ref.shape[0]].astype(BF16)
        start += ref.shape[0]


def in_hbm(x):
    return pltpu.with_memory_space_constraint(x, pltpu.HBM)


def experts(arrays, mine, other):
    width = arrays[0].shape[1]
    hidden = 2 * mine[0].shape[1]
    total = sum(x.shape[0] for x in arrays)
    block = 256
    return pl.pallas_call(
        functools.partial(expert_kernel, n_in=len(arrays), block=block),
        grid=(1,),
        in_specs=[pl.BlockSpec(memory_space=pl.ANY)] * len(arrays)
        + [pl.BlockSpec(memory_space=pltpu.HBM)] * 6,
        out_specs=[vmem(x.shape) for x in arrays],
        out_shape=[pltpu.HBM(x.shape, BF16) for x in arrays],
        scratch_shapes=[
            pltpu.VMEM((total, width), BF16),
            pltpu.VMEM((total, hidden), BF16),
            pltpu.VMEM((width, hidden), BF16),
            pltpu.VMEM((width, hidden), BF16),
            pltpu.VMEM((hidden, width), BF16),
            pltpu.SemaphoreType.DMA((len(arrays),)),
            pltpu.SemaphoreType.DMA((hidden // block, 3)),
        ],
        compiler_params=pltpu.CompilerParams(vmem_limit_bytes=44 * MIB),
        cost_estimate=pl.CostEstimate(
            flops=600 * total * width * hidden,
            bytes_accessed=6 * width * hidden + 4 * total * width,
            transcendentals=total * hidden,
        ),
        name="experts",
    )(*arrays, *(in_hbm(w) for w in (*mine, *other)))


def combine_kernel(info_ref, back_ref, *refs, cuts):
    by_token = info_ref[...].T
    rows = by_token[:, 2 * TOP : 3 * TOP].astype(jnp.int32)
    at = lax.broadcasted_iota(jnp.int32, (rows.shape[0], back_ref.shape[0]), 1)
    picks = [(at == rows[:, k : k + 1]).astype(F32).astype(BF16) for k in range(TOP)]
    gates = [by_token[:, TOP + k : TOP + k + 1] for k in range(TOP)]
    if len(refs) > 1:
        far_ref, mid_hbm, out_ref, mid_ref, sem = refs
        copy = pltpu.make_async_copy(mid_hbm, mid_ref, sem)
        copy.start()
    else:
        [out_ref], copy = refs, None
    cols = out_ref.shape[1] // cuts
    for i in range(cuts):
        here = slice(i * cols, (i + 1) * cols)
        back = back_ref[:, here]
        terms = [
            jnp.dot(pick, back, preferred_element_type=F32) * gate
            for pick, gate in zip(picks, gates, strict=True)
        ]
        total = sum(terms[1:], terms[0])
        if copy is not None:
            if i == 0:
                copy.wait()
            total = mid_ref[:, here] + far_ref[:, here].astype(F32) + total
        out_ref[:, here] = total.astype(BF16)


def combine(info, back, mid=None, far=None):
    rows, width = info.shape[1], back.shape[1]
    held = pl.BlockSpec(memory_space=pltpu.VMEM)
    final = mid is not None
    return pl.pallas_call(
        functools.partial(combine_kernel, cuts=4),
        in_specs=[held] * (3 if final else 2)
        + [pl.BlockSpec(memory_space=pltpu.HBM)] * final,
        out_specs=held,
        out_shape=jax.ShapeDtypeStruct((rows, width), BF16),
        scratch_shapes=[pltpu.VMEM((rows, width), F32), pltpu.SemaphoreType.DMA(())] * final,
        compiler_params=pltpu.CompilerParams(vmem_limit_bytes=16 * MIB),
        name="combine",
    )(info, back, *([far, in_hbm(mid)] if final else []))


def spread_kernel(x_hbm, out_hbm, x_ref, in_sems, out_sems):
    n_seq, three, _, part = out_hbm.shape
    copies = [
        pltpu.make_async_copy(x_hbm.at[j], x_ref.at[j], in_sems.at[j]) for j in range(three)
    ]
    for copy in copies:
        copy.start()
    out = []
    for j, copy in enumerate(copies):
        copy.wait()
        for i in range(n_seq):
            out.append(
                pltpu.make_async_copy(
                    x_ref.at[j, :, pl.ds(i * part, part)], out_hbm.at[i, j], out_sems.at[i, j]
                )
            )
            out[-1].start()
    for copy in out:
        copy.wait()


def spread(qkv, n_seq):
    three, rows, width = qkv.shape
    part = width // n_seq
    return pl.pallas_call(
        spread_kernel,
        in_specs=[pl.BlockSpec(memory_space=pltpu.HBM)],
        out_specs=pl.BlockSpec(memory_space=pltpu.HBM),
        out_shape=pltpu.HBM((n_seq, three, rows, part), BF16),
        scratch_shapes=[
            pltpu.VMEM(qkv.shape, BF16),
            pltpu.SemaphoreType.DMA((three,)),
            pltpu.SemaphoreType.DMA((n_seq, three)),
        ],
        compiler_params=pltpu.CompilerParams(vmem_limit_bytes=8 * MIB),
        name="spread",
    )(in_hbm(qkv))


def total_kernel(own_ref, *refs):
    *in_refs, out_hbm, out_ref, sems = refs
    start, copies = 0, []
    for i, (up_ref, down_ref) in enumerate(zip(in_refs[::2], in_refs[1::2], strict=True)):
        n = up_ref.shape[0]
        total = own_ref[start : start + n].astype(F32) + up_ref[...].astype(F32)
        out_ref[start : start + n] = (total + down_ref[...].astype(F32)).astype(BF16)
        here = pl.ds(start, n)
        copies.append(pltpu.make_async_copy(out_ref.at[here], out_hbm.at[here], sems.at[i]))
        copies[-1].start()
        start += n
    for copy in copies:
        copy.wait()


def add_up(own, pairs):
    arrays = [own, *(x for pair in pairs for x in pair)]
    return pl.pallas_call(
        total_kernel,
        in_specs=[pl.BlockSpec(memory_space=pltpu.VMEM)] * len(arrays),
        out_specs=pl.BlockSpec(memory_space=pltpu.HBM),
        out_shape=pltpu.HBM(own.shape, BF16),
        scratch_shapes=[
            pltpu.VMEM(own.shape, BF16),
            pltpu.SemaphoreType.DMA((len(pairs),)),
        ],
        compiler_params=pltpu.CompilerParams(vmem_limit_bytes=16 * MIB),
        name="add_up",
    )(*arrays)


def per_device(stream_in, qkv_heads, expert_ids, gate_weights, w_out, w_gate, w_up, w_down):
    rows, width = stream_in.shape[1:]
    seq, exp = ("y", "core"), ("z", "x")
    n_y, n_seq, n_exp = lax.axis_size("y"), lax.axis_size(seq), lax.axis_size(exp)
    capacity = 3 * TOP * rows // (2 * n_exp)
    slots = n_exp * capacity

    def swap(x):
        return lax.ppermute(x, "core", [(0, 1), (1, 0)])

    def shift(x, by):
        return lax.ppermute(x, "y", [(i, (i + by) % n_y) for i in range(n_y)])

    def exchange(x):
        return lax.all_to_all(x, exp, split_axis=0, concat_axis=0, tiled=True)

    mine = [w[0] for w in (w_gate, w_up, w_down)]
    other = [swap(w) for w in mine]
    info = jnp.concatenate(
        [expert_ids[0].T.astype(F32), gate_weights[0].T, jnp.zeros((8 - 2 * TOP, rows), F32)]
    )
    info = plan(info, n_exp, capacity)
    info_far = shift(info, 2)
    qkv = spread(qkv_heads[0].transpose(1, 0, 2), n_seq)
    arrived = lax.all_to_all(qkv, seq, split_axis=0, concat_axis=0, tiled=True)
    context, w_held = attention(arrived, w_out)
    context, info_far, other = lax.optimization_barrier((context, info_far, other))
    merged = lax.all_to_all(context, seq, split_axis=0, concat_axis=0, tiled=True)
    mid, normed, buffer = project(merged, w_held, stream_in[0], info, slots)

    tie = lax.optimization_barrier
    far_tokens = shift(normed, 2)
    own = exchange(buffer)
    eighth = own.shape[0] // 8
    bounds = (0, 3 * eighth, 6 * eighth, 8 * eighth)
    parts = [own[i:j] for i, j in zip(bounds[:-1], bounds[1:], strict=True)]
    far_tokens, parts = tie((far_tokens, parts))
    far_buffer = route(far_tokens, info_far, slots)
    ups = [shift(x, 1) for x in parts[:2]]
    downs = [shift(x, -1) for x in parts[:2]]
    parts[2], ups[0], downs[0] = tie((parts[2], ups[0], downs[0]))
    ups.append(shift(parts[2], 1))
    downs.append(shift(parts[2], -1))

    def near(i):
        return experts([ups[i], downs[i]], mine, other)

    [own_part] = experts([own], mine, other)
    ups[0], downs[0], own_part = tie((ups[0], downs[0], own_part))
    far_rows = exchange(far_buffer)
    back0 = near(0)
    ups[1], downs[1], back0 = tie((ups[1], downs[1], back0))
    back1 = near(1)
    far_rows, back1 = tie((far_rows, back1))
    [far_part] = experts([far_rows], mine, other)
    home = [(shift(u, -1), shift(d, 1)) for u, d in (back0, back1)]
    ups[2], downs[2], far_part, home[0] = tie((ups[2], downs[2], far_part, home[0]))
    back2 = near(2)
    home.append((shift(back2[0], -1), shift(back2[1], 1)))
    far_back = exchange(far_part)
    far_sum = combine(info_far, far_back)
    total = add_up(own_part, home)
    total, far_back = tie((total, far_back))
    back = exchange(total)
    far_home = shift(far_sum, 2)
    return combine(info, back, mid, far_home)[None]


def solution(mesh):
    split = Mesh(mesh.devices.reshape(-1, 2, 4, 4), ("y", "core", "z", "x"))
    seq, exp = ("y", "core"), ("z", "x")
    in_specs = (
        P(exp, seq, None),
        P(exp, seq, None, None),
        P(exp, seq, None),
        P(exp, seq, None),
        P(),
        P(exp, None, seq),
        P(exp, None, seq),
        P(exp, seq, None),
    )
    return jax.shard_map(
        per_device, mesh=split, in_specs=in_specs, out_specs=P(exp, seq, None), check_vma=False
    )
```

```python
import functools

import jax
import jax.numpy as jnp
from jax import lax
from jax.experimental import pallas as pl
from jax.experimental.pallas import tpu as pltpu
from jax.sharding import Mesh
from jax.sharding import PartitionSpec as P

HD = 64
LANES = 128
MIB = 1 << 20
BF16 = jnp.bfloat16
F32 = jnp.float32
LOG2E = 1.4426950408889634
TOP = 2


def vmem(shape):
    return pl.BlockSpec(shape, lambda *_: (0,) * len(shape))


def attention_kernel(x_ref, w_hbm, out_ref, w_ref, sems, *, block):
    cuts = sems.shape[0]
    rows = w_hbm.shape[0] // cuts
    fetch = [
        pltpu.make_async_copy(
            w_hbm.at[pl.ds(i * rows, rows)], w_ref.at[pl.ds(i * rows, rows)], sems.at[i]
        )
        for i in range(cuts)
    ]

    @pl.when(pl.program_id(0) == 0)
    def _():
        for copy in fetch:
            copy.start()

    n_src, _, rows, lanes = x_ref.shape
    length = n_src * rows
    keys = x_ref[:, 1].reshape(length, lanes)
    values = x_ref[:, 2].reshape(length, lanes)
    wide = jnp.concatenate([values, jnp.ones((length, lanes), BF16)], axis=1)
    lane = lax.broadcasted_iota(jnp.int32, (1, lanes), 1)
    first = lane < HD
    scale = float(HD) ** (-0.5) * LOG2E
    per = block // rows
    for i in range(length // block):
        query = x_ref[i * per : (i + 1) * per, 0].reshape(block, lanes)
        parts = []
        for head in range(2):
            mine = jnp.where(first if head == 0 else ~first, query, jnp.zeros_like(query))
            scores = lax.dot_general(
                mine, keys, (((1,), (1,)), ((), ())), preferred_element_type=F32
            )
            top = jnp.max(scores, axis=1, keepdims=True)
            weights = jnp.exp2((scores - top) * scale).astype(BF16)
            both = jnp.dot(weights, wide, preferred_element_type=F32)
            parts.append(both[:, :lanes] / both[:, lanes:])
        context = jnp.where(first, parts[0], parts[1]).astype(BF16)
        out_ref[i * per : (i + 1) * per] = context.reshape(per, rows, lanes)

    @pl.when(pl.program_id(0) == pl.num_programs(0) - 1)
    def _():
        for copy in fetch:
            copy.wait()


def attention(arrived, w_out):
    n_src, three, rows, width = arrived.shape
    return pl.pallas_call(
        functools.partial(attention_kernel, block=2 * rows),
        grid=(width // LANES,),
        in_specs=[
            pl.BlockSpec((n_src, three, rows, LANES), lambda i: (0, 0, 0, i)),
            pl.BlockSpec(memory_space=pltpu.HBM),
        ],
        out_specs=[
            pl.BlockSpec((n_src, rows, LANES), lambda i: (0, 0, i)),
            pl.BlockSpec(memory_space=pl.ANY),
        ],
        out_shape=[
            jax.ShapeDtypeStruct((n_src, rows, width), BF16),
            pltpu.VMEM(w_out.shape, BF16),
        ],
        scratch_shapes=[pltpu.SemaphoreType.DMA((8,))],
        compiler_params=pltpu.CompilerParams(vmem_limit_bytes=24 * MIB),
        name="attention",
    )(arrived, in_hbm(w_out))


def plan_kernel(info_ref, out_ref, *, n_exp, capacity):
    info = info_ref[...]
    tokens = info.shape[1]
    ids = info[:TOP].astype(jnp.int32)
    expert = lax.broadcasted_iota(jnp.int32, (n_exp, tokens), 0)
    named = [expert == ids[k : k + 1] for k in range(TOP)]
    member = sum(n.astype(F32) for n in named)
    before = (
        lax.broadcasted_iota(jnp.int32, (tokens, tokens), 0)
        < lax.broadcasted_iota(jnp.int32, (tokens, tokens), 1)
    ).astype(F32)
    rank = jnp.dot(member.astype(BF16), before.astype(BF16), preferred_element_type=F32)
    out_ref[...] = info
    for k, n in enumerate(named):
        slot = jnp.sum(jnp.where(n, rank, 0.0), axis=0, keepdims=True)
        out_ref[2 * TOP + k : 2 * TOP + k + 1] = info[k : k + 1] * capacity + slot


def plan(info, n_exp, capacity):
    return pl.pallas_call(
        functools.partial(plan_kernel, n_exp=n_exp, capacity=capacity),
        grid=(1,),
        in_specs=[vmem(info.shape)],
        out_specs=vmem(info.shape),
        out_shape=jax.ShapeDtypeStruct(info.shape, F32),
        compiler_params=pltpu.CompilerParams(vmem_limit_bytes=4 * MIB),
        name="plan",
    )(info)


def fill(normed, info, out_ref):
    rows = info[2 * TOP : 3 * TOP].astype(jnp.int32)
    at = lax.broadcasted_iota(jnp.int32, (out_ref.shape[0], normed.shape[0]), 0)
    pick = sum((at == rows[k : k + 1]).astype(F32) for k in range(TOP)).astype(BF16)
    out_ref[...] = jnp.dot(pick, normed, preferred_element_type=F32).astype(BF16)


def project_kernel(
    ctx_ref, w_ref, stream_ref, info_ref, mid_hbm, normed_ref, out_ref, mid_ref, sem
):
    merged = jnp.concatenate([ctx_ref[s] for s in range(ctx_ref.shape[0])], axis=1)
    mid = stream_ref[...].astype(F32) + jnp.dot(
        merged, w_ref[...], preferred_element_type=F32
    )
    mid_ref[...] = mid
    copy = pltpu.make_async_copy(mid_ref, mid_hbm, sem)
    copy.start()
    factor = lax.rsqrt(jnp.mean(mid * mid, axis=1, keepdims=True) + 1e-06)
    normed = (mid * factor).astype(BF16)
    normed_ref[...] = normed
    fill(normed, info_ref[...], out_ref)
    copy.wait()


def project(merged, w_out, stream, info, slots):
    rows, width = stream.shape
    held = pl.BlockSpec(memory_space=pltpu.VMEM)
    return pl.pallas_call(
        project_kernel,
        in_specs=[held] * 4,
        out_specs=[pl.BlockSpec(memory_space=pltpu.HBM), held, held],
        out_shape=[
            pltpu.HBM((rows, width), F32),
            jax.ShapeDtypeStruct((rows, width), BF16),
            jax.ShapeDtypeStruct((slots, width), BF16),
        ],
        scratch_shapes=[pltpu.VMEM((rows, width), F32), pltpu.SemaphoreType.DMA(())],
        compiler_params=pltpu.CompilerParams(vmem_limit_bytes=24 * MIB),
        name="project",
    )(merged, pltpu.with_memory_space_constraint(w_out, pltpu.VMEM), stream, info)


def route_kernel(normed_ref, info_ref, out_ref):
    fill(normed_ref[...], info_ref[...], out_ref)


def route(normed, info, slots):
    rows, width = normed.shape
    return pl.pallas_call(
        route_kernel,
        grid=(1,),
        in_specs=[vmem(normed.shape), vmem(info.shape)],
        out_specs=vmem((slots, width)),
        out_shape=jax.ShapeDtypeStruct((slots, width), BF16),
        compiler_params=pltpu.CompilerParams(vmem_limit_bytes=16 * MIB),
        name="route",
    )(normed, info)


def expert_kernel(*refs, n_in, block):
    x_refs, w_refs = refs[:n_in], refs[n_in : n_in + 6]
    *out_refs, rows_ref, hidden_ref, gate_ref, up_ref, down_ref, x_sems, w_sems = refs[
        n_in + 6 :
    ]
    share = w_refs[0].shape[1]
    per = share // block

    def weight_copies(i):
        gate, up, down = w_refs[:3] if i < per else w_refs[3:]
        there, here = pl.ds(i % per * block, block), pl.ds(i * block, block)
        return (
            pltpu.make_async_copy(gate.at[:, there], gate_ref.at[:, here], w_sems.at[i, 0]),
            pltpu.make_async_copy(up.at[:, there], up_ref.at[:, here], w_sems.at[i, 1]),
            pltpu.make_async_copy(down.at[there], down_ref.at[here], w_sems.at[i, 2]),
        )

    row_copies, start = [], 0
    for i, ref in enumerate(x_refs):
        here = pl.ds(start, ref.shape[0])
        row_copies.append(pltpu.make_async_copy(ref, rows_ref.at[here], x_sems.at[i]))
        start += ref.shape[0]
    copies = [weight_copies(i) for i in range(2 * per)]
    for copy in (*row_copies, *copies[0], *copies[1]):
        copy.start()
    for copy in row_copies:
        copy.wait()
    rows = rows_ref[...]
    for i in range(2 * per):
        here = slice(i * block, (i + 1) * block)
        copies[i][0].wait()
        copies[i][1].wait()
        if i + 2 < 2 * per:
            for copy in copies[i + 2]:
                copy.start()
        gate = jnp.dot(rows, gate_ref[:, here], preferred_element_type=F32)
        up = jnp.dot(rows, up_ref[:, here], preferred_element_type=F32)
        half = 0.5 * gate
        hidden_ref[:, here] = ((half + half * jnp.tanh(half)) * up).astype(BF16)
    for copy in copies:
        copy[2].wait()
    total = jnp.dot(hidden_ref[...], down_ref[...], preferred_element_type=F32)
    start = 0
    for ref in out_refs:
        ref[...] = total[start : start + ref.shape[0]].astype(BF16)
        start += ref.shape[0]


def in_hbm(x):
    return pltpu.with_memory_space_constraint(x, pltpu.HBM)


def experts(arrays, mine, other):
    width = arrays[0].shape[1]
    hidden = 2 * mine[0].shape[1]
    total = sum(x.shape[0] for x in arrays)
    block = 256
    return pl.pallas_call(
        functools.partial(expert_kernel, n_in=len(arrays), block=block),
        grid=(1,),
        in_specs=[pl.BlockSpec(memory_space=pl.ANY)] * len(arrays)
        + [pl.BlockSpec(memory_space=pltpu.HBM)] * 6,
        out_specs=[vmem(x.shape) for x in arrays],
        out_shape=[pltpu.HBM(x.shape, BF16) for x in arrays],
        scratch_shapes=[
            pltpu.VMEM((total, width), BF16),
            pltpu.VMEM((total, hidden), BF16),
            pltpu.VMEM((width, hidden), BF16),
            pltpu.VMEM((width, hidden), BF16),
            pltpu.VMEM((hidden, width), BF16),
            pltpu.SemaphoreType.DMA((len(arrays),)),
            pltpu.SemaphoreType.DMA((hidden // block, 3)),
        ],
        compiler_params=pltpu.CompilerParams(vmem_limit_bytes=44 * MIB),
        cost_estimate=pl.CostEstimate(
            flops=600 * total * width * hidden,
            bytes_accessed=6 * width * hidden + 4 * total * width,
            transcendentals=total * hidden,
        ),
        name="experts",
    )(*arrays, *(in_hbm(w) for w in (*mine, *other)))


def keep_kernel(x_ref, out_ref):
    pass


def keep(x):
    return pl.pallas_call(
        keep_kernel,
        in_specs=[pl.BlockSpec(memory_space=pltpu.HBM)],
        out_specs=pl.BlockSpec(memory_space=pltpu.HBM),
        out_shape=pltpu.HBM(x.shape, x.dtype),
        input_output_aliases={0: 0},
        compiler_params=pltpu.CompilerParams(vmem_limit_bytes=MIB),
        cost_estimate=pl.CostEstimate(flops=100_000_000_000, bytes_accessed=1, transcendentals=0),
        name="keep",
    )(in_hbm(x))


def combine_kernel(info_ref, back_ref, *refs, cuts):
    by_token = info_ref[...].T
    rows = by_token[:, 2 * TOP : 3 * TOP].astype(jnp.int32)
    at = lax.broadcasted_iota(jnp.int32, (rows.shape[0], back_ref.shape[0]), 1)
    picks = [(at == rows[:, k : k + 1]).astype(F32).astype(BF16) for k in range(TOP)]
    gates = [by_token[:, TOP + k : TOP + k + 1] for k in range(TOP)]
    if len(refs) > 1:
        far_ref, mid_hbm, out_ref, mid_ref, sem = refs
        copy = pltpu.make_async_copy(mid_hbm, mid_ref, sem)
        copy.start()
    else:
        [out_ref], copy = refs, None
    cols = out_ref.shape[1] // cuts
    for i in range(cuts):
        here = slice(i * cols, (i + 1) * cols)
        back = back_ref[:, here]
        terms = [
            jnp.dot(pick, back, preferred_element_type=F32) * gate
            for pick, gate in zip(picks, gates, strict=True)
        ]
        total = sum(terms[1:], terms[0])
        if copy is not None:
            if i == 0:
                copy.wait()
            total = mid_ref[:, here] + far_ref[:, here].astype(F32) + total
        out_ref[:, here] = total.astype(BF16)


def combine(info, back, mid=None, far=None):
    rows, width = info.shape[1], back.shape[1]
    held = pl.BlockSpec(memory_space=pltpu.VMEM)
    final = mid is not None
    return pl.pallas_call(
        functools.partial(combine_kernel, cuts=4),
        in_specs=[held] * (3 if final else 2)
        + [pl.BlockSpec(memory_space=pltpu.HBM)] * final,
        out_specs=held,
        out_shape=jax.ShapeDtypeStruct((rows, width), BF16),
        scratch_shapes=[pltpu.VMEM((rows, width), F32), pltpu.SemaphoreType.DMA(())] * final,
        compiler_params=pltpu.CompilerParams(vmem_limit_bytes=16 * MIB),
        name="combine",
    )(info, back, *([far, in_hbm(mid)] if final else []))


def spread_kernel(x_hbm, out_hbm, x_ref, in_sems, out_sems):
    n_seq, three, _, part = out_hbm.shape
    copies = [
        pltpu.make_async_copy(x_hbm.at[j], x_ref.at[j], in_sems.at[j]) for j in range(three)
    ]
    for copy in copies:
        copy.start()
    out = []
    for j, copy in enumerate(copies):
        copy.wait()
        for i in range(n_seq):
            out.append(
                pltpu.make_async_copy(
                    x_ref.at[j, :, pl.ds(i * part, part)], out_hbm.at[i, j], out_sems.at[i, j]
                )
            )
            out[-1].start()
    for copy in out:
        copy.wait()


def spread(qkv, n_seq):
    three, rows, width = qkv.shape
    part = width // n_seq
    return pl.pallas_call(
        spread_kernel,
        in_specs=[pl.BlockSpec(memory_space=pltpu.HBM)],
        out_specs=pl.BlockSpec(memory_space=pltpu.HBM),
        out_shape=pltpu.HBM((n_seq, three, rows, part), BF16),
        scratch_shapes=[
            pltpu.VMEM(qkv.shape, BF16),
            pltpu.SemaphoreType.DMA((three,)),
            pltpu.SemaphoreType.DMA((n_seq, three)),
        ],
        compiler_params=pltpu.CompilerParams(vmem_limit_bytes=8 * MIB),
        name="spread",
    )(in_hbm(qkv))


def total_kernel(own_ref, *refs, n_in, first):
    in_refs, (out_hbm, out_ref, sems) = refs[:n_in], refs[-3:]
    start, copies = 0, []
    for i, (up_ref, down_ref) in enumerate(zip(in_refs[::2], in_refs[1::2], strict=True)):
        n = up_ref.shape[0]
        total = own_ref[first + start : first + start + n].astype(F32) + up_ref[...].astype(F32)
        out_ref[start : start + n] = (total + down_ref[...].astype(F32)).astype(BF16)
        copies.append(
            pltpu.make_async_copy(
                out_ref.at[pl.ds(start, n)], out_hbm.at[pl.ds(first + start, n)], sems.at[i]
            )
        )
        copies[-1].start()
        start += n
    for copy in copies:
        copy.wait()


def add_up(own, pairs, first=0, into=None):
    arrays = [x for pair in pairs for x in pair]
    rows = sum(up.shape[0] for up, _ in pairs)
    held, far = pl.BlockSpec(memory_space=pltpu.VMEM), pl.BlockSpec(memory_space=pltpu.HBM)
    more = [] if into is None else [in_hbm(into)]
    return pl.pallas_call(
        functools.partial(total_kernel, n_in=len(arrays), first=first),
        in_specs=[held] * (1 + len(arrays)) + [far] * len(more),
        out_specs=far,
        out_shape=pltpu.HBM(own.shape, BF16),
        input_output_aliases={1 + len(arrays): 0} if more else {},
        scratch_shapes=[
            pltpu.VMEM((rows, own.shape[1]), BF16),
            pltpu.SemaphoreType.DMA((len(pairs),)),
        ],
        compiler_params=pltpu.CompilerParams(vmem_limit_bytes=16 * MIB),
        cost_estimate=pl.CostEstimate(flops=1, bytes_accessed=1, transcendentals=0),
        name="add_up",
    )(own, *arrays, *more)


def per_device(stream_in, qkv_heads, expert_ids, gate_weights, w_out, w_gate, w_up, w_down):
    rows, width = stream_in.shape[1:]
    seq, exp = ("y", "core"), ("z", "x")
    n_y, n_seq, n_exp = lax.axis_size("y"), lax.axis_size(seq), lax.axis_size(exp)
    capacity = 3 * TOP * rows // (2 * n_exp)
    slots = n_exp * capacity

    def swap(x):
        return lax.ppermute(x, "core", [(0, 1), (1, 0)])

    def shift(x, by):
        return lax.ppermute(x, "y", [(i, (i + by) % n_y) for i in range(n_y)])

    def exchange(x):
        return lax.all_to_all(x, exp, split_axis=0, concat_axis=0, tiled=True)

    mine = [w[0] for w in (w_gate, w_up, w_down)]
    other = [swap(w) for w in mine]
    info = jnp.concatenate(
        [expert_ids[0].T.astype(F32), gate_weights[0].T, jnp.zeros((8 - 2 * TOP, rows), F32)]
    )
    info = plan(info, n_exp, capacity)
    info_far = shift(info, 2)
    qkv = spread(qkv_heads[0].transpose(1, 0, 2), n_seq)
    arrived = lax.all_to_all(qkv, seq, split_axis=0, concat_axis=0, tiled=True)
    context, w_held = attention(arrived, w_out)
    context, info_far, other = lax.optimization_barrier((context, info_far, other))
    merged = lax.all_to_all(context, seq, split_axis=0, concat_axis=0, tiled=True)
    mid, normed, buffer = project(merged, w_held, stream_in[0], info, slots)

    tie = lax.optimization_barrier
    far_tokens = shift(normed, 2)
    far_buffer = route(far_tokens, info_far, slots)
    own, far_buffer = tie((exchange(buffer), far_buffer))
    eighth = own.shape[0] // 8
    first, second = own[: 3 * eighth], own[3 * eighth : 6 * eighth]
    rest, first, second = tie((own, first, second))
    third = rest[6 * eighth :]
    third, far_buffer = tie((third, far_buffer))
    far_rows = exchange(far_buffer)

    def send(x):
        return shift(x, 1), shift(x, -1)

    def give_back(pair):
        return shift(pair[0], -1), shift(pair[1], 1)

    at_first, at_second = send(first), send(second)
    third, at_first = tie((third, at_first))
    at_third = send(third)
    own_part, *back = experts([own, *at_first], mine, other)
    home = [give_back(back)]
    far_rows, at_second, own_part = tie((far_rows, at_second, own_part))
    far_part, *back = experts([far_rows, *at_second], mine, other)
    home.append(give_back(back))
    at_third, far_part, home[0] = tie((at_third, far_part, home[0]))
    far_back = exchange(keep(far_part))
    back = experts(at_third, mine, other)
    home.append(give_back(back))
    far_sum = combine(info_far, far_back)
    total = add_up(own_part, home[:2])
    total = add_up(own_part, home[2:], 6 * eighth, total)
    total, far_back = tie((total, far_back))
    back = exchange(total)
    far_home = shift(far_sum, 2)
    return combine(info, back, mid, far_home)[None]


def solution(mesh):
    split = Mesh(mesh.devices.reshape(-1, 2, 4, 4), ("y", "core", "z", "x"))
    seq, exp = ("y", "core"), ("z", "x")
    in_specs = (
        P(exp, seq, None),
        P(exp, seq, None, None),
        P(exp, seq, None),
        P(exp, seq, None),
        P(),
        P(exp, None, seq),
        P(exp, None, seq),
        P(exp, seq, None),
    )
    return jax.shard_map(
        per_device, mesh=split, in_specs=in_specs, out_specs=P(exp, seq, None), check_vma=False
    )
```

```python
import functools

import jax
import jax.numpy as jnp
from jax import lax
from jax.experimental import pallas as pl
from jax.experimental.pallas import tpu as pltpu
from jax.sharding import Mesh
from jax.sharding import PartitionSpec as P

HD = 64
LANES = 128
MIB = 1 << 20
BF16 = jnp.bfloat16
F32 = jnp.float32
LOG2E = 1.4426950408889634
TOP = 2


def vmem(shape):
    return pl.BlockSpec(shape, lambda *_: (0,) * len(shape))


def attention_kernel(x_ref, w_hbm, out_ref, w_ref, sems, *, block):
    cuts = sems.shape[0]
    rows = w_hbm.shape[0] // cuts
    fetch = [
        pltpu.make_async_copy(
            w_hbm.at[pl.ds(i * rows, rows)], w_ref.at[pl.ds(i * rows, rows)], sems.at[i]
        )
        for i in range(cuts)
    ]

    @pl.when(pl.program_id(0) == 0)
    def _():
        for copy in fetch:
            copy.start()

    n_src, _, rows, lanes = x_ref.shape
    length = n_src * rows
    keys = x_ref[:, 1].reshape(length, lanes)
    values = x_ref[:, 2].reshape(length, lanes)
    wide = jnp.concatenate([values, jnp.ones((length, lanes), BF16)], axis=1)
    lane = lax.broadcasted_iota(jnp.int32, (1, lanes), 1)
    first = lane < HD
    scale = float(HD) ** (-0.5) * LOG2E
    per = block // rows
    for i in range(length // block):
        query = x_ref[i * per : (i + 1) * per, 0].reshape(block, lanes)
        parts = []
        for head in range(2):
            mine = jnp.where(first if head == 0 else ~first, query, jnp.zeros_like(query))
            scores = lax.dot_general(
                mine, keys, (((1,), (1,)), ((), ())), preferred_element_type=F32
            )
            top = jnp.max(scores, axis=1, keepdims=True)
            weights = jnp.exp2((scores - top) * scale).astype(BF16)
            both = jnp.dot(weights, wide, preferred_element_type=F32)
            parts.append(both[:, :lanes] / both[:, lanes:])
        context = jnp.where(first, parts[0], parts[1]).astype(BF16)
        out_ref[i * per : (i + 1) * per] = context.reshape(per, rows, lanes)

    @pl.when(pl.program_id(0) == pl.num_programs(0) - 1)
    def _():
        for copy in fetch:
            copy.wait()


def attention(arrived, w_out):
    n_src, three, rows, width = arrived.shape
    return pl.pallas_call(
        functools.partial(attention_kernel, block=2 * rows),
        grid=(width // LANES,),
        in_specs=[
            pl.BlockSpec((n_src, three, rows, LANES), lambda i: (0, 0, 0, i)),
            pl.BlockSpec(memory_space=pltpu.HBM),
        ],
        out_specs=[
            pl.BlockSpec((n_src, rows, LANES), lambda i: (0, 0, i)),
            pl.BlockSpec(memory_space=pl.ANY),
        ],
        out_shape=[
            jax.ShapeDtypeStruct((n_src, rows, width), BF16),
            pltpu.VMEM(w_out.shape, BF16),
        ],
        scratch_shapes=[pltpu.SemaphoreType.DMA((8,))],
        compiler_params=pltpu.CompilerParams(vmem_limit_bytes=24 * MIB),
        name="attention",
    )(arrived, in_hbm(w_out))


def plan_kernel(info_ref, out_ref, *, n_exp, capacity):
    info = info_ref[...]
    tokens = info.shape[1]
    ids = info[:TOP].astype(jnp.int32)
    expert = lax.broadcasted_iota(jnp.int32, (n_exp, tokens), 0)
    named = [expert == ids[k : k + 1] for k in range(TOP)]
    member = sum(n.astype(F32) for n in named)
    before = (
        lax.broadcasted_iota(jnp.int32, (tokens, tokens), 0)
        < lax.broadcasted_iota(jnp.int32, (tokens, tokens), 1)
    ).astype(F32)
    rank = jnp.dot(member.astype(BF16), before.astype(BF16), preferred_element_type=F32)
    out_ref[...] = info
    for k, n in enumerate(named):
        slot = jnp.sum(jnp.where(n, rank, 0.0), axis=0, keepdims=True)
        out_ref[2 * TOP + k : 2 * TOP + k + 1] = info[k : k + 1] * capacity + slot


def plan(info, n_exp, capacity):
    return pl.pallas_call(
        functools.partial(plan_kernel, n_exp=n_exp, capacity=capacity),
        grid=(1,),
        in_specs=[vmem(info.shape)],
        out_specs=vmem(info.shape),
        out_shape=jax.ShapeDtypeStruct(info.shape, F32),
        compiler_params=pltpu.CompilerParams(vmem_limit_bytes=4 * MIB),
        name="plan",
    )(info)


def fill(normed, info, out_ref):
    rows = info[2 * TOP : 3 * TOP].astype(jnp.int32)
    at = lax.broadcasted_iota(jnp.int32, (out_ref.shape[0], normed.shape[0]), 0)
    pick = sum((at == rows[k : k + 1]).astype(F32) for k in range(TOP)).astype(BF16)
    out_ref[...] = jnp.dot(pick, normed, preferred_element_type=F32).astype(BF16)


def project_kernel(
    ctx_ref, w_ref, stream_ref, info_ref, mid_hbm, normed_ref, out_ref, mid_ref, sem
):
    merged = jnp.concatenate([ctx_ref[s] for s in range(ctx_ref.shape[0])], axis=1)
    mid = stream_ref[...].astype(F32) + jnp.dot(
        merged, w_ref[...], preferred_element_type=F32
    )
    mid_ref[...] = mid
    copy = pltpu.make_async_copy(mid_ref, mid_hbm, sem)
    copy.start()
    factor = lax.rsqrt(jnp.mean(mid * mid, axis=1, keepdims=True) + 1e-06)
    normed = (mid * factor).astype(BF16)
    normed_ref[...] = normed
    fill(normed, info_ref[...], out_ref)
    copy.wait()


def project(merged, w_out, stream, info, slots):
    rows, width = stream.shape
    held = pl.BlockSpec(memory_space=pltpu.VMEM)
    return pl.pallas_call(
        project_kernel,
        in_specs=[held] * 4,
        out_specs=[pl.BlockSpec(memory_space=pltpu.HBM), held, held],
        out_shape=[
            pltpu.HBM((rows, width), F32),
            jax.ShapeDtypeStruct((rows, width), BF16),
            jax.ShapeDtypeStruct((slots, width), BF16),
        ],
        scratch_shapes=[pltpu.VMEM((rows, width), F32), pltpu.SemaphoreType.DMA(())],
        compiler_params=pltpu.CompilerParams(vmem_limit_bytes=24 * MIB),
        name="project",
    )(merged, pltpu.with_memory_space_constraint(w_out, pltpu.VMEM), stream, info)


def route_kernel(normed_ref, info_ref, out_ref):
    fill(normed_ref[...], info_ref[...], out_ref)


def route(normed, info, slots):
    rows, width = normed.shape
    return pl.pallas_call(
        route_kernel,
        grid=(1,),
        in_specs=[vmem(normed.shape), vmem(info.shape)],
        out_specs=vmem((slots, width)),
        out_shape=jax.ShapeDtypeStruct((slots, width), BF16),
        compiler_params=pltpu.CompilerParams(vmem_limit_bytes=16 * MIB),
        name="route",
    )(normed, info)


def expert_kernel(*refs, n_in, block):
    x_refs, w_refs = refs[:n_in], refs[n_in : n_in + 6]
    *out_refs, rows_ref, hidden_ref, gate_ref, up_ref, down_ref, x_sems, w_sems = refs[
        n_in + 6 :
    ]
    share = w_refs[0].shape[1]
    per = share // block

    def weight_copies(i):
        gate, up, down = w_refs[:3] if i < per else w_refs[3:]
        there, here = pl.ds(i % per * block, block), pl.ds(i * block, block)
        return (
            pltpu.make_async_copy(gate.at[:, there], gate_ref.at[:, here], w_sems.at[i, 0]),
            pltpu.make_async_copy(up.at[:, there], up_ref.at[:, here], w_sems.at[i, 1]),
            pltpu.make_async_copy(down.at[there], down_ref.at[here], w_sems.at[i, 2]),
        )

    row_copies, start = [], 0
    for i, ref in enumerate(x_refs):
        here = pl.ds(start, ref.shape[0])
        row_copies.append(pltpu.make_async_copy(ref, rows_ref.at[here], x_sems.at[i]))
        start += ref.shape[0]
    copies = [weight_copies(i) for i in range(2 * per)]
    for copy in (*row_copies, *copies[0], *copies[1]):
        copy.start()
    for copy in row_copies:
        copy.wait()
    rows = rows_ref[...]
    for i in range(2 * per):
        here = slice(i * block, (i + 1) * block)
        copies[i][0].wait()
        copies[i][1].wait()
        if i + 2 < 2 * per:
            for copy in copies[i + 2]:
                copy.start()
        gate = jnp.dot(rows, gate_ref[:, here], preferred_element_type=F32)
        up = jnp.dot(rows, up_ref[:, here], preferred_element_type=F32)
        half = 0.5 * gate
        hidden_ref[:, here] = ((half + half * jnp.tanh(half)) * up).astype(BF16)
    for copy in copies:
        copy[2].wait()
    total = jnp.dot(hidden_ref[...], down_ref[...], preferred_element_type=F32)
    start = 0
    for ref in out_refs:
        ref[...] = total[start : start + ref.shape[0]].astype(BF16)
        start += ref.shape[0]


def in_hbm(x):
    return pltpu.with_memory_space_constraint(x, pltpu.HBM)


def experts(arrays, mine, other):
    width = arrays[0].shape[1]
    hidden = 2 * mine[0].shape[1]
    total = sum(x.shape[0] for x in arrays)
    block = 256
    return pl.pallas_call(
        functools.partial(expert_kernel, n_in=len(arrays), block=block),
        grid=(1,),
        in_specs=[pl.BlockSpec(memory_space=pl.ANY)] * len(arrays)
        + [pl.BlockSpec(memory_space=pltpu.HBM)] * 6,
        out_specs=[vmem(x.shape) for x in arrays],
        out_shape=[pltpu.HBM(x.shape, BF16) for x in arrays],
        scratch_shapes=[
            pltpu.VMEM((total, width), BF16),
            pltpu.VMEM((total, hidden), BF16),
            pltpu.VMEM((width, hidden), BF16),
            pltpu.VMEM((width, hidden), BF16),
            pltpu.VMEM((hidden, width), BF16),
            pltpu.SemaphoreType.DMA((len(arrays),)),
            pltpu.SemaphoreType.DMA((hidden // block, 3)),
        ],
        compiler_params=pltpu.CompilerParams(vmem_limit_bytes=44 * MIB),
        cost_estimate=pl.CostEstimate(
            flops=600 * total * width * hidden,
            bytes_accessed=6 * width * hidden + 4 * total * width,
            transcendentals=total * hidden,
        ),
        name="experts",
    )(*arrays, *(in_hbm(w) for w in (*mine, *other)))


def keep_kernel(x_ref, out_ref):
    pass


def keep(x):
    return pl.pallas_call(
        keep_kernel,
        in_specs=[pl.BlockSpec(memory_space=pltpu.HBM)],
        out_specs=pl.BlockSpec(memory_space=pltpu.HBM),
        out_shape=pltpu.HBM(x.shape, x.dtype),
        input_output_aliases={0: 0},
        compiler_params=pltpu.CompilerParams(vmem_limit_bytes=MIB),
        cost_estimate=pl.CostEstimate(flops=100_000_000_000, bytes_accessed=1, transcendentals=0),
        name="keep",
    )(in_hbm(x))


def combine_kernel(info_ref, back_ref, *refs, cuts):
    by_token = info_ref[...].T
    rows = by_token[:, 2 * TOP : 3 * TOP].astype(jnp.int32)
    at = lax.broadcasted_iota(jnp.int32, (rows.shape[0], back_ref.shape[0]), 1)
    picks = [(at == rows[:, k : k + 1]).astype(F32).astype(BF16) for k in range(TOP)]
    gates = [by_token[:, TOP + k : TOP + k + 1] for k in range(TOP)]
    if len(refs) > 1:
        far_ref, mid_hbm, out_ref, mid_ref, sem = refs
        copy = pltpu.make_async_copy(mid_hbm, mid_ref, sem)
        copy.start()
    else:
        [out_ref], copy = refs, None
    cols = out_ref.shape[1] // cuts
    for i in range(cuts):
        here = slice(i * cols, (i + 1) * cols)
        back = back_ref[:, here]
        terms = [
            jnp.dot(pick, back, preferred_element_type=F32) * gate
            for pick, gate in zip(picks, gates, strict=True)
        ]
        total = sum(terms[1:], terms[0])
        if copy is not None:
            if i == 0:
                copy.wait()
            total = mid_ref[:, here] + far_ref[:, here].astype(F32) + total
        out_ref[:, here] = total.astype(BF16)


def combine(info, back, mid=None, far=None):
    rows, width = info.shape[1], back.shape[1]
    held = pl.BlockSpec(memory_space=pltpu.VMEM)
    final = mid is not None
    return pl.pallas_call(
        functools.partial(combine_kernel, cuts=4),
        in_specs=[held] * (3 if final else 2)
        + [pl.BlockSpec(memory_space=pltpu.HBM)] * final,
        out_specs=held,
        out_shape=jax.ShapeDtypeStruct((rows, width), BF16),
        scratch_shapes=[pltpu.VMEM((rows, width), F32), pltpu.SemaphoreType.DMA(())] * final,
        compiler_params=pltpu.CompilerParams(vmem_limit_bytes=16 * MIB),
        name="combine",
    )(info, back, *([far, in_hbm(mid)] if final else []))


def spread_kernel(x_hbm, out_hbm, x_ref, in_sems, out_sems):
    n_seq, three, _, part = out_hbm.shape
    copies = [
        pltpu.make_async_copy(x_hbm.at[j], x_ref.at[j], in_sems.at[j]) for j in range(three)
    ]
    for copy in copies:
        copy.start()
    out = []
    for j, copy in enumerate(copies):
        copy.wait()
        for i in range(n_seq):
            out.append(
                pltpu.make_async_copy(
                    x_ref.at[j, :, pl.ds(i * part, part)], out_hbm.at[i, j], out_sems.at[i, j]
                )
            )
            out[-1].start()
    for copy in out:
        copy.wait()


def spread(qkv, n_seq):
    three, rows, width = qkv.shape
    part = width // n_seq
    return pl.pallas_call(
        spread_kernel,
        in_specs=[pl.BlockSpec(memory_space=pltpu.HBM)],
        out_specs=pl.BlockSpec(memory_space=pltpu.HBM),
        out_shape=pltpu.HBM((n_seq, three, rows, part), BF16),
        scratch_shapes=[
            pltpu.VMEM(qkv.shape, BF16),
            pltpu.SemaphoreType.DMA((three,)),
            pltpu.SemaphoreType.DMA((n_seq, three)),
        ],
        compiler_params=pltpu.CompilerParams(vmem_limit_bytes=8 * MIB),
        name="spread",
    )(in_hbm(qkv))


def total_kernel(own_ref, *refs, n_in, first):
    in_refs, (out_hbm, out_ref, sems) = refs[:n_in], refs[-3:]
    start, copies = 0, []
    for i, (up_ref, down_ref) in enumerate(zip(in_refs[::2], in_refs[1::2], strict=True)):
        n = up_ref.shape[0]
        total = own_ref[first + start : first + start + n].astype(F32) + up_ref[...].astype(F32)
        out_ref[start : start + n] = (total + down_ref[...].astype(F32)).astype(BF16)
        copies.append(
            pltpu.make_async_copy(
                out_ref.at[pl.ds(start, n)], out_hbm.at[pl.ds(first + start, n)], sems.at[i]
            )
        )
        copies[-1].start()
        start += n
    for copy in copies:
        copy.wait()


def add_up(own, pairs, first=0, into=None):
    arrays = [x for pair in pairs for x in pair]
    rows = sum(up.shape[0] for up, _ in pairs)
    held, far = pl.BlockSpec(memory_space=pltpu.VMEM), pl.BlockSpec(memory_space=pltpu.HBM)
    more = [] if into is None else [in_hbm(into)]
    return pl.pallas_call(
        functools.partial(total_kernel, n_in=len(arrays), first=first),
        in_specs=[held] * (1 + len(arrays)) + [far] * len(more),
        out_specs=far,
        out_shape=pltpu.HBM(own.shape, BF16),
        input_output_aliases={1 + len(arrays): 0} if more else {},
        scratch_shapes=[
            pltpu.VMEM((rows, own.shape[1]), BF16),
            pltpu.SemaphoreType.DMA((len(pairs),)),
        ],
        compiler_params=pltpu.CompilerParams(vmem_limit_bytes=16 * MIB),
        cost_estimate=pl.CostEstimate(flops=1, bytes_accessed=1, transcendentals=0),
        name="add_up",
    )(own, *arrays, *more)


def per_device(stream_in, qkv_heads, expert_ids, gate_weights, w_out, w_gate, w_up, w_down):
    rows, width = stream_in.shape[1:]
    seq, exp = ("y", "core"), ("z", "x")
    n_y, n_seq, n_exp = lax.axis_size("y"), lax.axis_size(seq), lax.axis_size(exp)
    capacity = 3 * TOP * rows // (2 * n_exp)
    slots = n_exp * capacity

    def swap(x):
        return lax.ppermute(x, "core", [(0, 1), (1, 0)])

    def shift(x, by):
        return lax.ppermute(x, "y", [(i, (i + by) % n_y) for i in range(n_y)])

    def exchange(x):
        return lax.all_to_all(x, exp, split_axis=0, concat_axis=0, tiled=True)

    mine = [w[0] for w in (w_gate, w_up, w_down)]
    other = [swap(w) for w in mine]
    info = jnp.concatenate(
        [expert_ids[0].T.astype(F32), gate_weights[0].T, jnp.zeros((8 - 2 * TOP, rows), F32)]
    )
    info = plan(info, n_exp, capacity)
    info_far = shift(info, 2)
    qkv = spread(qkv_heads[0].transpose(1, 0, 2), n_seq)
    arrived = lax.all_to_all(qkv, seq, split_axis=0, concat_axis=0, tiled=True)
    context, w_held = attention(arrived, w_out)
    context, info_far, other = lax.optimization_barrier((context, info_far, other))
    merged = lax.all_to_all(context, seq, split_axis=0, concat_axis=0, tiled=True)
    mid, normed, buffer = project(merged, w_held, stream_in[0], info, slots)

    tie = lax.optimization_barrier
    far_tokens = shift(normed, 2)
    far_buffer = route(far_tokens, info_far, slots)
    own, far_buffer = tie((exchange(buffer), far_buffer))
    eighth = own.shape[0] // 8
    first, second = own[: 3 * eighth], own[3 * eighth : 6 * eighth]
    rest, first, second = tie((own, first, second))
    third = rest[6 * eighth :]
    third, far_buffer = tie((third, far_buffer))
    far_rows = exchange(far_buffer)

    def send(x):
        return shift(x, 1), shift(x, -1)

    def give_back(pair):
        return shift(pair[0], -1), shift(pair[1], 1)

    at_first, at_second = send(first), send(second)
    third, at_first = tie((third, at_first))
    at_third = send(third)
    [own_part] = experts([own], mine, other)
    at_first, own_part = tie((at_first, own_part))
    back = experts(at_first, mine, other)
    home = [give_back(back)]
    far_rows, at_second, back = tie((far_rows, at_second, back))
    far_part, *back = experts([far_rows, *at_second], mine, other)
    home.append(give_back(back))
    at_third, far_part, home[0] = tie((at_third, far_part, home[0]))
    far_back = exchange(keep(far_part))
    back = experts(at_third, mine, other)
    home.append(give_back(back))
    far_sum = combine(info_far, far_back)
    total = add_up(own_part, home[:2])
    total = add_up(own_part, home[2:], 6 * eighth, total)
    total, far_back = tie((total, far_back))
    back = exchange(total)
    far_home = shift(far_sum, 2)
    return combine(info, back, mid, far_home)[None]


def solution(mesh):
    split = Mesh(mesh.devices.reshape(-1, 2, 4, 4), ("y", "core", "z", "x"))
    seq, exp = ("y", "core"), ("z", "x")
    in_specs = (
        P(exp, seq, None),
        P(exp, seq, None, None),
        P(exp, seq, None),
        P(exp, seq, None),
        P(),
        P(exp, None, seq),
        P(exp, None, seq),
        P(exp, seq, None),
    )
    return jax.shard_map(
        per_device, mesh=split, in_specs=in_specs, out_specs=P(exp, seq, None), check_vma=False
    )
```

```python
import functools

import jax
import jax.numpy as jnp
from jax import lax
from jax.experimental import pallas as pl
from jax.experimental.pallas import tpu as pltpu
from jax.sharding import Mesh
from jax.sharding import PartitionSpec as P

HD = 64
LANES = 128
MIB = 1 << 20
BF16 = jnp.bfloat16
F32 = jnp.float32
LOG2E = 1.4426950408889634
TOP = 2


def vmem(shape):
    return pl.BlockSpec(shape, lambda *_: (0,) * len(shape))


def attention_kernel(x_ref, w_hbm, out_ref, w_ref, sems, *, block):
    cuts = sems.shape[0]
    rows = w_hbm.shape[0] // cuts
    fetch = [
        pltpu.make_async_copy(
            w_hbm.at[pl.ds(i * rows, rows)], w_ref.at[pl.ds(i * rows, rows)], sems.at[i]
        )
        for i in range(cuts)
    ]

    @pl.when(pl.program_id(0) == 0)
    def _():
        for copy in fetch:
            copy.start()

    n_src, _, rows, lanes = x_ref.shape
    length = n_src * rows
    keys = x_ref[:, 1].reshape(length, lanes)
    values = x_ref[:, 2].reshape(length, lanes)
    wide = jnp.concatenate([values, jnp.ones((length, lanes), BF16)], axis=1)
    lane = lax.broadcasted_iota(jnp.int32, (1, lanes), 1)
    first = lane < HD
    scale = float(HD) ** (-0.5) * LOG2E
    per = block // rows
    for i in range(length // block):
        query = x_ref[i * per : (i + 1) * per, 0].reshape(block, lanes)
        parts = []
        for head in range(2):
            mine = jnp.where(first if head == 0 else ~first, query, jnp.zeros_like(query))
            scores = lax.dot_general(
                mine, keys, (((1,), (1,)), ((), ())), preferred_element_type=F32
            )
            top = jnp.max(scores, axis=1, keepdims=True)
            weights = jnp.exp2((scores - top) * scale).astype(BF16)
            both = jnp.dot(weights, wide, preferred_element_type=F32)
            parts.append(both[:, :lanes] / both[:, lanes:])
        context = jnp.where(first, parts[0], parts[1]).astype(BF16)
        out_ref[i * per : (i + 1) * per] = context.reshape(per, rows, lanes)

    @pl.when(pl.program_id(0) == pl.num_programs(0) - 1)
    def _():
        for copy in fetch:
            copy.wait()


def attention(arrived, w_out):
    n_src, three, rows, width = arrived.shape
    return pl.pallas_call(
        functools.partial(attention_kernel, block=2 * rows),
        grid=(width // LANES,),
        in_specs=[
            pl.BlockSpec((n_src, three, rows, LANES), lambda i: (0, 0, 0, i)),
            pl.BlockSpec(memory_space=pltpu.HBM),
        ],
        out_specs=[
            pl.BlockSpec((n_src, rows, LANES), lambda i: (0, 0, i)),
            pl.BlockSpec(memory_space=pl.ANY),
        ],
        out_shape=[
            jax.ShapeDtypeStruct((n_src, rows, width), BF16),
            pltpu.VMEM(w_out.shape, BF16),
        ],
        scratch_shapes=[pltpu.SemaphoreType.DMA((8,))],
        compiler_params=pltpu.CompilerParams(vmem_limit_bytes=24 * MIB),
        name="attention",
    )(arrived, in_hbm(w_out))


def plan_kernel(info_ref, out_ref, *, n_exp, capacity):
    info = info_ref[...]
    tokens = info.shape[1]
    ids = info[:TOP].astype(jnp.int32)
    expert = lax.broadcasted_iota(jnp.int32, (n_exp, tokens), 0)
    named = [expert == ids[k : k + 1] for k in range(TOP)]
    member = sum(n.astype(F32) for n in named)
    before = (
        lax.broadcasted_iota(jnp.int32, (tokens, tokens), 0)
        < lax.broadcasted_iota(jnp.int32, (tokens, tokens), 1)
    ).astype(F32)
    rank = jnp.dot(member.astype(BF16), before.astype(BF16), preferred_element_type=F32)
    out_ref[...] = info
    for k, n in enumerate(named):
        slot = jnp.sum(jnp.where(n, rank, 0.0), axis=0, keepdims=True)
        out_ref[2 * TOP + k : 2 * TOP + k + 1] = info[k : k + 1] * capacity + slot


def plan(info, n_exp, capacity):
    return pl.pallas_call(
        functools.partial(plan_kernel, n_exp=n_exp, capacity=capacity),
        grid=(1,),
        in_specs=[vmem(info.shape)],
        out_specs=vmem(info.shape),
        out_shape=jax.ShapeDtypeStruct(info.shape, F32),
        compiler_params=pltpu.CompilerParams(vmem_limit_bytes=4 * MIB),
        name="plan",
    )(info)


def fill(normed, info, out_ref):
    rows = info[2 * TOP : 3 * TOP].astype(jnp.int32)
    at = lax.broadcasted_iota(jnp.int32, (out_ref.shape[0], normed.shape[0]), 0)
    pick = sum((at == rows[k : k + 1]).astype(F32) for k in range(TOP)).astype(BF16)
    out_ref[...] = jnp.dot(pick, normed, preferred_element_type=F32).astype(BF16)


def project_kernel(
    ctx_ref, w_ref, stream_ref, info_ref, mid_hbm, normed_ref, out_ref, mid_ref, sem
):
    merged = jnp.concatenate([ctx_ref[s] for s in range(ctx_ref.shape[0])], axis=1)
    mid = stream_ref[...].astype(F32) + jnp.dot(
        merged, w_ref[...], preferred_element_type=F32
    )
    mid_ref[...] = mid
    copy = pltpu.make_async_copy(mid_ref, mid_hbm, sem)
    copy.start()
    factor = lax.rsqrt(jnp.mean(mid * mid, axis=1, keepdims=True) + 1e-06)
    normed = (mid * factor).astype(BF16)
    normed_ref[...] = normed
    fill(normed, info_ref[...], out_ref)
    copy.wait()


def project(merged, w_out, stream, info, slots):
    rows, width = stream.shape
    held = pl.BlockSpec(memory_space=pltpu.VMEM)
    return pl.pallas_call(
        project_kernel,
        in_specs=[held] * 4,
        out_specs=[pl.BlockSpec(memory_space=pltpu.HBM), held, held],
        out_shape=[
            pltpu.HBM((rows, width), F32),
            jax.ShapeDtypeStruct((rows, width), BF16),
            jax.ShapeDtypeStruct((slots, width), BF16),
        ],
        scratch_shapes=[pltpu.VMEM((rows, width), F32), pltpu.SemaphoreType.DMA(())],
        compiler_params=pltpu.CompilerParams(vmem_limit_bytes=24 * MIB),
        name="project",
    )(merged, pltpu.with_memory_space_constraint(w_out, pltpu.VMEM), stream, info)


def route_kernel(normed_ref, info_ref, out_ref):
    fill(normed_ref[...], info_ref[...], out_ref)


def route(normed, info, slots):
    rows, width = normed.shape
    return pl.pallas_call(
        route_kernel,
        grid=(1,),
        in_specs=[vmem(normed.shape), vmem(info.shape)],
        out_specs=vmem((slots, width)),
        out_shape=jax.ShapeDtypeStruct((slots, width), BF16),
        compiler_params=pltpu.CompilerParams(vmem_limit_bytes=16 * MIB),
        name="route",
    )(normed, info)


def expert_kernel(*refs, n_in, block):
    x_refs, w_refs = refs[:n_in], refs[n_in : n_in + 6]
    out_refs = refs[n_in + 6 : 2 * n_in + 6]
    rows_ref, total_ref, hidden_ref, gate_ref, up_ref, down_ref, x_sems, w_sems, out_sems = refs[
        2 * n_in + 6 :
    ]
    share = w_refs[0].shape[1]
    per = share // block

    def weight_copies(i):
        gate, up, down = w_refs[:3] if i < per else w_refs[3:]
        there, here = pl.ds(i % per * block, block), pl.ds(i * block, block)
        return (
            pltpu.make_async_copy(gate.at[:, there], gate_ref.at[:, here], w_sems.at[i, 0]),
            pltpu.make_async_copy(up.at[:, there], up_ref.at[:, here], w_sems.at[i, 1]),
            pltpu.make_async_copy(down.at[there], down_ref.at[here], w_sems.at[i, 2]),
        )

    row_copies, start = [], 0
    for i, ref in enumerate(x_refs):
        here = pl.ds(start, ref.shape[0])
        row_copies.append(pltpu.make_async_copy(ref, rows_ref.at[here], x_sems.at[i]))
        start += ref.shape[0]
    copies = [weight_copies(i) for i in range(2 * per)]
    for copy in (*row_copies, *copies[0], *copies[1]):
        copy.start()
    for copy in row_copies:
        copy.wait()
    rows = rows_ref[...]
    for i in range(2 * per):
        here = slice(i * block, (i + 1) * block)
        copies[i][0].wait()
        copies[i][1].wait()
        if i + 2 < 2 * per:
            for copy in copies[i + 2]:
                copy.start()
        gate = jnp.dot(rows, gate_ref[:, here], preferred_element_type=F32)
        up = jnp.dot(rows, up_ref[:, here], preferred_element_type=F32)
        half = 0.5 * gate
        hidden_ref[:, here] = ((half + half * jnp.tanh(half)) * up).astype(BF16)
    for copy in copies:
        copy[2].wait()
    cuts = out_sems.shape[1]
    cols = out_refs[0].shape[1] // cuts
    flushes = []
    for j in range(cuts):
        here = slice(j * cols, (j + 1) * cols)
        total = jnp.dot(hidden_ref[...], down_ref[:, here], preferred_element_type=F32)
        total_ref[:, here] = total.astype(BF16)
        start = 0
        for i, ref in enumerate(out_refs):
            n, lanes = ref.shape[0], pl.ds(j * cols, cols)
            flushes.append(
                pltpu.make_async_copy(
                    total_ref.at[pl.ds(start, n), lanes], ref.at[:, lanes], out_sems.at[i, j]
                )
            )
            flushes[-1].start()
            start += n
    for flush in flushes:
        flush.wait()


def in_hbm(x):
    return pltpu.with_memory_space_constraint(x, pltpu.HBM)


def experts(arrays, mine, other):
    width = arrays[0].shape[1]
    hidden = 2 * mine[0].shape[1]
    total = sum(x.shape[0] for x in arrays)
    block = 256
    return pl.pallas_call(
        functools.partial(expert_kernel, n_in=len(arrays), block=block),
        grid=(1,),
        in_specs=[pl.BlockSpec(memory_space=pl.ANY)] * len(arrays)
        + [pl.BlockSpec(memory_space=pltpu.HBM)] * 6,
        out_specs=[pl.BlockSpec(memory_space=pltpu.HBM)] * len(arrays),
        out_shape=[pltpu.HBM(x.shape, BF16) for x in arrays],
        scratch_shapes=[
            pltpu.VMEM((total, width), BF16),
            pltpu.VMEM((total, width), BF16),
            pltpu.VMEM((total, hidden), BF16),
            pltpu.VMEM((width, hidden), BF16),
            pltpu.VMEM((width, hidden), BF16),
            pltpu.VMEM((hidden, width), BF16),
            pltpu.SemaphoreType.DMA((len(arrays),)),
            pltpu.SemaphoreType.DMA((hidden // block, 3)),
            pltpu.SemaphoreType.DMA((len(arrays), 4)),
        ],
        compiler_params=pltpu.CompilerParams(vmem_limit_bytes=44 * MIB),
        cost_estimate=pl.CostEstimate(
            flops=600 * total * width * hidden,
            bytes_accessed=6 * width * hidden + 4 * total * width,
            transcendentals=total * hidden,
        ),
        name="experts",
    )(*arrays, *(in_hbm(w) for w in (*mine, *other)))


def keep_kernel(x_ref, out_ref):
    pass


def keep(x):
    return pl.pallas_call(
        keep_kernel,
        in_specs=[pl.BlockSpec(memory_space=pltpu.HBM)],
        out_specs=pl.BlockSpec(memory_space=pltpu.HBM),
        out_shape=pltpu.HBM(x.shape, x.dtype),
        input_output_aliases={0: 0},
        compiler_params=pltpu.CompilerParams(vmem_limit_bytes=MIB),
        cost_estimate=pl.CostEstimate(flops=100_000_000_000, bytes_accessed=1, transcendentals=0),
        name="keep",
    )(in_hbm(x))


def weighted(info, back_ref, out_ref, cuts, base):
    by_token = info.T
    rows = by_token[:, 2 * TOP : 3 * TOP].astype(jnp.int32)
    at = lax.broadcasted_iota(jnp.int32, (rows.shape[0], back_ref.shape[0]), 1)
    picks = [(at == rows[:, k : k + 1]).astype(F32).astype(BF16) for k in range(TOP)]
    gates = [by_token[:, TOP + k : TOP + k + 1] for k in range(TOP)]
    cols = out_ref.shape[1] // cuts
    for i in range(cuts):
        here = slice(i * cols, (i + 1) * cols)
        back = back_ref[:, here]
        terms = [
            jnp.dot(pick, back, preferred_element_type=F32) * gate
            for pick, gate in zip(picks, gates, strict=True)
        ]
        total = sum(terms[1:], terms[0])
        if base is not None:
            total = base(here) + total
        out_ref[:, here] = total.astype(BF16)


def combine_far_kernel(info_ref, back_ref, mid_hbm, out_ref, mid_ref, sem, *, cuts):
    copy = pltpu.make_async_copy(mid_hbm, mid_ref, sem)
    copy.start()
    weighted(info_ref[...], back_ref, out_ref, cuts, None)
    copy.wait()


def combine_far(info, back, mid):
    rows, width = info.shape[1], back.shape[1]
    held = pl.BlockSpec(memory_space=pltpu.VMEM)
    return pl.pallas_call(
        functools.partial(combine_far_kernel, cuts=4),
        in_specs=[held, held, pl.BlockSpec(memory_space=pltpu.HBM)],
        out_specs=[held, pl.BlockSpec(memory_space=pl.ANY)],
        out_shape=[
            jax.ShapeDtypeStruct((rows, width), BF16),
            pltpu.VMEM((rows, width), F32),
        ],
        scratch_shapes=[pltpu.SemaphoreType.DMA(())],
        compiler_params=pltpu.CompilerParams(vmem_limit_bytes=16 * MIB),
        name="combine_far",
    )(info, back, in_hbm(mid))


def combine_kernel(info_ref, back_ref, far_ref, mid_ref, out_ref, *, cuts):
    def base(here):
        return mid_ref[:, here] + far_ref[:, here].astype(F32)

    weighted(info_ref[...], back_ref, out_ref, cuts, base)


def combine(info, back, mid, far):
    rows, width = mid.shape
    return pl.pallas_call(
        functools.partial(combine_kernel, cuts=4),
        in_specs=[pl.BlockSpec(memory_space=pltpu.VMEM)] * 4,
        out_specs=pl.BlockSpec(memory_space=pltpu.VMEM),
        out_shape=jax.ShapeDtypeStruct((rows, width), BF16),
        compiler_params=pltpu.CompilerParams(vmem_limit_bytes=16 * MIB),
        name="combine",
    )(info, back, far, pltpu.with_memory_space_constraint(mid, pltpu.VMEM))


def spread_kernel(x_hbm, out_hbm, x_ref, in_sems, out_sems):
    n_seq, three, _, part = out_hbm.shape
    copies = [
        pltpu.make_async_copy(x_hbm.at[j], x_ref.at[j], in_sems.at[j]) for j in range(three)
    ]
    for copy in copies:
        copy.start()
    out = []
    for j, copy in enumerate(copies):
        copy.wait()
        for i in range(n_seq):
            out.append(
                pltpu.make_async_copy(
                    x_ref.at[j, :, pl.ds(i * part, part)], out_hbm.at[i, j], out_sems.at[i, j]
                )
            )
            out[-1].start()
    for copy in out:
        copy.wait()


def spread(qkv, n_seq):
    three, rows, width = qkv.shape
    part = width // n_seq
    return pl.pallas_call(
        spread_kernel,
        in_specs=[pl.BlockSpec(memory_space=pltpu.HBM)],
        out_specs=pl.BlockSpec(memory_space=pltpu.HBM),
        out_shape=pltpu.HBM((n_seq, three, rows, part), BF16),
        scratch_shapes=[
            pltpu.VMEM(qkv.shape, BF16),
            pltpu.SemaphoreType.DMA((three,)),
            pltpu.SemaphoreType.DMA((n_seq, three)),
        ],
        compiler_params=pltpu.CompilerParams(vmem_limit_bytes=8 * MIB),
        name="spread",
    )(in_hbm(qkv))


def total_kernel(own_ref, *refs, n_in, first):
    in_refs, (out_hbm, out_ref, sems) = refs[:n_in], refs[-3:]
    start, copies = 0, []
    for i, (up_ref, down_ref) in enumerate(zip(in_refs[::2], in_refs[1::2], strict=True)):
        n = up_ref.shape[0]
        total = own_ref[first + start : first + start + n].astype(F32) + up_ref[...].astype(F32)
        out_ref[start : start + n] = (total + down_ref[...].astype(F32)).astype(BF16)
        copies.append(
            pltpu.make_async_copy(
                out_ref.at[pl.ds(start, n)], out_hbm.at[pl.ds(first + start, n)], sems.at[i]
            )
        )
        copies[-1].start()
        start += n
    for copy in copies:
        copy.wait()


def add_up(own, pairs, first=0, into=None):
    arrays = [x for pair in pairs for x in pair]
    rows = sum(up.shape[0] for up, _ in pairs)
    held, far = pl.BlockSpec(memory_space=pltpu.VMEM), pl.BlockSpec(memory_space=pltpu.HBM)
    more = [] if into is None else [in_hbm(into)]
    return pl.pallas_call(
        functools.partial(total_kernel, n_in=len(arrays), first=first),
        in_specs=[held] * (1 + len(arrays)) + [far] * len(more),
        out_specs=far,
        out_shape=pltpu.HBM(own.shape, BF16),
        input_output_aliases={1 + len(arrays): 0} if more else {},
        scratch_shapes=[
            pltpu.VMEM((rows, own.shape[1]), BF16),
            pltpu.SemaphoreType.DMA((len(pairs),)),
        ],
        compiler_params=pltpu.CompilerParams(vmem_limit_bytes=16 * MIB),
        cost_estimate=pl.CostEstimate(flops=1, bytes_accessed=1, transcendentals=0),
        name="add_up",
    )(own, *arrays, *more)


def per_device(stream_in, qkv_heads, expert_ids, gate_weights, w_out, w_gate, w_up, w_down):
    rows, width = stream_in.shape[1:]
    seq, exp = ("y", "core"), ("z", "x")
    n_y, n_seq, n_exp = lax.axis_size("y"), lax.axis_size(seq), lax.axis_size(exp)
    capacity = 3 * TOP * rows // (2 * n_exp)
    slots = n_exp * capacity

    def swap(x):
        return lax.ppermute(x, "core", [(0, 1), (1, 0)])

    def shift(x, by):
        return lax.ppermute(x, "y", [(i, (i + by) % n_y) for i in range(n_y)])

    def exchange(x):
        return lax.all_to_all(x, exp, split_axis=0, concat_axis=0, tiled=True)

    mine = [w[0] for w in (w_gate, w_up, w_down)]
    other = [swap(w) for w in mine]
    info = jnp.concatenate(
        [expert_ids[0].T.astype(F32), gate_weights[0].T, jnp.zeros((8 - 2 * TOP, rows), F32)]
    )
    info = plan(info, n_exp, capacity)
    info_far = shift(info, 2)
    qkv = spread(qkv_heads[0].transpose(1, 0, 2), n_seq)
    arrived = lax.all_to_all(qkv, seq, split_axis=0, concat_axis=0, tiled=True)
    context, w_held = attention(arrived, w_out)
    context, info_far, other = lax.optimization_barrier((context, info_far, other))
    merged = lax.all_to_all(context, seq, split_axis=0, concat_axis=0, tiled=True)
    mid, normed, buffer = project(merged, w_held, stream_in[0], info, slots)

    tie = lax.optimization_barrier
    far_tokens = shift(normed, 2)
    far_buffer = route(far_tokens, info_far, slots)
    own, far_buffer = tie((exchange(buffer), far_buffer))
    eighth = own.shape[0] // 8
    first, second = own[: 3 * eighth], own[3 * eighth : 6 * eighth]
    rest, first, second = tie((own, first, second))
    third = rest[6 * eighth :]
    third, far_buffer = tie((third, far_buffer))
    far_rows = exchange(far_buffer)

    def send(x):
        return shift(x, 1), shift(x, -1)

    def give_back(pair):
        return shift(pair[0], -1), shift(pair[1], 1)

    at_first, at_second = send(first), send(second)
    third, at_first = tie((third, at_first))
    at_third = send(third)
    own_part, *back = experts([own, *at_first], mine, other)
    home = [give_back(back)]
    far_rows, at_second, own_part = tie((far_rows, at_second, own_part))
    far_part, *back = experts([far_rows, *at_second], mine, other)
    home.append(give_back(back))
    at_third, far_part, home[0] = tie((at_third, far_part, home[0]))
    far_back = exchange(keep(far_part))
    back = experts(at_third, mine, other)
    home.append(give_back(back))
    far_sum, mid = combine_far(info_far, far_back, mid)
    total = add_up(own_part, home[:2])
    total = add_up(own_part, home[2:], 6 * eighth, total)
    total, far_back = tie((total, far_back))
    back = exchange(total)
    far_home = shift(far_sum, 2)
    return combine(info, back, mid, far_home)[None]


def solution(mesh):
    split = Mesh(mesh.devices.reshape(-1, 2, 4, 4), ("y", "core", "z", "x"))
    seq, exp = ("y", "core"), ("z", "x")
    in_specs = (
        P(exp, seq, None),
        P(exp, seq, None, None),
        P(exp, seq, None),
        P(exp, seq, None),
        P(),
        P(exp, None, seq),
        P(exp, None, seq),
        P(exp, seq, None),
    )
    return jax.shard_map(
        per_device, mesh=split, in_specs=in_specs, out_specs=P(exp, seq, None), check_vma=False
    )
```

```python
import functools

import jax
import jax.numpy as jnp
from jax import lax
from jax.experimental import pallas as pl
from jax.experimental.pallas import tpu as pltpu
from jax.sharding import Mesh
from jax.sharding import PartitionSpec as P

HD = 64
LANES = 128
MIB = 1 << 20
BF16 = jnp.bfloat16
F32 = jnp.float32
LOG2E = 1.4426950408889634
TOP = 2


def vmem(shape):
    return pl.BlockSpec(shape, lambda *_: (0,) * len(shape))


def attention_kernel(x_ref, w_hbm, out_ref, w_ref, sems, *, block):
    cuts = sems.shape[0]
    rows = w_hbm.shape[0] // cuts
    fetch = [
        pltpu.make_async_copy(
            w_hbm.at[pl.ds(i * rows, rows)], w_ref.at[pl.ds(i * rows, rows)], sems.at[i]
        )
        for i in range(cuts)
    ]

    @pl.when(pl.program_id(0) == 0)
    def _():
        for copy in fetch:
            copy.start()

    n_src, _, rows, lanes = x_ref.shape
    length = n_src * rows
    keys = x_ref[:, 1].reshape(length, lanes)
    values = x_ref[:, 2].reshape(length, lanes)
    wide = jnp.concatenate([values, jnp.ones((length, lanes), BF16)], axis=1)
    lane = lax.broadcasted_iota(jnp.int32, (1, lanes), 1)
    first = lane < HD
    scale = float(HD) ** (-0.5) * LOG2E
    per = block // rows
    for i in range(length // block):
        query = x_ref[i * per : (i + 1) * per, 0].reshape(block, lanes)
        parts = []
        for head in range(2):
            mine = jnp.where(first if head == 0 else ~first, query, jnp.zeros_like(query))
            scores = lax.dot_general(
                mine, keys, (((1,), (1,)), ((), ())), preferred_element_type=F32
            )
            top = jnp.max(scores, axis=1, keepdims=True)
            weights = jnp.exp2((scores - top) * scale).astype(BF16)
            both = jnp.dot(weights, wide, preferred_element_type=F32)
            parts.append(both[:, :lanes] / both[:, lanes:])
        context = jnp.where(first, parts[0], parts[1]).astype(BF16)
        out_ref[i * per : (i + 1) * per] = context.reshape(per, rows, lanes)

    @pl.when(pl.program_id(0) == pl.num_programs(0) - 1)
    def _():
        for copy in fetch:
            copy.wait()


def attention(arrived, w_out):
    n_src, three, rows, width = arrived.shape
    return pl.pallas_call(
        functools.partial(attention_kernel, block=2 * rows),
        grid=(width // LANES,),
        in_specs=[
            pl.BlockSpec((n_src, three, rows, LANES), lambda i: (0, 0, 0, i)),
            pl.BlockSpec(memory_space=pltpu.HBM),
        ],
        out_specs=[
            pl.BlockSpec((n_src, rows, LANES), lambda i: (0, 0, i)),
            pl.BlockSpec(memory_space=pl.ANY),
        ],
        out_shape=[
            jax.ShapeDtypeStruct((n_src, rows, width), BF16),
            pltpu.VMEM(w_out.shape, BF16),
        ],
        scratch_shapes=[pltpu.SemaphoreType.DMA((8,))],
        compiler_params=pltpu.CompilerParams(vmem_limit_bytes=24 * MIB),
        name="attention",
    )(arrived, in_hbm(w_out))


def plan_kernel(info_ref, out_ref, *, n_exp, capacity):
    info = info_ref[...]
    tokens = info.shape[1]
    ids = info[:TOP].astype(jnp.int32)
    expert = lax.broadcasted_iota(jnp.int32, (n_exp, tokens), 0)
    named = [expert == ids[k : k + 1] for k in range(TOP)]
    member = sum(n.astype(F32) for n in named)
    before = (
        lax.broadcasted_iota(jnp.int32, (tokens, tokens), 0)
        < lax.broadcasted_iota(jnp.int32, (tokens, tokens), 1)
    ).astype(F32)
    rank = jnp.dot(member.astype(BF16), before.astype(BF16), preferred_element_type=F32)
    out_ref[...] = info
    for k, n in enumerate(named):
        slot = jnp.sum(jnp.where(n, rank, 0.0), axis=0, keepdims=True)
        out_ref[2 * TOP + k : 2 * TOP + k + 1] = info[k : k + 1] * capacity + slot


def plan(info, n_exp, capacity):
    return pl.pallas_call(
        functools.partial(plan_kernel, n_exp=n_exp, capacity=capacity),
        grid=(1,),
        in_specs=[vmem(info.shape)],
        out_specs=vmem(info.shape),
        out_shape=jax.ShapeDtypeStruct(info.shape, F32),
        compiler_params=pltpu.CompilerParams(vmem_limit_bytes=4 * MIB),
        name="plan",
    )(info)


def fill(normed, info, out_ref):
    rows = info[2 * TOP : 3 * TOP].astype(jnp.int32)
    at = lax.broadcasted_iota(jnp.int32, (out_ref.shape[0], normed.shape[0]), 0)
    pick = sum((at == rows[k : k + 1]).astype(F32) for k in range(TOP)).astype(BF16)
    out_ref[...] = jnp.dot(pick, normed, preferred_element_type=F32).astype(BF16)


def project_kernel(
    ctx_ref, w_ref, stream_ref, info_ref, mid_hbm, normed_ref, out_ref, mid_ref, sem
):
    merged = jnp.concatenate([ctx_ref[s] for s in range(ctx_ref.shape[0])], axis=1)
    mid = stream_ref[...].astype(F32) + jnp.dot(
        merged, w_ref[...], preferred_element_type=F32
    )
    mid_ref[...] = mid
    copy = pltpu.make_async_copy(mid_ref, mid_hbm, sem)
    copy.start()
    factor = lax.rsqrt(jnp.mean(mid * mid, axis=1, keepdims=True) + 1e-06)
    normed = (mid * factor).astype(BF16)
    normed_ref[...] = normed
    fill(normed, info_ref[...], out_ref)
    copy.wait()


def project(merged, w_out, stream, info, slots):
    rows, width = stream.shape
    held = pl.BlockSpec(memory_space=pltpu.VMEM)
    return pl.pallas_call(
        project_kernel,
        in_specs=[held] * 4,
        out_specs=[pl.BlockSpec(memory_space=pltpu.HBM), held, held],
        out_shape=[
            pltpu.HBM((rows, width), F32),
            jax.ShapeDtypeStruct((rows, width), BF16),
            jax.ShapeDtypeStruct((slots, width), BF16),
        ],
        scratch_shapes=[pltpu.VMEM((rows, width), F32), pltpu.SemaphoreType.DMA(())],
        compiler_params=pltpu.CompilerParams(vmem_limit_bytes=24 * MIB),
        name="project",
    )(merged, pltpu.with_memory_space_constraint(w_out, pltpu.VMEM), stream, info)


def route_kernel(normed_ref, info_ref, out_ref):
    fill(normed_ref[...], info_ref[...], out_ref)


def route(normed, info, slots):
    rows, width = normed.shape
    return pl.pallas_call(
        route_kernel,
        grid=(1,),
        in_specs=[vmem(normed.shape), vmem(info.shape)],
        out_specs=vmem((slots, width)),
        out_shape=jax.ShapeDtypeStruct((slots, width), BF16),
        compiler_params=pltpu.CompilerParams(vmem_limit_bytes=16 * MIB),
        name="route",
    )(normed, info)


def expert_kernel(*refs, n_in, block):
    x_refs, w_refs = refs[:n_in], refs[n_in : n_in + 6]
    out_refs = refs[n_in + 6 : 2 * n_in + 6]
    rows_ref, total_ref, hidden_ref, gate_ref, up_ref, down_ref, x_sems, w_sems, out_sems = refs[
        2 * n_in + 6 :
    ]
    share = w_refs[0].shape[1]
    per = share // block

    def weight_copies(i):
        gate, up, down = w_refs[:3] if i < per else w_refs[3:]
        there, here = pl.ds(i % per * block, block), pl.ds(i * block, block)
        return (
            pltpu.make_async_copy(gate.at[:, there], gate_ref.at[:, here], w_sems.at[i, 0]),
            pltpu.make_async_copy(up.at[:, there], up_ref.at[:, here], w_sems.at[i, 1]),
            pltpu.make_async_copy(down.at[there], down_ref.at[here], w_sems.at[i, 2]),
        )

    row_copies, start = [], 0
    for i, ref in enumerate(x_refs):
        here = pl.ds(start, ref.shape[0])
        row_copies.append(pltpu.make_async_copy(ref, rows_ref.at[here], x_sems.at[i]))
        start += ref.shape[0]
    copies = [weight_copies(i) for i in range(2 * per)]
    for copy in (*row_copies, *copies[0], *copies[1]):
        copy.start()
    for copy in row_copies:
        copy.wait()
    rows = rows_ref[...]
    for i in range(2 * per):
        here = slice(i * block, (i + 1) * block)
        copies[i][0].wait()
        copies[i][1].wait()
        if i + 2 < 2 * per:
            for copy in copies[i + 2]:
                copy.start()
        gate = jnp.dot(rows, gate_ref[:, here], preferred_element_type=F32)
        up = jnp.dot(rows, up_ref[:, here], preferred_element_type=F32)
        half = 0.5 * gate
        hidden_ref[:, here] = ((half + half * jnp.tanh(half)) * up).astype(BF16)
    for copy in copies:
        copy[2].wait()
    cuts = out_sems.shape[1]
    cols = out_refs[0].shape[1] // cuts
    flushes = []
    for j in range(cuts):
        here = slice(j * cols, (j + 1) * cols)
        total = jnp.dot(hidden_ref[...], down_ref[:, here], preferred_element_type=F32)
        total_ref[:, here] = total.astype(BF16)
        start = 0
        for i, ref in enumerate(out_refs):
            n, lanes = ref.shape[0], pl.ds(j * cols, cols)
            flushes.append(
                pltpu.make_async_copy(
                    total_ref.at[pl.ds(start, n), lanes], ref.at[:, lanes], out_sems.at[i, j]
                )
            )
            flushes[-1].start()
            start += n
    for flush in flushes:
        flush.wait()


def in_hbm(x):
    return pltpu.with_memory_space_constraint(x, pltpu.HBM)


def experts(arrays, mine, other):
    width = arrays[0].shape[1]
    hidden = 2 * mine[0].shape[1]
    total = sum(x.shape[0] for x in arrays)
    block = 256
    return pl.pallas_call(
        functools.partial(expert_kernel, n_in=len(arrays), block=block),
        grid=(1,),
        in_specs=[pl.BlockSpec(memory_space=pl.ANY)] * len(arrays)
        + [pl.BlockSpec(memory_space=pltpu.HBM)] * 6,
        out_specs=[pl.BlockSpec(memory_space=pltpu.HBM)] * len(arrays),
        out_shape=[pltpu.HBM(x.shape, BF16) for x in arrays],
        scratch_shapes=[
            pltpu.VMEM((total, width), BF16),
            pltpu.VMEM((total, width), BF16),
            pltpu.VMEM((total, hidden), BF16),
            pltpu.VMEM((width, hidden), BF16),
            pltpu.VMEM((width, hidden), BF16),
            pltpu.VMEM((hidden, width), BF16),
            pltpu.SemaphoreType.DMA((len(arrays),)),
            pltpu.SemaphoreType.DMA((hidden // block, 3)),
            pltpu.SemaphoreType.DMA((len(arrays), 4)),
        ],
        compiler_params=pltpu.CompilerParams(vmem_limit_bytes=44 * MIB),
        cost_estimate=pl.CostEstimate(
            flops=600 * total * width * hidden,
            bytes_accessed=6 * width * hidden + 4 * total * width,
            transcendentals=total * hidden,
        ),
        name="experts",
    )(*arrays, *(in_hbm(w) for w in (*mine, *other)))


def keep_kernel(x_ref, out_ref):
    pass


def keep(x):
    return pl.pallas_call(
        keep_kernel,
        in_specs=[pl.BlockSpec(memory_space=pltpu.HBM)],
        out_specs=pl.BlockSpec(memory_space=pltpu.HBM),
        out_shape=pltpu.HBM(x.shape, x.dtype),
        input_output_aliases={0: 0},
        compiler_params=pltpu.CompilerParams(vmem_limit_bytes=MIB),
        cost_estimate=pl.CostEstimate(flops=100_000_000_000, bytes_accessed=1, transcendentals=0),
        name="keep",
    )(in_hbm(x))


def weighted(info, back_ref, out_ref, cuts, base):
    by_token = info.T
    rows = by_token[:, 2 * TOP : 3 * TOP].astype(jnp.int32)
    at = lax.broadcasted_iota(jnp.int32, (rows.shape[0], back_ref.shape[0]), 1)
    picks = [(at == rows[:, k : k + 1]).astype(F32).astype(BF16) for k in range(TOP)]
    gates = [by_token[:, TOP + k : TOP + k + 1] for k in range(TOP)]
    cols = out_ref.shape[1] // cuts
    for i in range(cuts):
        here = slice(i * cols, (i + 1) * cols)
        back = back_ref[:, here]
        terms = [
            jnp.dot(pick, back, preferred_element_type=F32) * gate
            for pick, gate in zip(picks, gates, strict=True)
        ]
        total = sum(terms[1:], terms[0])
        if base is not None:
            total = base(here) + total
        out_ref[:, here] = total.astype(BF16)


def combine_far_kernel(info_ref, back_ref, mid_hbm, out_ref, mid_ref, sem, *, cuts):
    copy = pltpu.make_async_copy(mid_hbm, mid_ref, sem)
    copy.start()
    weighted(info_ref[...], back_ref, out_ref, cuts, None)
    copy.wait()


def combine_far(info, back, mid):
    rows, width = info.shape[1], back.shape[1]
    held = pl.BlockSpec(memory_space=pltpu.VMEM)
    return pl.pallas_call(
        functools.partial(combine_far_kernel, cuts=4),
        in_specs=[held, held, pl.BlockSpec(memory_space=pltpu.HBM)],
        out_specs=[held, pl.BlockSpec(memory_space=pl.ANY)],
        out_shape=[
            jax.ShapeDtypeStruct((rows, width), BF16),
            pltpu.VMEM((rows, width), F32),
        ],
        scratch_shapes=[pltpu.SemaphoreType.DMA(())],
        compiler_params=pltpu.CompilerParams(vmem_limit_bytes=16 * MIB),
        name="combine_far",
    )(info, back, in_hbm(mid))


def combine_kernel(info_ref, back_ref, far_ref, mid_ref, out_ref, *, cuts):
    def base(here):
        return mid_ref[:, here] + far_ref[:, here].astype(F32)

    weighted(info_ref[...], back_ref, out_ref, cuts, base)


def combine(info, back, mid, far):
    rows, width = mid.shape
    return pl.pallas_call(
        functools.partial(combine_kernel, cuts=4),
        in_specs=[pl.BlockSpec(memory_space=pltpu.VMEM)] * 4,
        out_specs=pl.BlockSpec(memory_space=pltpu.VMEM),
        out_shape=jax.ShapeDtypeStruct((rows, width), BF16),
        compiler_params=pltpu.CompilerParams(vmem_limit_bytes=16 * MIB),
        name="combine",
    )(info, back, far, pltpu.with_memory_space_constraint(mid, pltpu.VMEM))


def spread_kernel(x_hbm, out_hbm, x_ref, in_sems, out_sems):
    n_seq, three, _, part = out_hbm.shape
    copies = [
        pltpu.make_async_copy(x_hbm.at[j], x_ref.at[j], in_sems.at[j]) for j in range(three)
    ]
    for copy in copies:
        copy.start()
    out = []
    for j, copy in enumerate(copies):
        copy.wait()
        for i in range(n_seq):
            out.append(
                pltpu.make_async_copy(
                    x_ref.at[j, :, pl.ds(i * part, part)], out_hbm.at[i, j], out_sems.at[i, j]
                )
            )
            out[-1].start()
    for copy in out:
        copy.wait()


def spread(qkv, n_seq):
    three, rows, width = qkv.shape
    part = width // n_seq
    return pl.pallas_call(
        spread_kernel,
        in_specs=[pl.BlockSpec(memory_space=pltpu.HBM)],
        out_specs=pl.BlockSpec(memory_space=pltpu.HBM),
        out_shape=pltpu.HBM((n_seq, three, rows, part), BF16),
        scratch_shapes=[
            pltpu.VMEM(qkv.shape, BF16),
            pltpu.SemaphoreType.DMA((three,)),
            pltpu.SemaphoreType.DMA((n_seq, three)),
        ],
        compiler_params=pltpu.CompilerParams(vmem_limit_bytes=8 * MIB),
        name="spread",
    )(in_hbm(qkv))


def total_kernel(own_ref, *refs, n_in, first):
    in_refs, (out_hbm, out_ref, sems) = refs[:n_in], refs[-3:]
    start, copies = 0, []
    for i, (up_ref, down_ref) in enumerate(zip(in_refs[::2], in_refs[1::2], strict=True)):
        n = up_ref.shape[0]
        total = own_ref[first + start : first + start + n].astype(F32) + up_ref[...].astype(F32)
        out_ref[start : start + n] = (total + down_ref[...].astype(F32)).astype(BF16)
        copies.append(
            pltpu.make_async_copy(
                out_ref.at[pl.ds(start, n)], out_hbm.at[pl.ds(first + start, n)], sems.at[i]
            )
        )
        copies[-1].start()
        start += n
    for copy in copies:
        copy.wait()


def add_up(own, pairs, first=0, into=None):
    arrays = [x for pair in pairs for x in pair]
    rows = sum(up.shape[0] for up, _ in pairs)
    held, far = pl.BlockSpec(memory_space=pltpu.VMEM), pl.BlockSpec(memory_space=pltpu.HBM)
    more = [] if into is None else [in_hbm(into)]
    return pl.pallas_call(
        functools.partial(total_kernel, n_in=len(arrays), first=first),
        in_specs=[held] * (1 + len(arrays)) + [far] * len(more),
        out_specs=far,
        out_shape=pltpu.HBM(own.shape, BF16),
        input_output_aliases={1 + len(arrays): 0} if more else {},
        scratch_shapes=[
            pltpu.VMEM((rows, own.shape[1]), BF16),
            pltpu.SemaphoreType.DMA((len(pairs),)),
        ],
        compiler_params=pltpu.CompilerParams(vmem_limit_bytes=16 * MIB),
        cost_estimate=pl.CostEstimate(flops=1, bytes_accessed=1, transcendentals=0),
        name="add_up",
    )(own, *arrays, *more)


def per_device(stream_in, qkv_heads, expert_ids, gate_weights, w_out, w_gate, w_up, w_down):
    rows, width = stream_in.shape[1:]
    seq, exp = ("y", "core"), ("z", "x")
    n_y, n_seq, n_exp = lax.axis_size("y"), lax.axis_size(seq), lax.axis_size(exp)
    capacity = 3 * TOP * rows // (2 * n_exp)
    slots = n_exp * capacity

    def swap(x):
        return lax.ppermute(x, "core", [(0, 1), (1, 0)])

    def shift(x, by):
        return lax.ppermute(x, "y", [(i, (i + by) % n_y) for i in range(n_y)])

    def exchange(x):
        return lax.all_to_all(x, exp, split_axis=0, concat_axis=0, tiled=True)

    mine = [w[0] for w in (w_gate, w_up, w_down)]
    other = [swap(w) for w in mine]
    info = jnp.concatenate(
        [expert_ids[0].T.astype(F32), gate_weights[0].T, jnp.zeros((8 - 2 * TOP, rows), F32)]
    )
    info = plan(info, n_exp, capacity)
    info_far = shift(info, 2)
    qkv = spread(qkv_heads[0].transpose(1, 0, 2), n_seq)
    arrived = lax.all_to_all(qkv, seq, split_axis=0, concat_axis=0, tiled=True)
    context, w_held = attention(arrived, w_out)
    context, info_far, other = lax.optimization_barrier((context, info_far, other))
    merged = lax.all_to_all(context, seq, split_axis=0, concat_axis=0, tiled=True)
    mid, normed, buffer = project(merged, w_held, stream_in[0], info, slots)

    tie = lax.optimization_barrier
    far_tokens = shift(normed, 2)
    far_buffer = route(far_tokens, info_far, slots)
    own, far_buffer = tie((exchange(buffer), far_buffer))
    eighth = own.shape[0] // 8
    first, second = own[: 2 * eighth], own[2 * eighth : 5 * eighth]
    rest, first, second = tie((own, first, second))
    third = rest[5 * eighth :]
    third, far_buffer = tie((third, far_buffer))
    far_rows = exchange(far_buffer)

    def send(x):
        return shift(x, 1), shift(x, -1)

    def give_back(pair):
        return shift(pair[0], -1), shift(pair[1], 1)

    at_first, at_second = send(first), send(second)
    third, at_first = tie((third, at_first))
    at_third = send(third)
    own_part, *back = experts([own, *at_first], mine, other)
    home = [give_back(back)]
    far_rows, at_second, own_part = tie((far_rows, at_second, own_part))
    far_part, *back = experts([far_rows, *at_second], mine, other)
    home.append(give_back(back))
    at_third, far_part, home[0] = tie((at_third, far_part, home[0]))
    far_back = exchange(keep(far_part))
    back = experts(at_third, mine, other)
    home.append(give_back(back))
    far_sum, mid = combine_far(info_far, far_back, mid)
    total = add_up(own_part, home[:2])
    total = add_up(own_part, home[2:], 5 * eighth, total)
    total, far_back = tie((total, far_back))
    back = exchange(total)
    far_home = shift(far_sum, 2)
    return combine(info, back, mid, far_home)[None]


def solution(mesh):
    split = Mesh(mesh.devices.reshape(-1, 2, 4, 4), ("y", "core", "z", "x"))
    seq, exp = ("y", "core"), ("z", "x")
    in_specs = (
        P(exp, seq, None),
        P(exp, seq, None, None),
        P(exp, seq, None),
        P(exp, seq, None),
        P(),
        P(exp, None, seq),
        P(exp, None, seq),
        P(exp, seq, None),
    )
    return jax.shard_map(
        per_device, mesh=split, in_specs=in_specs, out_specs=P(exp, seq, None), check_vma=False
    )
```

```python
import functools

import jax
import jax.numpy as jnp
from jax import lax
from jax.experimental import pallas as pl
from jax.experimental.pallas import tpu as pltpu
from jax.sharding import Mesh
from jax.sharding import PartitionSpec as P

HD = 64
LANES = 128
MIB = 1 << 20
BF16 = jnp.bfloat16
F32 = jnp.float32
LOG2E = 1.4426950408889634
TOP = 2


def vmem(shape):
    return pl.BlockSpec(shape, lambda *_: (0,) * len(shape))


def attention_kernel(x_ref, w_hbm, out_ref, w_ref, sems, *, block):
    cuts = sems.shape[0]
    rows = w_hbm.shape[0] // cuts
    fetch = [
        pltpu.make_async_copy(
            w_hbm.at[pl.ds(i * rows, rows)], w_ref.at[pl.ds(i * rows, rows)], sems.at[i]
        )
        for i in range(cuts)
    ]

    @pl.when(pl.program_id(0) == 0)
    def _():
        for copy in fetch:
            copy.start()

    n_src, _, rows, lanes = x_ref.shape
    length = n_src * rows
    keys = x_ref[:, 1].reshape(length, lanes)
    values = x_ref[:, 2].reshape(length, lanes)
    wide = jnp.concatenate([values, jnp.ones((length, lanes), BF16)], axis=1)
    lane = lax.broadcasted_iota(jnp.int32, (1, lanes), 1)
    first = lane < HD
    scale = float(HD) ** (-0.5) * LOG2E
    per = block // rows
    for i in range(length // block):
        query = x_ref[i * per : (i + 1) * per, 0].reshape(block, lanes)
        parts = []
        for head in range(2):
            mine = jnp.where(first if head == 0 else ~first, query, jnp.zeros_like(query))
            scores = lax.dot_general(
                mine, keys, (((1,), (1,)), ((), ())), preferred_element_type=F32
            )
            top = jnp.max(scores, axis=1, keepdims=True)
            weights = jnp.exp2((scores - top) * scale).astype(BF16)
            both = jnp.dot(weights, wide, preferred_element_type=F32)
            parts.append(both[:, :lanes] / both[:, lanes:])
        context = jnp.where(first, parts[0], parts[1]).astype(BF16)
        out_ref[i * per : (i + 1) * per] = context.reshape(per, rows, lanes)

    @pl.when(pl.program_id(0) == pl.num_programs(0) - 1)
    def _():
        for copy in fetch:
            copy.wait()


def attention(arrived, w_out):
    n_src, three, rows, width = arrived.shape
    return pl.pallas_call(
        functools.partial(attention_kernel, block=2 * rows),
        grid=(width // LANES,),
        in_specs=[
            pl.BlockSpec((n_src, three, rows, LANES), lambda i: (0, 0, 0, i)),
            pl.BlockSpec(memory_space=pltpu.HBM),
        ],
        out_specs=[
            pl.BlockSpec((n_src, rows, LANES), lambda i: (0, 0, i)),
            pl.BlockSpec(memory_space=pl.ANY),
        ],
        out_shape=[
            jax.ShapeDtypeStruct((n_src, rows, width), BF16),
            pltpu.VMEM(w_out.shape, BF16),
        ],
        scratch_shapes=[pltpu.SemaphoreType.DMA((8,))],
        compiler_params=pltpu.CompilerParams(vmem_limit_bytes=24 * MIB),
        name="attention",
    )(arrived, in_hbm(w_out))


def plan_kernel(info_ref, out_ref, *, n_exp, capacity):
    info = info_ref[...]
    tokens = info.shape[1]
    ids = info[:TOP].astype(jnp.int32)
    expert = lax.broadcasted_iota(jnp.int32, (n_exp, tokens), 0)
    named = [expert == ids[k : k + 1] for k in range(TOP)]
    member = sum(n.astype(F32) for n in named)
    before = (
        lax.broadcasted_iota(jnp.int32, (tokens, tokens), 0)
        < lax.broadcasted_iota(jnp.int32, (tokens, tokens), 1)
    ).astype(F32)
    rank = jnp.dot(member.astype(BF16), before.astype(BF16), preferred_element_type=F32)
    out_ref[...] = info
    for k, n in enumerate(named):
        slot = jnp.sum(jnp.where(n, rank, 0.0), axis=0, keepdims=True)
        out_ref[2 * TOP + k : 2 * TOP + k + 1] = info[k : k + 1] * capacity + slot


def plan(info, n_exp, capacity):
    return pl.pallas_call(
        functools.partial(plan_kernel, n_exp=n_exp, capacity=capacity),
        grid=(1,),
        in_specs=[vmem(info.shape)],
        out_specs=vmem(info.shape),
        out_shape=jax.ShapeDtypeStruct(info.shape, F32),
        compiler_params=pltpu.CompilerParams(vmem_limit_bytes=4 * MIB),
        name="plan",
    )(info)


def fill(normed, info, out_ref):
    rows = info[2 * TOP : 3 * TOP].astype(jnp.int32)
    at = lax.broadcasted_iota(jnp.int32, (out_ref.shape[0], normed.shape[0]), 0)
    pick = sum((at == rows[k : k + 1]).astype(F32) for k in range(TOP)).astype(BF16)
    out_ref[...] = jnp.dot(pick, normed, preferred_element_type=F32).astype(BF16)


def project_kernel(
    ctx_ref, w_ref, stream_ref, info_ref, mid_hbm, normed_ref, out_ref, mid_ref, sem
):
    merged = jnp.concatenate([ctx_ref[s] for s in range(ctx_ref.shape[0])], axis=1)
    mid = stream_ref[...].astype(F32) + jnp.dot(
        merged, w_ref[...], preferred_element_type=F32
    )
    mid_ref[...] = mid
    copy = pltpu.make_async_copy(mid_ref, mid_hbm, sem)
    copy.start()
    factor = lax.rsqrt(jnp.mean(mid * mid, axis=1, keepdims=True) + 1e-06)
    normed = (mid * factor).astype(BF16)
    normed_ref[...] = normed
    fill(normed, info_ref[...], out_ref)
    copy.wait()


def project(merged, w_out, stream, info, slots):
    rows, width = stream.shape
    held = pl.BlockSpec(memory_space=pltpu.VMEM)
    return pl.pallas_call(
        project_kernel,
        in_specs=[held] * 4,
        out_specs=[pl.BlockSpec(memory_space=pltpu.HBM), held, held],
        out_shape=[
            pltpu.HBM((rows, width), F32),
            jax.ShapeDtypeStruct((rows, width), BF16),
            jax.ShapeDtypeStruct((slots, width), BF16),
        ],
        scratch_shapes=[pltpu.VMEM((rows, width), F32), pltpu.SemaphoreType.DMA(())],
        compiler_params=pltpu.CompilerParams(vmem_limit_bytes=24 * MIB),
        name="project",
    )(merged, pltpu.with_memory_space_constraint(w_out, pltpu.VMEM), stream, info)


def route_kernel(normed_ref, info_ref, out_ref):
    fill(normed_ref[...], info_ref[...], out_ref)


def route(normed, info, slots):
    rows, width = normed.shape
    return pl.pallas_call(
        route_kernel,
        grid=(1,),
        in_specs=[vmem(normed.shape), vmem(info.shape)],
        out_specs=vmem((slots, width)),
        out_shape=jax.ShapeDtypeStruct((slots, width), BF16),
        compiler_params=pltpu.CompilerParams(vmem_limit_bytes=16 * MIB),
        name="route",
    )(normed, info)


def expert_kernel(*refs, n_in, block):
    x_refs, w_refs = refs[:n_in], refs[n_in : n_in + 6]
    out_refs = refs[n_in + 6 : 2 * n_in + 6]
    rows_ref, total_ref, hidden_ref, gate_ref, up_ref, down_ref, x_sems, w_sems, out_sems = refs[
        2 * n_in + 6 :
    ]
    share = w_refs[0].shape[1]
    per = share // block

    def weight_copies(i):
        gate, up, down = w_refs[:3] if i < per else w_refs[3:]
        there, here = pl.ds(i % per * block, block), pl.ds(i * block, block)
        return (
            pltpu.make_async_copy(gate.at[:, there], gate_ref.at[:, here], w_sems.at[i, 0]),
            pltpu.make_async_copy(up.at[:, there], up_ref.at[:, here], w_sems.at[i, 1]),
            pltpu.make_async_copy(down.at[there], down_ref.at[here], w_sems.at[i, 2]),
        )

    row_copies, start = [], 0
    for i, ref in enumerate(x_refs):
        here = pl.ds(start, ref.shape[0])
        row_copies.append(pltpu.make_async_copy(ref, rows_ref.at[here], x_sems.at[i]))
        start += ref.shape[0]
    copies = [weight_copies(i) for i in range(2 * per)]
    for copy in (*row_copies, *copies[0], *copies[1]):
        copy.start()
    for copy in row_copies:
        copy.wait()
    rows = rows_ref[...]
    for i in range(2 * per):
        here = slice(i * block, (i + 1) * block)
        copies[i][0].wait()
        copies[i][1].wait()
        if i + 2 < 2 * per:
            for copy in copies[i + 2]:
                copy.start()
        gate = jnp.dot(rows, gate_ref[:, here], preferred_element_type=F32)
        up = jnp.dot(rows, up_ref[:, here], preferred_element_type=F32)
        half = 0.5 * gate
        hidden_ref[:, here] = ((half + half * jnp.tanh(half)) * up).astype(BF16)
    for copy in copies:
        copy[2].wait()
    cuts = out_sems.shape[1]
    cols = out_refs[0].shape[1] // cuts
    flushes = []
    for j in range(cuts):
        here = slice(j * cols, (j + 1) * cols)
        total = jnp.dot(hidden_ref[...], down_ref[:, here], preferred_element_type=F32)
        total_ref[:, here] = total.astype(BF16)
        start = 0
        for i, ref in enumerate(out_refs):
            n, lanes = ref.shape[0], pl.ds(j * cols, cols)
            flushes.append(
                pltpu.make_async_copy(
                    total_ref.at[pl.ds(start, n), lanes], ref.at[:, lanes], out_sems.at[i, j]
                )
            )
            flushes[-1].start()
            start += n
    for flush in flushes:
        flush.wait()


def in_hbm(x):
    return pltpu.with_memory_space_constraint(x, pltpu.HBM)


def experts(arrays, mine, other):
    width = arrays[0].shape[1]
    hidden = 2 * mine[0].shape[1]
    total = sum(x.shape[0] for x in arrays)
    block = 256
    return pl.pallas_call(
        functools.partial(expert_kernel, n_in=len(arrays), block=block),
        grid=(1,),
        in_specs=[pl.BlockSpec(memory_space=pl.ANY)] * len(arrays)
        + [pl.BlockSpec(memory_space=pltpu.HBM)] * 6,
        out_specs=[pl.BlockSpec(memory_space=pltpu.HBM)] * len(arrays),
        out_shape=[pltpu.HBM(x.shape, BF16) for x in arrays],
        scratch_shapes=[
            pltpu.VMEM((total, width), BF16),
            pltpu.VMEM((total, width), BF16),
            pltpu.VMEM((total, hidden), BF16),
            pltpu.VMEM((width, hidden), BF16),
            pltpu.VMEM((width, hidden), BF16),
            pltpu.VMEM((hidden, width), BF16),
            pltpu.SemaphoreType.DMA((len(arrays),)),
            pltpu.SemaphoreType.DMA((hidden // block, 3)),
            pltpu.SemaphoreType.DMA((len(arrays), 4)),
        ],
        compiler_params=pltpu.CompilerParams(vmem_limit_bytes=44 * MIB),
        cost_estimate=pl.CostEstimate(
            flops=600 * total * width * hidden,
            bytes_accessed=6 * width * hidden + 4 * total * width,
            transcendentals=total * hidden,
        ),
        name="experts",
    )(*arrays, *(in_hbm(w) for w in (*mine, *other)))


def keep_kernel(x_ref, out_ref):
    pass


def keep(x):
    return pl.pallas_call(
        keep_kernel,
        in_specs=[pl.BlockSpec(memory_space=pltpu.HBM)],
        out_specs=pl.BlockSpec(memory_space=pltpu.HBM),
        out_shape=pltpu.HBM(x.shape, x.dtype),
        input_output_aliases={0: 0},
        compiler_params=pltpu.CompilerParams(vmem_limit_bytes=MIB),
        cost_estimate=pl.CostEstimate(flops=100_000_000_000, bytes_accessed=1, transcendentals=0),
        name="keep",
    )(in_hbm(x))


def weighted(info, back_ref, out_ref, cuts, base):
    by_token = info.T
    rows = by_token[:, 2 * TOP : 3 * TOP].astype(jnp.int32)
    at = lax.broadcasted_iota(jnp.int32, (rows.shape[0], back_ref.shape[0]), 1)
    picks = [(at == rows[:, k : k + 1]).astype(F32).astype(BF16) for k in range(TOP)]
    gates = [by_token[:, TOP + k : TOP + k + 1] for k in range(TOP)]
    cols = out_ref.shape[1] // cuts
    for i in range(cuts):
        here = slice(i * cols, (i + 1) * cols)
        back = back_ref[:, here]
        terms = [
            jnp.dot(pick, back, preferred_element_type=F32) * gate
            for pick, gate in zip(picks, gates, strict=True)
        ]
        total = sum(terms[1:], terms[0])
        if base is not None:
            total = base(here) + total
        out_ref[:, here] = total.astype(BF16)


def combine_far_kernel(info_ref, back_ref, mid_hbm, out_ref, mid_ref, sem, *, cuts):
    copy = pltpu.make_async_copy(mid_hbm, mid_ref, sem)
    copy.start()
    weighted(info_ref[...], back_ref, out_ref, cuts, None)
    copy.wait()


def combine_far(info, back, mid):
    rows, width = info.shape[1], back.shape[1]
    held = pl.BlockSpec(memory_space=pltpu.VMEM)
    return pl.pallas_call(
        functools.partial(combine_far_kernel, cuts=4),
        in_specs=[held, held, pl.BlockSpec(memory_space=pltpu.HBM)],
        out_specs=[held, pl.BlockSpec(memory_space=pl.ANY)],
        out_shape=[
            jax.ShapeDtypeStruct((rows, width), BF16),
            pltpu.VMEM((rows, width), F32),
        ],
        scratch_shapes=[pltpu.SemaphoreType.DMA(())],
        compiler_params=pltpu.CompilerParams(vmem_limit_bytes=16 * MIB),
        name="combine_far",
    )(info, back, in_hbm(mid))


def combine_kernel(info_ref, back_ref, far_ref, mid_ref, out_ref, *, cuts):
    def base(here):
        return mid_ref[:, here] + far_ref[:, here].astype(F32)

    weighted(info_ref[...], back_ref, out_ref, cuts, base)


def combine(info, back, mid, far):
    rows, width = mid.shape
    return pl.pallas_call(
        functools.partial(combine_kernel, cuts=4),
        in_specs=[pl.BlockSpec(memory_space=pltpu.VMEM)] * 4,
        out_specs=pl.BlockSpec(memory_space=pltpu.VMEM),
        out_shape=jax.ShapeDtypeStruct((rows, width), BF16),
        compiler_params=pltpu.CompilerParams(vmem_limit_bytes=16 * MIB),
        name="combine",
    )(info, back, far, pltpu.with_memory_space_constraint(mid, pltpu.VMEM))


def spread_kernel(x_hbm, out_hbm, x_ref, in_sems, out_sems):
    n_seq, three, _, part = out_hbm.shape
    copies = [
        pltpu.make_async_copy(x_hbm.at[j], x_ref.at[j], in_sems.at[j]) for j in range(three)
    ]
    for copy in copies:
        copy.start()
    out = []
    for j, copy in enumerate(copies):
        copy.wait()
        for i in range(n_seq):
            out.append(
                pltpu.make_async_copy(
                    x_ref.at[j, :, pl.ds(i * part, part)], out_hbm.at[i, j], out_sems.at[i, j]
                )
            )
            out[-1].start()
    for copy in out:
        copy.wait()


def spread(qkv, n_seq):
    three, rows, width = qkv.shape
    part = width // n_seq
    return pl.pallas_call(
        spread_kernel,
        in_specs=[pl.BlockSpec(memory_space=pltpu.HBM)],
        out_specs=pl.BlockSpec(memory_space=pltpu.HBM),
        out_shape=pltpu.HBM((n_seq, three, rows, part), BF16),
        scratch_shapes=[
            pltpu.VMEM(qkv.shape, BF16),
            pltpu.SemaphoreType.DMA((three,)),
            pltpu.SemaphoreType.DMA((n_seq, three)),
        ],
        compiler_params=pltpu.CompilerParams(vmem_limit_bytes=8 * MIB),
        name="spread",
    )(in_hbm(qkv))


def total_kernel(own_ref, *refs, n_in, first):
    in_refs, (out_hbm, out_ref, sems) = refs[:n_in], refs[-3:]
    start, copies = 0, []
    for i, (up_ref, down_ref) in enumerate(zip(in_refs[::2], in_refs[1::2], strict=True)):
        n = up_ref.shape[0]
        total = own_ref[first + start : first + start + n].astype(F32) + up_ref[...].astype(F32)
        out_ref[start : start + n] = (total + down_ref[...].astype(F32)).astype(BF16)
        copies.append(
            pltpu.make_async_copy(
                out_ref.at[pl.ds(start, n)], out_hbm.at[pl.ds(first + start, n)], sems.at[i]
            )
        )
        copies[-1].start()
        start += n
    for copy in copies:
        copy.wait()


def add_up(own, pairs, first=0, into=None):
    arrays = [x for pair in pairs for x in pair]
    rows = sum(up.shape[0] for up, _ in pairs)
    held, far = pl.BlockSpec(memory_space=pltpu.VMEM), pl.BlockSpec(memory_space=pltpu.HBM)
    more = [] if into is None else [in_hbm(into)]
    return pl.pallas_call(
        functools.partial(total_kernel, n_in=len(arrays), first=first),
        in_specs=[held] * (1 + len(arrays)) + [far] * len(more),
        out_specs=far,
        out_shape=pltpu.HBM(own.shape, BF16),
        input_output_aliases={1 + len(arrays): 0} if more else {},
        scratch_shapes=[
            pltpu.VMEM((rows, own.shape[1]), BF16),
            pltpu.SemaphoreType.DMA((len(pairs),)),
        ],
        compiler_params=pltpu.CompilerParams(vmem_limit_bytes=16 * MIB),
        cost_estimate=pl.CostEstimate(flops=1, bytes_accessed=1, transcendentals=0),
        name="add_up",
    )(own, *arrays, *more)


def per_device(stream_in, qkv_heads, expert_ids, gate_weights, w_out, w_gate, w_up, w_down):
    rows, width = stream_in.shape[1:]
    seq, exp = ("y", "core"), ("z", "x")
    n_y, n_seq, n_exp = lax.axis_size("y"), lax.axis_size(seq), lax.axis_size(exp)
    capacity = 3 * TOP * rows // (2 * n_exp)
    slots = n_exp * capacity

    def swap(x):
        return lax.ppermute(x, "core", [(0, 1), (1, 0)])

    def shift(x, by):
        return lax.ppermute(x, "y", [(i, (i + by) % n_y) for i in range(n_y)])

    def exchange(x):
        return lax.all_to_all(x, exp, split_axis=0, concat_axis=0, tiled=True)

    mine = [w[0] for w in (w_gate, w_up, w_down)]
    other = [swap(w) for w in mine]
    info = jnp.concatenate(
        [expert_ids[0].T.astype(F32), gate_weights[0].T, jnp.zeros((8 - 2 * TOP, rows), F32)]
    )
    info = plan(info, n_exp, capacity)
    info_far = shift(info, 2)
    qkv = spread(qkv_heads[0].transpose(1, 0, 2), n_seq)
    arrived = lax.all_to_all(qkv, seq, split_axis=0, concat_axis=0, tiled=True)
    context, w_held = attention(arrived, w_out)
    context, info_far, other = lax.optimization_barrier((context, info_far, other))
    merged = lax.all_to_all(context, seq, split_axis=0, concat_axis=0, tiled=True)
    mid, normed, buffer = project(merged, w_held, stream_in[0], info, slots)

    tie = lax.optimization_barrier
    far_tokens = shift(normed, 2)
    far_buffer = route(far_tokens, info_far, slots)
    own, far_buffer = tie((exchange(buffer), far_buffer))
    eighth = own.shape[0] // 8
    first, second = own[: 2 * eighth], own[2 * eighth : 6 * eighth]
    rest, first, second = tie((own, first, second))
    third = rest[6 * eighth :]
    third, far_buffer = tie((third, far_buffer))
    far_rows = exchange(far_buffer)

    def send(x):
        return shift(x, 1), shift(x, -1)

    def give_back(pair):
        return shift(pair[0], -1), shift(pair[1], 1)

    at_first, at_second = send(first), send(second)
    third, at_first = tie((third, at_first))
    at_third = send(third)
    own_part, *back = experts([own, *at_first], mine, other)
    home = [give_back(back)]
    far_rows, at_second, own_part = tie((far_rows, at_second, own_part))
    far_part, *back = experts([far_rows, *at_second], mine, other)
    home.append(give_back(back))
    at_third, far_part, home[0] = tie((at_third, far_part, home[0]))
    far_back = exchange(keep(far_part))
    back = experts(at_third, mine, other)
    home.append(give_back(back))
    far_sum, mid = combine_far(info_far, far_back, mid)
    total = add_up(own_part, home[:2])
    total = add_up(own_part, home[2:], 6 * eighth, total)
    total, far_back = tie((total, far_back))
    back = exchange(total)
    far_home = shift(far_sum, 2)
    return combine(info, back, mid, far_home)[None]


def solution(mesh):
    split = Mesh(mesh.devices.reshape(-1, 2, 4, 4), ("y", "core", "z", "x"))
    seq, exp = ("y", "core"), ("z", "x")
    in_specs = (
        P(exp, seq, None),
        P(exp, seq, None, None),
        P(exp, seq, None),
        P(exp, seq, None),
        P(),
        P(exp, None, seq),
        P(exp, None, seq),
        P(exp, seq, None),
    )
    return jax.shard_map(
        per_device, mesh=split, in_specs=in_specs, out_specs=P(exp, seq, None), check_vma=False
    )
```

```python
import functools

import jax
import jax.numpy as jnp
from jax import lax
from jax.experimental import pallas as pl
from jax.experimental.pallas import tpu as pltpu
from jax.sharding import Mesh
from jax.sharding import PartitionSpec as P

HD = 64
LANES = 128
MIB = 1 << 20
BF16 = jnp.bfloat16
F32 = jnp.float32
LOG2E = 1.4426950408889634
TOP = 2


def vmem(shape):
    return pl.BlockSpec(shape, lambda *_: (0,) * len(shape))


def attention_kernel(x_ref, w_hbm, out_ref, w_ref, sems, *, block):
    cuts = sems.shape[0]
    rows = w_hbm.shape[0] // cuts
    fetch = [
        pltpu.make_async_copy(
            w_hbm.at[pl.ds(i * rows, rows)], w_ref.at[pl.ds(i * rows, rows)], sems.at[i]
        )
        for i in range(cuts)
    ]

    @pl.when(pl.program_id(0) == 0)
    def _():
        for copy in fetch:
            copy.start()

    n_src, _, rows, lanes = x_ref.shape
    length = n_src * rows
    keys = x_ref[:, 1].reshape(length, lanes)
    values = x_ref[:, 2].reshape(length, lanes)
    wide = jnp.concatenate([values, jnp.ones((length, lanes), BF16)], axis=1)
    lane = lax.broadcasted_iota(jnp.int32, (1, lanes), 1)
    first = lane < HD
    scale = float(HD) ** (-0.5) * LOG2E
    per = block // rows
    steps = [(i, head) for i in range(length // block) for head in range(2)]

    def score(i, head):
        query = x_ref[i * per : (i + 1) * per, 0].reshape(block, lanes)
        mine = jnp.where(first if head == 0 else ~first, query, jnp.zeros_like(query))
        return lax.dot_general(mine, keys, (((1,), (1,)), ((), ())), preferred_element_type=F32)

    following, parts = score(*steps[0]), []
    for step, (i, head) in enumerate(steps):
        scores = following
        if step + 1 < len(steps):
            following = score(*steps[step + 1])
        top = jnp.max(scores, axis=1, keepdims=True)
        weights = jnp.exp2((scores - top) * scale).astype(BF16)
        both = jnp.dot(weights, wide, preferred_element_type=F32)
        parts.append(both[:, :lanes] / both[:, lanes:])
        if head == 1:
            context = jnp.where(first, parts[0], parts[1]).astype(BF16)
            out_ref[i * per : (i + 1) * per] = context.reshape(per, rows, lanes)
            parts = []

    @pl.when(pl.program_id(0) == pl.num_programs(0) - 1)
    def _():
        for copy in fetch:
            copy.wait()


def attention(arrived, w_out):
    n_src, three, rows, width = arrived.shape
    return pl.pallas_call(
        functools.partial(attention_kernel, block=2 * rows),
        grid=(width // LANES,),
        in_specs=[
            pl.BlockSpec((n_src, three, rows, LANES), lambda i: (0, 0, 0, i)),
            pl.BlockSpec(memory_space=pltpu.HBM),
        ],
        out_specs=[
            pl.BlockSpec((n_src, rows, LANES), lambda i: (0, 0, i)),
            pl.BlockSpec(memory_space=pl.ANY),
        ],
        out_shape=[
            jax.ShapeDtypeStruct((n_src, rows, width), BF16),
            pltpu.VMEM(w_out.shape, BF16),
        ],
        scratch_shapes=[pltpu.SemaphoreType.DMA((8,))],
        compiler_params=pltpu.CompilerParams(vmem_limit_bytes=24 * MIB),
        name="attention",
    )(arrived, in_hbm(w_out))


def plan_kernel(info_ref, out_ref, *, n_exp, capacity):
    info = info_ref[...]
    tokens = info.shape[1]
    ids = info[:TOP].astype(jnp.int32)
    expert = lax.broadcasted_iota(jnp.int32, (n_exp, tokens), 0)
    named = [expert == ids[k : k + 1] for k in range(TOP)]
    member = sum(n.astype(F32) for n in named)
    before = (
        lax.broadcasted_iota(jnp.int32, (tokens, tokens), 0)
        < lax.broadcasted_iota(jnp.int32, (tokens, tokens), 1)
    ).astype(F32)
    rank = jnp.dot(member.astype(BF16), before.astype(BF16), preferred_element_type=F32)
    out_ref[...] = info
    for k, n in enumerate(named):
        slot = jnp.sum(jnp.where(n, rank, 0.0), axis=0, keepdims=True)
        out_ref[2 * TOP + k : 2 * TOP + k + 1] = info[k : k + 1] * capacity + slot


def plan(info, n_exp, capacity):
    return pl.pallas_call(
        functools.partial(plan_kernel, n_exp=n_exp, capacity=capacity),
        grid=(1,),
        in_specs=[vmem(info.shape)],
        out_specs=vmem(info.shape),
        out_shape=jax.ShapeDtypeStruct(info.shape, F32),
        compiler_params=pltpu.CompilerParams(vmem_limit_bytes=4 * MIB),
        name="plan",
    )(info)


def fill(normed, info, out_ref):
    rows = info[2 * TOP : 3 * TOP].astype(jnp.int32)
    at = lax.broadcasted_iota(jnp.int32, (out_ref.shape[0], normed.shape[0]), 0)
    pick = sum((at == rows[k : k + 1]).astype(F32) for k in range(TOP)).astype(BF16)
    out_ref[...] = jnp.dot(pick, normed, preferred_element_type=F32).astype(BF16)


def project_kernel(
    ctx_ref, w_ref, stream_ref, info_ref, mid_hbm, normed_ref, out_ref, mid_ref, sem
):
    merged = jnp.concatenate([ctx_ref[s] for s in range(ctx_ref.shape[0])], axis=1)
    mid = stream_ref[...].astype(F32) + jnp.dot(
        merged, w_ref[...], preferred_element_type=F32
    )
    mid_ref[...] = mid
    copy = pltpu.make_async_copy(mid_ref, mid_hbm, sem)
    copy.start()
    factor = lax.rsqrt(jnp.mean(mid * mid, axis=1, keepdims=True) + 1e-06)
    normed = (mid * factor).astype(BF16)
    normed_ref[...] = normed
    fill(normed, info_ref[...], out_ref)
    copy.wait()


def project(merged, w_out, stream, info, slots):
    rows, width = stream.shape
    held = pl.BlockSpec(memory_space=pltpu.VMEM)
    return pl.pallas_call(
        project_kernel,
        in_specs=[held] * 4,
        out_specs=[pl.BlockSpec(memory_space=pltpu.HBM), held, held],
        out_shape=[
            pltpu.HBM((rows, width), F32),
            jax.ShapeDtypeStruct((rows, width), BF16),
            jax.ShapeDtypeStruct((slots, width), BF16),
        ],
        scratch_shapes=[pltpu.VMEM((rows, width), F32), pltpu.SemaphoreType.DMA(())],
        compiler_params=pltpu.CompilerParams(vmem_limit_bytes=24 * MIB),
        name="project",
    )(merged, pltpu.with_memory_space_constraint(w_out, pltpu.VMEM), stream, info)


def route_kernel(normed_ref, info_ref, out_ref):
    fill(normed_ref[...], info_ref[...], out_ref)


def route(normed, info, slots):
    rows, width = normed.shape
    return pl.pallas_call(
        route_kernel,
        grid=(1,),
        in_specs=[vmem(normed.shape), vmem(info.shape)],
        out_specs=vmem((slots, width)),
        out_shape=jax.ShapeDtypeStruct((slots, width), BF16),
        compiler_params=pltpu.CompilerParams(vmem_limit_bytes=16 * MIB),
        name="route",
    )(normed, info)


def expert_kernel(*refs, n_in, block):
    x_refs, w_refs = refs[:n_in], refs[n_in : n_in + 6]
    out_refs = refs[n_in + 6 : 2 * n_in + 6]
    rows_ref, total_ref, hidden_ref, gate_ref, up_ref, down_ref, x_sems, w_sems, out_sems = refs[
        2 * n_in + 6 :
    ]
    share = w_refs[0].shape[1]
    per = share // block

    def weight_copies(i):
        gate, up, down = w_refs[:3] if i < per else w_refs[3:]
        there, here = pl.ds(i % per * block, block), pl.ds(i * block, block)
        return (
            pltpu.make_async_copy(gate.at[:, there], gate_ref.at[:, here], w_sems.at[i, 0]),
            pltpu.make_async_copy(up.at[:, there], up_ref.at[:, here], w_sems.at[i, 1]),
            pltpu.make_async_copy(down.at[there], down_ref.at[here], w_sems.at[i, 2]),
        )

    row_copies, start = [], 0
    for i, ref in enumerate(x_refs):
        here = pl.ds(start, ref.shape[0])
        row_copies.append(pltpu.make_async_copy(ref, rows_ref.at[here], x_sems.at[i]))
        start += ref.shape[0]
    copies = [weight_copies(i) for i in range(2 * per)]
    for copy in (*row_copies, *copies[0], *copies[1]):
        copy.start()
    for copy in row_copies:
        copy.wait()
    rows = rows_ref[...]
    for i in range(2 * per):
        here = slice(i * block, (i + 1) * block)
        copies[i][0].wait()
        copies[i][1].wait()
        if i + 2 < 2 * per:
            for copy in copies[i + 2]:
                copy.start()
        gate = jnp.dot(rows, gate_ref[:, here], preferred_element_type=F32)
        up = jnp.dot(rows, up_ref[:, here], preferred_element_type=F32)
        half = 0.5 * gate
        hidden_ref[:, here] = ((half + half * jnp.tanh(half)) * up).astype(BF16)
    for copy in copies:
        copy[2].wait()
    cuts = out_sems.shape[1]
    cols = out_refs[0].shape[1] // cuts
    flushes = []
    for j in range(cuts):
        here = slice(j * cols, (j + 1) * cols)
        total = jnp.dot(hidden_ref[...], down_ref[:, here], preferred_element_type=F32)
        total_ref[:, here] = total.astype(BF16)
        start = 0
        for i, ref in enumerate(out_refs):
            n, lanes = ref.shape[0], pl.ds(j * cols, cols)
            flushes.append(
                pltpu.make_async_copy(
                    total_ref.at[pl.ds(start, n), lanes], ref.at[:, lanes], out_sems.at[i, j]
                )
            )
            flushes[-1].start()
            start += n
    for flush in flushes:
        flush.wait()


def in_hbm(x):
    return pltpu.with_memory_space_constraint(x, pltpu.HBM)


def experts(arrays, mine, other):
    width = arrays[0].shape[1]
    hidden = 2 * mine[0].shape[1]
    total = sum(x.shape[0] for x in arrays)
    block = 256
    return pl.pallas_call(
        functools.partial(expert_kernel, n_in=len(arrays), block=block),
        grid=(1,),
        in_specs=[pl.BlockSpec(memory_space=pl.ANY)] * len(arrays)
        + [pl.BlockSpec(memory_space=pltpu.HBM)] * 6,
        out_specs=[pl.BlockSpec(memory_space=pltpu.HBM)] * len(arrays),
        out_shape=[pltpu.HBM(x.shape, BF16) for x in arrays],
        scratch_shapes=[
            pltpu.VMEM((total, width), BF16),
            pltpu.VMEM((total, width), BF16),
            pltpu.VMEM((total, hidden), BF16),
            pltpu.VMEM((width, hidden), BF16),
            pltpu.VMEM((width, hidden), BF16),
            pltpu.VMEM((hidden, width), BF16),
            pltpu.SemaphoreType.DMA((len(arrays),)),
            pltpu.SemaphoreType.DMA((hidden // block, 3)),
            pltpu.SemaphoreType.DMA((len(arrays), 4)),
        ],
        compiler_params=pltpu.CompilerParams(vmem_limit_bytes=44 * MIB),
        cost_estimate=pl.CostEstimate(
            flops=600 * total * width * hidden,
            bytes_accessed=6 * width * hidden + 4 * total * width,
            transcendentals=total * hidden,
        ),
        name="experts",
    )(*arrays, *(in_hbm(w) for w in (*mine, *other)))


def keep_kernel(x_ref, out_ref):
    pass


def keep(x):
    return pl.pallas_call(
        keep_kernel,
        in_specs=[pl.BlockSpec(memory_space=pltpu.HBM)],
        out_specs=pl.BlockSpec(memory_space=pltpu.HBM),
        out_shape=pltpu.HBM(x.shape, x.dtype),
        input_output_aliases={0: 0},
        compiler_params=pltpu.CompilerParams(vmem_limit_bytes=MIB),
        cost_estimate=pl.CostEstimate(flops=100_000_000_000, bytes_accessed=1, transcendentals=0),
        name="keep",
    )(in_hbm(x))


def weighted(info, back_ref, out_ref, cuts, base):
    by_token = info.T
    rows = by_token[:, 2 * TOP : 3 * TOP].astype(jnp.int32)
    at = lax.broadcasted_iota(jnp.int32, (rows.shape[0], back_ref.shape[0]), 1)
    picks = [(at == rows[:, k : k + 1]).astype(F32).astype(BF16) for k in range(TOP)]
    gates = [by_token[:, TOP + k : TOP + k + 1] for k in range(TOP)]
    cols = out_ref.shape[1] // cuts
    for i in range(cuts):
        here = slice(i * cols, (i + 1) * cols)
        back = back_ref[:, here]
        terms = [
            jnp.dot(pick, back, preferred_element_type=F32) * gate
            for pick, gate in zip(picks, gates, strict=True)
        ]
        total = sum(terms[1:], terms[0])
        if base is not None:
            total = base(here) + total
        out_ref[:, here] = total.astype(BF16)


def combine_far_kernel(info_ref, back_ref, mid_hbm, out_ref, mid_ref, sem, *, cuts):
    copy = pltpu.make_async_copy(mid_hbm, mid_ref, sem)
    copy.start()
    weighted(info_ref[...], back_ref, out_ref, cuts, None)
    copy.wait()


def combine_far(info, back, mid):
    rows, width = info.shape[1], back.shape[1]
    held = pl.BlockSpec(memory_space=pltpu.VMEM)
    return pl.pallas_call(
        functools.partial(combine_far_kernel, cuts=4),
        in_specs=[held, held, pl.BlockSpec(memory_space=pltpu.HBM)],
        out_specs=[held, pl.BlockSpec(memory_space=pl.ANY)],
        out_shape=[
            jax.ShapeDtypeStruct((rows, width), BF16),
            pltpu.VMEM((rows, width), F32),
        ],
        scratch_shapes=[pltpu.SemaphoreType.DMA(())],
        compiler_params=pltpu.CompilerParams(vmem_limit_bytes=16 * MIB),
        name="combine_far",
    )(info, back, in_hbm(mid))


def combine_kernel(info_ref, back_ref, far_ref, mid_ref, out_ref, *, cuts):
    def base(here):
        return mid_ref[:, here] + far_ref[:, here].astype(F32)

    weighted(info_ref[...], back_ref, out_ref, cuts, base)


def combine(info, back, mid, far):
    rows, width = mid.shape
    return pl.pallas_call(
        functools.partial(combine_kernel, cuts=4),
        in_specs=[pl.BlockSpec(memory_space=pltpu.VMEM)] * 4,
        out_specs=pl.BlockSpec(memory_space=pltpu.VMEM),
        out_shape=jax.ShapeDtypeStruct((rows, width), BF16),
        compiler_params=pltpu.CompilerParams(vmem_limit_bytes=16 * MIB),
        name="combine",
    )(info, back, far, pltpu.with_memory_space_constraint(mid, pltpu.VMEM))


def spread_kernel(x_hbm, out_hbm, x_ref, in_sems, out_sems):
    n_seq, three, _, part = out_hbm.shape
    copies = [
        pltpu.make_async_copy(x_hbm.at[j], x_ref.at[j], in_sems.at[j]) for j in range(three)
    ]
    for copy in copies:
        copy.start()
    out = []
    for j, copy in enumerate(copies):
        copy.wait()
        for i in range(n_seq):
            out.append(
                pltpu.make_async_copy(
                    x_ref.at[j, :, pl.ds(i * part, part)], out_hbm.at[i, j], out_sems.at[i, j]
                )
            )
            out[-1].start()
    for copy in out:
        copy.wait()


def spread(qkv, n_seq):
    three, rows, width = qkv.shape
    part = width // n_seq
    return pl.pallas_call(
        spread_kernel,
        in_specs=[pl.BlockSpec(memory_space=pltpu.HBM)],
        out_specs=pl.BlockSpec(memory_space=pltpu.HBM),
        out_shape=pltpu.HBM((n_seq, three, rows, part), BF16),
        scratch_shapes=[
            pltpu.VMEM(qkv.shape, BF16),
            pltpu.SemaphoreType.DMA((three,)),
            pltpu.SemaphoreType.DMA((n_seq, three)),
        ],
        compiler_params=pltpu.CompilerParams(vmem_limit_bytes=8 * MIB),
        name="spread",
    )(in_hbm(qkv))


def total_kernel(own_ref, *refs, n_in, first):
    in_refs, (out_hbm, out_ref, sems) = refs[:n_in], refs[-3:]
    start, copies = 0, []
    for i, (up_ref, down_ref) in enumerate(zip(in_refs[::2], in_refs[1::2], strict=True)):
        n = up_ref.shape[0]
        total = own_ref[first + start : first + start + n].astype(F32) + up_ref[...].astype(F32)
        out_ref[start : start + n] = (total + down_ref[...].astype(F32)).astype(BF16)
        copies.append(
            pltpu.make_async_copy(
                out_ref.at[pl.ds(start, n)], out_hbm.at[pl.ds(first + start, n)], sems.at[i]
            )
        )
        copies[-1].start()
        start += n
    for copy in copies:
        copy.wait()


def add_up(own, pairs, first=0, into=None):
    arrays = [x for pair in pairs for x in pair]
    rows = sum(up.shape[0] for up, _ in pairs)
    held, far = pl.BlockSpec(memory_space=pltpu.VMEM), pl.BlockSpec(memory_space=pltpu.HBM)
    more = [] if into is None else [in_hbm(into)]
    return pl.pallas_call(
        functools.partial(total_kernel, n_in=len(arrays), first=first),
        in_specs=[held] * (1 + len(arrays)) + [far] * len(more),
        out_specs=far,
        out_shape=pltpu.HBM(own.shape, BF16),
        input_output_aliases={1 + len(arrays): 0} if more else {},
        scratch_shapes=[
            pltpu.VMEM((rows, own.shape[1]), BF16),
            pltpu.SemaphoreType.DMA((len(pairs),)),
        ],
        compiler_params=pltpu.CompilerParams(vmem_limit_bytes=16 * MIB),
        cost_estimate=pl.CostEstimate(flops=1, bytes_accessed=1, transcendentals=0),
        name="add_up",
    )(own, *arrays, *more)


def per_device(stream_in, qkv_heads, expert_ids, gate_weights, w_out, w_gate, w_up, w_down):
    rows, width = stream_in.shape[1:]
    seq, exp = ("y", "core"), ("z", "x")
    n_y, n_seq, n_exp = lax.axis_size("y"), lax.axis_size(seq), lax.axis_size(exp)
    capacity = 3 * TOP * rows // (2 * n_exp)
    slots = n_exp * capacity

    def swap(x):
        return lax.ppermute(x, "core", [(0, 1), (1, 0)])

    def shift(x, by):
        return lax.ppermute(x, "y", [(i, (i + by) % n_y) for i in range(n_y)])

    def exchange(x):
        return lax.all_to_all(x, exp, split_axis=0, concat_axis=0, tiled=True)

    mine = [w[0] for w in (w_gate, w_up, w_down)]
    other = [swap(w) for w in mine]
    info = jnp.concatenate(
        [expert_ids[0].T.astype(F32), gate_weights[0].T, jnp.zeros((8 - 2 * TOP, rows), F32)]
    )
    info = plan(info, n_exp, capacity)
    info_far = shift(info, 2)
    qkv = spread(qkv_heads[0].transpose(1, 0, 2), n_seq)
    arrived = lax.all_to_all(qkv, seq, split_axis=0, concat_axis=0, tiled=True)
    context, w_held = attention(arrived, w_out)
    context, info_far, other = lax.optimization_barrier((context, info_far, other))
    merged = lax.all_to_all(context, seq, split_axis=0, concat_axis=0, tiled=True)
    mid, normed, buffer = project(merged, w_held, stream_in[0], info, slots)

    tie = lax.optimization_barrier
    far_tokens = shift(normed, 2)
    far_buffer = route(far_tokens, info_far, slots)
    own, far_buffer = tie((exchange(buffer), far_buffer))
    eighth = own.shape[0] // 8
    first, second = own[: 2 * eighth], own[2 * eighth : 6 * eighth]
    rest, first, second = tie((own, first, second))
    third = rest[6 * eighth :]
    third, far_buffer = tie((third, far_buffer))
    far_rows = exchange(far_buffer)

    def send(x):
        return shift(x, 1), shift(x, -1)

    def give_back(pair):
        return shift(pair[0], -1), shift(pair[1], 1)

    at_first, at_second = send(first), send(second)
    third, at_first = tie((third, at_first))
    at_third = send(third)
    own_part, *back = experts([own, *at_first], mine, other)
    home = [give_back(back)]
    far_rows, at_second, own_part = tie((far_rows, at_second, own_part))
    far_part, *back = experts([far_rows, *at_second], mine, other)
    home.append(give_back(back))
    at_third, far_part, home[0] = tie((at_third, far_part, home[0]))
    far_back = exchange(keep(far_part))
    back = experts(at_third, mine, other)
    home.append(give_back(back))
    far_sum, mid = combine_far(info_far, far_back, mid)
    total = add_up(own_part, home[:2])
    total = add_up(own_part, home[2:], 6 * eighth, total)
    total, far_back = tie((total, far_back))
    back = exchange(total)
    far_home = shift(far_sum, 2)
    return combine(info, back, mid, far_home)[None]


def solution(mesh):
    split = Mesh(mesh.devices.reshape(-1, 2, 4, 4), ("y", "core", "z", "x"))
    seq, exp = ("y", "core"), ("z", "x")
    in_specs = (
        P(exp, seq, None),
        P(exp, seq, None, None),
        P(exp, seq, None),
        P(exp, seq, None),
        P(),
        P(exp, None, seq),
        P(exp, None, seq),
        P(exp, seq, None),
    )
    return jax.shard_map(
        per_device, mesh=split, in_specs=in_specs, out_specs=P(exp, seq, None), check_vma=False
    )
```

```python
import functools

import jax
import jax.numpy as jnp
from jax import lax
from jax.experimental import pallas as pl
from jax.experimental.pallas import tpu as pltpu
from jax.sharding import Mesh
from jax.sharding import PartitionSpec as P

HD = 64
LANES = 128
MIB = 1 << 20
BF16 = jnp.bfloat16
F32 = jnp.float32
LOG2E = 1.4426950408889634
TOP = 2


def vmem(shape):
    return pl.BlockSpec(shape, lambda *_: (0,) * len(shape))


def attention_kernel(x_ref, w_hbm, out_ref, w_ref, sems, *, block):
    cuts = sems.shape[0]
    rows = w_hbm.shape[0] // cuts
    fetch = [
        pltpu.make_async_copy(
            w_hbm.at[pl.ds(i * rows, rows)], w_ref.at[pl.ds(i * rows, rows)], sems.at[i]
        )
        for i in range(cuts)
    ]

    @pl.when(pl.program_id(0) == 0)
    def _():
        for copy in fetch:
            copy.start()

    n_src, _, rows, lanes = x_ref.shape
    length = n_src * rows
    keys = x_ref[:, 1].reshape(length, lanes)
    values = x_ref[:, 2].reshape(length, lanes)
    wide = jnp.concatenate([values, jnp.ones((length, lanes), BF16)], axis=1)
    lane = lax.broadcasted_iota(jnp.int32, (1, lanes), 1)
    first = lane < HD
    scale = float(HD) ** (-0.5) * LOG2E
    per = block // rows
    steps = [(i, head) for i in range(length // block) for head in range(2)]

    def score(i, head):
        query = x_ref[i * per : (i + 1) * per, 0].reshape(block, lanes)
        mine = jnp.where(first if head == 0 else ~first, query, jnp.zeros_like(query))
        return lax.dot_general(mine, keys, (((1,), (1,)), ((), ())), preferred_element_type=F32)

    following, parts = score(*steps[0]), []
    for step, (i, head) in enumerate(steps):
        scores = following
        if step + 1 < len(steps):
            following = score(*steps[step + 1])
        top = jnp.max(scores, axis=1, keepdims=True)
        weights = jnp.exp2((scores - top) * scale).astype(BF16)
        both = jnp.dot(weights, wide, preferred_element_type=F32)
        parts.append(both[:, :lanes] / both[:, lanes:])
        if head == 1:
            context = jnp.where(first, parts[0], parts[1]).astype(BF16)
            out_ref[i * per : (i + 1) * per] = context.reshape(per, rows, lanes)
            parts = []

    @pl.when(pl.program_id(0) == pl.num_programs(0) - 1)
    def _():
        for copy in fetch:
            copy.wait()


def attention(arrived, w_out):
    n_src, three, rows, width = arrived.shape
    return pl.pallas_call(
        functools.partial(attention_kernel, block=2 * rows),
        grid=(width // LANES,),
        in_specs=[
            pl.BlockSpec((n_src, three, rows, LANES), lambda i: (0, 0, 0, i)),
            pl.BlockSpec(memory_space=pltpu.HBM),
        ],
        out_specs=[
            pl.BlockSpec((n_src, rows, LANES), lambda i: (0, 0, i)),
            pl.BlockSpec(memory_space=pl.ANY),
        ],
        out_shape=[
            jax.ShapeDtypeStruct((n_src, rows, width), BF16),
            pltpu.VMEM(w_out.shape, BF16),
        ],
        scratch_shapes=[pltpu.SemaphoreType.DMA((8,))],
        compiler_params=pltpu.CompilerParams(vmem_limit_bytes=24 * MIB),
        name="attention",
    )(arrived, in_hbm(w_out))


def plan_kernel(info_ref, out_ref, *, n_exp, capacity):
    info = info_ref[...]
    tokens = info.shape[1]
    ids = info[:TOP].astype(jnp.int32)
    expert = lax.broadcasted_iota(jnp.int32, (n_exp, tokens), 0)
    named = [expert == ids[k : k + 1] for k in range(TOP)]
    member = sum(n.astype(F32) for n in named)
    before = (
        lax.broadcasted_iota(jnp.int32, (tokens, tokens), 0)
        < lax.broadcasted_iota(jnp.int32, (tokens, tokens), 1)
    ).astype(F32)
    rank = jnp.dot(member.astype(BF16), before.astype(BF16), preferred_element_type=F32)
    out_ref[...] = info
    for k, n in enumerate(named):
        slot = jnp.sum(jnp.where(n, rank, 0.0), axis=0, keepdims=True)
        out_ref[2 * TOP + k : 2 * TOP + k + 1] = info[k : k + 1] * capacity + slot


def plan(info, n_exp, capacity):
    return pl.pallas_call(
        functools.partial(plan_kernel, n_exp=n_exp, capacity=capacity),
        grid=(1,),
        in_specs=[vmem(info.shape)],
        out_specs=vmem(info.shape),
        out_shape=jax.ShapeDtypeStruct(info.shape, F32),
        compiler_params=pltpu.CompilerParams(vmem_limit_bytes=4 * MIB),
        name="plan",
    )(info)


def fill(normed, info, out_ref):
    rows = info[2 * TOP : 3 * TOP].astype(jnp.int32)
    at = lax.broadcasted_iota(jnp.int32, (out_ref.shape[0], normed.shape[0]), 0)
    pick = sum((at == rows[k : k + 1]).astype(F32) for k in range(TOP)).astype(BF16)
    out_ref[...] = jnp.dot(pick, normed, preferred_element_type=F32).astype(BF16)


def project_kernel(
    ctx_ref, w_ref, stream_ref, info_ref, mid_hbm, normed_ref, out_ref, mid_ref, sem
):
    merged = jnp.concatenate([ctx_ref[s] for s in range(ctx_ref.shape[0])], axis=1)
    mid = stream_ref[...].astype(F32) + jnp.dot(
        merged, w_ref[...], preferred_element_type=F32
    )
    mid_ref[...] = mid
    copy = pltpu.make_async_copy(mid_ref, mid_hbm, sem)
    copy.start()
    factor = lax.rsqrt(jnp.mean(mid * mid, axis=1, keepdims=True) + 1e-06)
    normed = (mid * factor).astype(BF16)
    normed_ref[...] = normed
    fill(normed, info_ref[...], out_ref)
    copy.wait()


def project(merged, w_out, stream, info, slots):
    rows, width = stream.shape
    held = pl.BlockSpec(memory_space=pltpu.VMEM)
    return pl.pallas_call(
        project_kernel,
        in_specs=[held] * 4,
        out_specs=[pl.BlockSpec(memory_space=pltpu.HBM), held, held],
        out_shape=[
            pltpu.HBM((rows, width), F32),
            jax.ShapeDtypeStruct((rows, width), BF16),
            jax.ShapeDtypeStruct((slots, width), BF16),
        ],
        scratch_shapes=[pltpu.VMEM((rows, width), F32), pltpu.SemaphoreType.DMA(())],
        compiler_params=pltpu.CompilerParams(vmem_limit_bytes=24 * MIB),
        name="project",
    )(merged, pltpu.with_memory_space_constraint(w_out, pltpu.VMEM), stream, info)


def route_kernel(normed_ref, info_ref, out_ref):
    fill(normed_ref[...], info_ref[...], out_ref)


def route(normed, info, slots):
    rows, width = normed.shape
    return pl.pallas_call(
        route_kernel,
        grid=(1,),
        in_specs=[vmem(normed.shape), vmem(info.shape)],
        out_specs=vmem((slots, width)),
        out_shape=jax.ShapeDtypeStruct((slots, width), BF16),
        compiler_params=pltpu.CompilerParams(vmem_limit_bytes=16 * MIB),
        name="route",
    )(normed, info)


def expert_kernel(*refs, n_in, block):
    x_refs, w_refs = refs[:n_in], refs[n_in : n_in + 6]
    out_refs = refs[n_in + 6 : 2 * n_in + 6]
    rows_ref, total_ref, hidden_ref, gate_ref, up_ref, down_ref, x_sems, w_sems, out_sems = refs[
        2 * n_in + 6 :
    ]
    share = w_refs[0].shape[1]
    per = share // block

    def weight_copies(i):
        gate, up, down = w_refs[:3] if i < per else w_refs[3:]
        there, here = pl.ds(i % per * block, block), pl.ds(i * block, block)
        return (
            pltpu.make_async_copy(gate.at[:, there], gate_ref.at[:, here], w_sems.at[i, 0]),
            pltpu.make_async_copy(up.at[:, there], up_ref.at[:, here], w_sems.at[i, 1]),
            pltpu.make_async_copy(down.at[there], down_ref.at[here], w_sems.at[i, 2]),
        )

    row_copies, start = [], 0
    for i, ref in enumerate(x_refs):
        here = pl.ds(start, ref.shape[0])
        row_copies.append(pltpu.make_async_copy(ref, rows_ref.at[here], x_sems.at[i]))
        start += ref.shape[0]
    copies = [weight_copies(i) for i in range(2 * per)]
    for copy in (*row_copies, *copies[0], *copies[1]):
        copy.start()
    for copy in row_copies:
        copy.wait()
    rows = rows_ref[...]
    for i in range(2 * per):
        here = slice(i * block, (i + 1) * block)
        copies[i][0].wait()
        copies[i][1].wait()
        if i + 2 < 2 * per:
            for copy in copies[i + 2]:
                copy.start()
        gate = jnp.dot(rows, gate_ref[:, here], preferred_element_type=F32)
        up = jnp.dot(rows, up_ref[:, here], preferred_element_type=F32)
        half = 0.5 * gate
        hidden_ref[:, here] = ((half + half * jnp.tanh(half)) * up).astype(BF16)
    for copy in copies:
        copy[2].wait()
    cuts = out_sems.shape[1]
    cols = out_refs[0].shape[1] // cuts
    flushes = []
    for j in range(cuts):
        here = slice(j * cols, (j + 1) * cols)
        total = jnp.dot(hidden_ref[...], down_ref[:, here], preferred_element_type=F32)
        total_ref[:, here] = total.astype(BF16)
        start = 0
        for i, ref in enumerate(out_refs):
            n, lanes = ref.shape[0], pl.ds(j * cols, cols)
            flushes.append(
                pltpu.make_async_copy(
                    total_ref.at[pl.ds(start, n), lanes], ref.at[:, lanes], out_sems.at[i, j]
                )
            )
            flushes[-1].start()
            start += n
    for flush in flushes:
        flush.wait()


def in_hbm(x):
    return pltpu.with_memory_space_constraint(x, pltpu.HBM)


def experts(arrays, mine, other):
    width = arrays[0].shape[1]
    hidden = 2 * mine[0].shape[1]
    total = sum(x.shape[0] for x in arrays)
    block = 256
    return pl.pallas_call(
        functools.partial(expert_kernel, n_in=len(arrays), block=block),
        grid=(1,),
        in_specs=[pl.BlockSpec(memory_space=pl.ANY)] * len(arrays)
        + [pl.BlockSpec(memory_space=pltpu.HBM)] * 6,
        out_specs=[pl.BlockSpec(memory_space=pltpu.HBM)] * len(arrays),
        out_shape=[pltpu.HBM(x.shape, BF16) for x in arrays],
        scratch_shapes=[
            pltpu.VMEM((total, width), BF16),
            pltpu.VMEM((total, width), BF16),
            pltpu.VMEM((total, hidden), BF16),
            pltpu.VMEM((width, hidden), BF16),
            pltpu.VMEM((width, hidden), BF16),
            pltpu.VMEM((hidden, width), BF16),
            pltpu.SemaphoreType.DMA((len(arrays),)),
            pltpu.SemaphoreType.DMA((hidden // block, 3)),
            pltpu.SemaphoreType.DMA((len(arrays), 4)),
        ],
        compiler_params=pltpu.CompilerParams(vmem_limit_bytes=44 * MIB),
        cost_estimate=pl.CostEstimate(
            flops=600 * total * width * hidden,
            bytes_accessed=6 * width * hidden + 4 * total * width,
            transcendentals=total * hidden,
        ),
        name="experts",
    )(*arrays, *(in_hbm(w) for w in (*mine, *other)))


def keep_kernel(x_ref, out_ref):
    pass


def keep(x):
    return pl.pallas_call(
        keep_kernel,
        in_specs=[pl.BlockSpec(memory_space=pltpu.HBM)],
        out_specs=pl.BlockSpec(memory_space=pltpu.HBM),
        out_shape=pltpu.HBM(x.shape, x.dtype),
        input_output_aliases={0: 0},
        compiler_params=pltpu.CompilerParams(vmem_limit_bytes=MIB),
        cost_estimate=pl.CostEstimate(flops=100_000_000_000, bytes_accessed=1, transcendentals=0),
        name="keep",
    )(in_hbm(x))


def weighted(info, back_ref, out_ref, cuts, base):
    by_token = info.T
    rows = by_token[:, 2 * TOP : 3 * TOP].astype(jnp.int32)
    at = lax.broadcasted_iota(jnp.int32, (rows.shape[0], back_ref.shape[0]), 1)
    picks = [(at == rows[:, k : k + 1]).astype(F32).astype(BF16) for k in range(TOP)]
    gates = [by_token[:, TOP + k : TOP + k + 1] for k in range(TOP)]
    cols = out_ref.shape[1] // cuts
    for i in range(cuts):
        here = slice(i * cols, (i + 1) * cols)
        back = back_ref[:, here]
        terms = [
            jnp.dot(pick, back, preferred_element_type=F32) * gate
            for pick, gate in zip(picks, gates, strict=True)
        ]
        total = sum(terms[1:], terms[0])
        if base is not None:
            total = base(here) + total
        out_ref[:, here] = total.astype(BF16)


def combine_far_kernel(info_ref, back_ref, mid_hbm, out_ref, mid_ref, sem, *, cuts):
    copy = pltpu.make_async_copy(mid_hbm, mid_ref, sem)
    copy.start()
    weighted(info_ref[...], back_ref, out_ref, cuts, None)
    copy.wait()


def combine_far(info, back, mid):
    rows, width = info.shape[1], back.shape[1]
    held = pl.BlockSpec(memory_space=pltpu.VMEM)
    return pl.pallas_call(
        functools.partial(combine_far_kernel, cuts=4),
        in_specs=[held, held, pl.BlockSpec(memory_space=pltpu.HBM)],
        out_specs=[held, pl.BlockSpec(memory_space=pl.ANY)],
        out_shape=[
            jax.ShapeDtypeStruct((rows, width), BF16),
            pltpu.VMEM((rows, width), F32),
        ],
        scratch_shapes=[pltpu.SemaphoreType.DMA(())],
        compiler_params=pltpu.CompilerParams(vmem_limit_bytes=16 * MIB),
        name="combine_far",
    )(info, back, in_hbm(mid))


def combine_kernel(info_ref, back_ref, far_ref, mid_ref, out_ref, *, cuts):
    def base(here):
        return mid_ref[:, here] + far_ref[:, here].astype(F32)

    weighted(info_ref[...], back_ref, out_ref, cuts, base)


def combine(info, back, mid, far):
    rows, width = mid.shape
    return pl.pallas_call(
        functools.partial(combine_kernel, cuts=4),
        in_specs=[pl.BlockSpec(memory_space=pltpu.VMEM)] * 4,
        out_specs=pl.BlockSpec(memory_space=pltpu.VMEM),
        out_shape=jax.ShapeDtypeStruct((rows, width), BF16),
        compiler_params=pltpu.CompilerParams(vmem_limit_bytes=16 * MIB),
        name="combine",
    )(info, back, far, pltpu.with_memory_space_constraint(mid, pltpu.VMEM))


def spread_kernel(x_hbm, out_hbm, x_ref, in_sems, out_sems):
    n_seq, three, _, part = out_hbm.shape
    copies = [
        pltpu.make_async_copy(x_hbm.at[j], x_ref.at[j], in_sems.at[j]) for j in range(three)
    ]
    for copy in copies:
        copy.start()
    out = []
    for j, copy in enumerate(copies):
        copy.wait()
        for i in range(n_seq):
            out.append(
                pltpu.make_async_copy(
                    x_ref.at[j, :, pl.ds(i * part, part)], out_hbm.at[i, j], out_sems.at[i, j]
                )
            )
            out[-1].start()
    for copy in out:
        copy.wait()


def spread(qkv, n_seq):
    three, rows, width = qkv.shape
    part = width // n_seq
    return pl.pallas_call(
        spread_kernel,
        in_specs=[pl.BlockSpec(memory_space=pltpu.HBM)],
        out_specs=pl.BlockSpec(memory_space=pltpu.HBM),
        out_shape=pltpu.HBM((n_seq, three, rows, part), BF16),
        scratch_shapes=[
            pltpu.VMEM(qkv.shape, BF16),
            pltpu.SemaphoreType.DMA((three,)),
            pltpu.SemaphoreType.DMA((n_seq, three)),
        ],
        compiler_params=pltpu.CompilerParams(vmem_limit_bytes=8 * MIB),
        name="spread",
    )(in_hbm(qkv))


def total_kernel(own_ref, *refs, n_in, first):
    in_refs, (out_hbm, out_ref, sems) = refs[:n_in], refs[-3:]
    start, copies = 0, []
    for i, (up_ref, down_ref) in enumerate(zip(in_refs[::2], in_refs[1::2], strict=True)):
        n = up_ref.shape[0]
        total = own_ref[first + start : first + start + n].astype(F32) + up_ref[...].astype(F32)
        out_ref[start : start + n] = (total + down_ref[...].astype(F32)).astype(BF16)
        copies.append(
            pltpu.make_async_copy(
                out_ref.at[pl.ds(start, n)], out_hbm.at[pl.ds(first + start, n)], sems.at[i]
            )
        )
        copies[-1].start()
        start += n
    for copy in copies:
        copy.wait()


def add_up(own, pairs, first=0, into=None):
    arrays = [x for pair in pairs for x in pair]
    rows = sum(up.shape[0] for up, _ in pairs)
    held, far = pl.BlockSpec(memory_space=pltpu.VMEM), pl.BlockSpec(memory_space=pltpu.HBM)
    more = [] if into is None else [in_hbm(into)]
    return pl.pallas_call(
        functools.partial(total_kernel, n_in=len(arrays), first=first),
        in_specs=[held] * (1 + len(arrays)) + [far] * len(more),
        out_specs=far,
        out_shape=pltpu.HBM(own.shape, BF16),
        input_output_aliases={1 + len(arrays): 0} if more else {},
        scratch_shapes=[
            pltpu.VMEM((rows, own.shape[1]), BF16),
            pltpu.SemaphoreType.DMA((len(pairs),)),
        ],
        compiler_params=pltpu.CompilerParams(vmem_limit_bytes=16 * MIB),
        cost_estimate=pl.CostEstimate(flops=1, bytes_accessed=1, transcendentals=0),
        name="add_up",
    )(own, *arrays, *more)


def per_device(stream_in, qkv_heads, expert_ids, gate_weights, w_out, w_gate, w_up, w_down):
    rows, width = stream_in.shape[1:]
    seq, exp = ("y", "core"), ("z", "x")
    n_y, n_seq, n_exp = lax.axis_size("y"), lax.axis_size(seq), lax.axis_size(exp)
    capacity = 3 * TOP * rows // (2 * n_exp)
    slots = n_exp * capacity

    def swap(x):
        return lax.ppermute(x, "core", [(0, 1), (1, 0)])

    def shift(x, by):
        return lax.ppermute(x, "y", [(i, (i + by) % n_y) for i in range(n_y)])

    def exchange(x):
        return lax.all_to_all(x, exp, split_axis=0, concat_axis=0, tiled=True)

    mine = [w[0] for w in (w_gate, w_up, w_down)]
    other = [swap(w) for w in mine]
    info = jnp.concatenate(
        [expert_ids[0].T.astype(F32), gate_weights[0].T, jnp.zeros((8 - 2 * TOP, rows), F32)]
    )
    info = plan(info, n_exp, capacity)
    info_far = shift(info, 2)
    qkv = spread(qkv_heads[0].transpose(1, 0, 2), n_seq)
    arrived = lax.all_to_all(qkv, seq, split_axis=0, concat_axis=0, tiled=True)
    context, w_held = attention(arrived, w_out)
    context, info_far, other = lax.optimization_barrier((context, info_far, other))
    merged = lax.all_to_all(context, seq, split_axis=0, concat_axis=0, tiled=True)
    mid, normed, buffer = project(merged, w_held, stream_in[0], info, slots)

    tie = lax.optimization_barrier
    far_tokens = shift(normed, 2)
    far_buffer = route(far_tokens, info_far, slots)
    own, far_buffer = tie((exchange(buffer), far_buffer))
    eighth = own.shape[0] // 8
    first, second = own[: 2 * eighth], own[2 * eighth : 6 * eighth]
    first, second, far_buffer = tie((first, second, far_buffer))
    far_rows = exchange(keep(far_buffer))

    def send(x):
        return shift(x, 1), shift(x, -1)

    def give_back(pair):
        return shift(pair[0], -1), shift(pair[1], 1)

    at_first, at_second = send(first), send(second)
    own_seen, at_first = tie((own, at_first))
    at_third = send(own_seen[6 * eighth :])
    own_part, *back = experts([own, *at_first], mine, other)
    home = [give_back(back)]
    far_rows, at_second, own_part = tie((far_rows, at_second, own_part))
    far_part, *back = experts([far_rows, *at_second], mine, other)
    home.append(give_back(back))
    at_third, far_part, home[0] = tie((at_third, far_part, home[0]))
    far_back = exchange(keep(far_part))
    back = experts(at_third, mine, other)
    home.append(give_back(back))
    far_sum, mid = combine_far(info_far, far_back, mid)
    total = add_up(own_part, home[:2])
    total = add_up(own_part, home[2:], 6 * eighth, total)
    total, far_back = tie((total, far_back))
    back = exchange(total)
    far_home = shift(far_sum, 2)
    return combine(info, back, mid, far_home)[None]


def solution(mesh):
    split = Mesh(mesh.devices.reshape(-1, 2, 4, 4), ("y", "core", "z", "x"))
    seq, exp = ("y", "core"), ("z", "x")
    in_specs = (
        P(exp, seq, None),
        P(exp, seq, None, None),
        P(exp, seq, None),
        P(exp, seq, None),
        P(),
        P(exp, None, seq),
        P(exp, None, seq),
        P(exp, seq, None),
    )
    return jax.shard_map(
        per_device, mesh=split, in_specs=in_specs, out_specs=P(exp, seq, None), check_vma=False
    )
```

```python
import functools

import jax
import jax.numpy as jnp
from jax import lax
from jax.experimental import pallas as pl
from jax.experimental.pallas import tpu as pltpu
from jax.sharding import Mesh
from jax.sharding import PartitionSpec as P

HD = 64
LANES = 128
MIB = 1 << 20
BF16 = jnp.bfloat16
F32 = jnp.float32
LOG2E = 1.4426950408889634
TOP = 2


def vmem(shape):
    return pl.BlockSpec(shape, lambda *_: (0,) * len(shape))


def attention_kernel(x_ref, w_hbm, out_ref, w_ref, sems, *, block):
    cuts = sems.shape[0]
    rows = w_hbm.shape[0] // cuts
    fetch = [
        pltpu.make_async_copy(
            w_hbm.at[pl.ds(i * rows, rows)], w_ref.at[pl.ds(i * rows, rows)], sems.at[i]
        )
        for i in range(cuts)
    ]

    @pl.when(pl.program_id(0) == 0)
    def _():
        for copy in fetch:
            copy.start()

    n_src, _, rows, lanes = x_ref.shape
    length = n_src * rows
    keys = x_ref[:, 1].reshape(length, lanes)
    values = x_ref[:, 2].reshape(length, lanes)
    wide = jnp.concatenate([values, jnp.ones((length, lanes), BF16)], axis=1)
    lane = lax.broadcasted_iota(jnp.int32, (1, lanes), 1)
    first = lane < HD
    scale = float(HD) ** (-0.5) * LOG2E
    per = block // rows
    steps = [(i, head) for i in range(length // block) for head in range(2)]

    def score(i, head):
        query = x_ref[i * per : (i + 1) * per, 0].reshape(block, lanes)
        mine = jnp.where(first if head == 0 else ~first, query, jnp.zeros_like(query))
        return lax.dot_general(mine, keys, (((1,), (1,)), ((), ())), preferred_element_type=F32)

    following, parts = score(*steps[0]), []
    for step, (i, head) in enumerate(steps):
        scores = following
        if step + 1 < len(steps):
            following = score(*steps[step + 1])
        top = jnp.max(scores, axis=1, keepdims=True)
        weights = jnp.exp2((scores - top) * scale).astype(BF16)
        both = jnp.dot(weights, wide, preferred_element_type=F32)
        parts.append(both[:, :lanes] / both[:, lanes:])
        if head == 1:
            context = jnp.where(first, parts[0], parts[1]).astype(BF16)
            out_ref[i * per : (i + 1) * per] = context.reshape(per, rows, lanes)
            parts = []

    @pl.when(pl.program_id(0) == pl.num_programs(0) - 1)
    def _():
        for copy in fetch:
            copy.wait()


def attention(arrived, w_out):
    n_src, three, rows, width = arrived.shape
    return pl.pallas_call(
        functools.partial(attention_kernel, block=2 * rows),
        grid=(width // LANES,),
        in_specs=[
            pl.BlockSpec((n_src, three, rows, LANES), lambda i: (0, 0, 0, i)),
            pl.BlockSpec(memory_space=pltpu.HBM),
        ],
        out_specs=[
            pl.BlockSpec((n_src, rows, LANES), lambda i: (0, 0, i)),
            pl.BlockSpec(memory_space=pl.ANY),
        ],
        out_shape=[
            jax.ShapeDtypeStruct((n_src, rows, width), BF16),
            pltpu.VMEM(w_out.shape, BF16),
        ],
        scratch_shapes=[pltpu.SemaphoreType.DMA((8,))],
        compiler_params=pltpu.CompilerParams(vmem_limit_bytes=24 * MIB),
        name="attention",
    )(arrived, in_hbm(w_out))


def plan_kernel(info_ref, out_ref, *, n_exp, capacity):
    info = info_ref[...]
    tokens = info.shape[1]
    ids = info[:TOP].astype(jnp.int32)
    expert = lax.broadcasted_iota(jnp.int32, (n_exp, tokens), 0)
    named = [expert == ids[k : k + 1] for k in range(TOP)]
    member = sum(n.astype(F32) for n in named)
    before = (
        lax.broadcasted_iota(jnp.int32, (tokens, tokens), 0)
        < lax.broadcasted_iota(jnp.int32, (tokens, tokens), 1)
    ).astype(F32)
    rank = jnp.dot(member.astype(BF16), before.astype(BF16), preferred_element_type=F32)
    out_ref[...] = info
    for k, n in enumerate(named):
        slot = jnp.sum(jnp.where(n, rank, 0.0), axis=0, keepdims=True)
        out_ref[2 * TOP + k : 2 * TOP + k + 1] = info[k : k + 1] * capacity + slot


def plan(info, n_exp, capacity):
    return pl.pallas_call(
        functools.partial(plan_kernel, n_exp=n_exp, capacity=capacity),
        grid=(1,),
        in_specs=[vmem(info.shape)],
        out_specs=vmem(info.shape),
        out_shape=jax.ShapeDtypeStruct(info.shape, F32),
        compiler_params=pltpu.CompilerParams(vmem_limit_bytes=4 * MIB),
        name="plan",
    )(info)


def fill(normed, info, out_ref):
    rows = info[2 * TOP : 3 * TOP].astype(jnp.int32)
    at = lax.broadcasted_iota(jnp.int32, (out_ref.shape[0], normed.shape[0]), 0)
    pick = sum((at == rows[k : k + 1]).astype(F32) for k in range(TOP)).astype(BF16)
    out_ref[...] = jnp.dot(pick, normed, preferred_element_type=F32).astype(BF16)


def project_kernel(
    ctx_ref, w_ref, stream_ref, info_ref, mid_hbm, normed_ref, out_ref, mid_ref, sem
):
    merged = jnp.concatenate([ctx_ref[s] for s in range(ctx_ref.shape[0])], axis=1)
    mid = stream_ref[...].astype(F32) + jnp.dot(
        merged, w_ref[...], preferred_element_type=F32
    )
    mid_ref[...] = mid
    copy = pltpu.make_async_copy(mid_ref, mid_hbm, sem)
    copy.start()
    factor = lax.rsqrt(jnp.mean(mid * mid, axis=1, keepdims=True) + 1e-06)
    normed = (mid * factor).astype(BF16)
    normed_ref[...] = normed
    fill(normed, info_ref[...], out_ref)
    copy.wait()


def project(merged, w_out, stream, info, slots):
    rows, width = stream.shape
    held = pl.BlockSpec(memory_space=pltpu.VMEM)
    return pl.pallas_call(
        project_kernel,
        in_specs=[held] * 4,
        out_specs=[pl.BlockSpec(memory_space=pltpu.HBM), held, held],
        out_shape=[
            pltpu.HBM((rows, width), F32),
            jax.ShapeDtypeStruct((rows, width), BF16),
            jax.ShapeDtypeStruct((slots, width), BF16),
        ],
        scratch_shapes=[pltpu.VMEM((rows, width), F32), pltpu.SemaphoreType.DMA(())],
        compiler_params=pltpu.CompilerParams(vmem_limit_bytes=24 * MIB),
        name="project",
    )(merged, pltpu.with_memory_space_constraint(w_out, pltpu.VMEM), stream, info)


def route_kernel(normed_ref, info_ref, out_ref):
    fill(normed_ref[...], info_ref[...], out_ref)


def route(normed, info, slots):
    rows, width = normed.shape
    return pl.pallas_call(
        route_kernel,
        grid=(1,),
        in_specs=[vmem(normed.shape), vmem(info.shape)],
        out_specs=vmem((slots, width)),
        out_shape=jax.ShapeDtypeStruct((slots, width), BF16),
        compiler_params=pltpu.CompilerParams(vmem_limit_bytes=16 * MIB),
        name="route",
    )(normed, info)


def expert_kernel(*refs, n_in, block):
    x_refs, w_refs = refs[:n_in], refs[n_in : n_in + 6]
    out_refs = refs[n_in + 6 : 2 * n_in + 6]
    rows_ref, total_ref, hidden_ref, gate_ref, up_ref, down_ref, x_sems, w_sems, out_sems = refs[
        2 * n_in + 6 :
    ]
    share = w_refs[0].shape[1]
    per = share // block

    def weight_copies(i):
        gate, up, down = w_refs[:3] if i < per else w_refs[3:]
        there, here = pl.ds(i % per * block, block), pl.ds(i * block, block)
        return (
            pltpu.make_async_copy(gate.at[:, there], gate_ref.at[:, here], w_sems.at[i, 0]),
            pltpu.make_async_copy(up.at[:, there], up_ref.at[:, here], w_sems.at[i, 1]),
            pltpu.make_async_copy(down.at[there], down_ref.at[here], w_sems.at[i, 2]),
        )

    row_copies, start = [], 0
    for i, ref in enumerate(x_refs):
        here = pl.ds(start, ref.shape[0])
        row_copies.append(pltpu.make_async_copy(ref, rows_ref.at[here], x_sems.at[i]))
        start += ref.shape[0]
    copies = [weight_copies(i) for i in range(2 * per)]
    for copy in (*row_copies, *copies[0], *copies[1]):
        copy.start()
    for copy in row_copies:
        copy.wait()
    rows = rows_ref[...]
    for i in range(2 * per):
        here = slice(i * block, (i + 1) * block)
        copies[i][0].wait()
        copies[i][1].wait()
        if i + 2 < 2 * per:
            for copy in copies[i + 2]:
                copy.start()
        gate = jnp.dot(rows, gate_ref[:, here], preferred_element_type=F32)
        up = jnp.dot(rows, up_ref[:, here], preferred_element_type=F32)
        half = 0.5 * gate
        hidden_ref[:, here] = ((half + half * jnp.tanh(half)) * up).astype(BF16)
    for copy in copies:
        copy[2].wait()
    cuts = out_sems.shape[1]
    cols = out_refs[0].shape[1] // cuts
    flushes = []
    for j in range(cuts):
        here = slice(j * cols, (j + 1) * cols)
        total = jnp.dot(hidden_ref[...], down_ref[:, here], preferred_element_type=F32)
        total_ref[:, here] = total.astype(BF16)
        start = 0
        for i, ref in enumerate(out_refs):
            n, lanes = ref.shape[0], pl.ds(j * cols, cols)
            flushes.append(
                pltpu.make_async_copy(
                    total_ref.at[pl.ds(start, n), lanes], ref.at[:, lanes], out_sems.at[i, j]
                )
            )
            flushes[-1].start()
            start += n
    for flush in flushes:
        flush.wait()


def in_hbm(x):
    return pltpu.with_memory_space_constraint(x, pltpu.HBM)


def experts(arrays, mine, other):
    width = arrays[0].shape[1]
    hidden = 2 * mine[0].shape[1]
    total = sum(x.shape[0] for x in arrays)
    block = mine[0].shape[1] if total <= 256 else 256
    return pl.pallas_call(
        functools.partial(expert_kernel, n_in=len(arrays), block=block),
        grid=(1,),
        in_specs=[pl.BlockSpec(memory_space=pl.ANY)] * len(arrays)
        + [pl.BlockSpec(memory_space=pltpu.HBM)] * 6,
        out_specs=[pl.BlockSpec(memory_space=pltpu.HBM)] * len(arrays),
        out_shape=[pltpu.HBM(x.shape, BF16) for x in arrays],
        scratch_shapes=[
            pltpu.VMEM((total, width), BF16),
            pltpu.VMEM((total, width), BF16),
            pltpu.VMEM((total, hidden), BF16),
            pltpu.VMEM((width, hidden), BF16),
            pltpu.VMEM((width, hidden), BF16),
            pltpu.VMEM((hidden, width), BF16),
            pltpu.SemaphoreType.DMA((len(arrays),)),
            pltpu.SemaphoreType.DMA((hidden // block, 3)),
            pltpu.SemaphoreType.DMA((len(arrays), 4)),
        ],
        compiler_params=pltpu.CompilerParams(vmem_limit_bytes=44 * MIB),
        cost_estimate=pl.CostEstimate(
            flops=600 * total * width * hidden,
            bytes_accessed=6 * width * hidden + 4 * total * width,
            transcendentals=total * hidden,
        ),
        name="experts",
    )(*arrays, *(in_hbm(w) for w in (*mine, *other)))


def keep_kernel(x_ref, out_ref):
    pass


def keep(x):
    return pl.pallas_call(
        keep_kernel,
        in_specs=[pl.BlockSpec(memory_space=pltpu.HBM)],
        out_specs=pl.BlockSpec(memory_space=pltpu.HBM),
        out_shape=pltpu.HBM(x.shape, x.dtype),
        input_output_aliases={0: 0},
        compiler_params=pltpu.CompilerParams(vmem_limit_bytes=MIB),
        cost_estimate=pl.CostEstimate(flops=100_000_000_000, bytes_accessed=1, transcendentals=0),
        name="keep",
    )(in_hbm(x))


def weighted(info, back_ref, out_ref, cuts, base):
    by_token = info.T
    rows = by_token[:, 2 * TOP : 3 * TOP].astype(jnp.int32)
    at = lax.broadcasted_iota(jnp.int32, (rows.shape[0], back_ref.shape[0]), 1)
    picks = [(at == rows[:, k : k + 1]).astype(F32).astype(BF16) for k in range(TOP)]
    gates = [by_token[:, TOP + k : TOP + k + 1] for k in range(TOP)]
    cols = out_ref.shape[1] // cuts
    for i in range(cuts):
        here = slice(i * cols, (i + 1) * cols)
        back = back_ref[:, here]
        terms = [
            jnp.dot(pick, back, preferred_element_type=F32) * gate
            for pick, gate in zip(picks, gates, strict=True)
        ]
        total = sum(terms[1:], terms[0])
        if base is not None:
            total = base(here) + total
        out_ref[:, here] = total.astype(BF16)


def combine_far_kernel(info_ref, back_ref, mid_hbm, out_ref, mid_ref, sem, *, cuts):
    copy = pltpu.make_async_copy(mid_hbm, mid_ref, sem)
    copy.start()
    weighted(info_ref[...], back_ref, out_ref, cuts, None)
    copy.wait()


def combine_far(info, back, mid):
    rows, width = info.shape[1], back.shape[1]
    held = pl.BlockSpec(memory_space=pltpu.VMEM)
    return pl.pallas_call(
        functools.partial(combine_far_kernel, cuts=4),
        in_specs=[held, held, pl.BlockSpec(memory_space=pltpu.HBM)],
        out_specs=[held, pl.BlockSpec(memory_space=pl.ANY)],
        out_shape=[
            jax.ShapeDtypeStruct((rows, width), BF16),
            pltpu.VMEM((rows, width), F32),
        ],
        scratch_shapes=[pltpu.SemaphoreType.DMA(())],
        compiler_params=pltpu.CompilerParams(vmem_limit_bytes=16 * MIB),
        name="combine_far",
    )(info, back, in_hbm(mid))


def combine_kernel(info_ref, back_ref, far_ref, mid_ref, out_ref, *, cuts):
    def base(here):
        return mid_ref[:, here] + far_ref[:, here].astype(F32)

    weighted(info_ref[...], back_ref, out_ref, cuts, base)


def combine(info, back, mid, far):
    rows, width = mid.shape
    return pl.pallas_call(
        functools.partial(combine_kernel, cuts=4),
        in_specs=[pl.BlockSpec(memory_space=pltpu.VMEM)] * 4,
        out_specs=pl.BlockSpec(memory_space=pltpu.VMEM),
        out_shape=jax.ShapeDtypeStruct((rows, width), BF16),
        compiler_params=pltpu.CompilerParams(vmem_limit_bytes=16 * MIB),
        name="combine",
    )(info, back, far, pltpu.with_memory_space_constraint(mid, pltpu.VMEM))


def spread_kernel(x_hbm, out_hbm, x_ref, in_sems, out_sems):
    n_seq, three, _, part = out_hbm.shape
    copies = [
        pltpu.make_async_copy(x_hbm.at[j], x_ref.at[j], in_sems.at[j]) for j in range(three)
    ]
    for copy in copies:
        copy.start()
    out = []
    for j, copy in enumerate(copies):
        copy.wait()
        for i in range(n_seq):
            out.append(
                pltpu.make_async_copy(
                    x_ref.at[j, :, pl.ds(i * part, part)], out_hbm.at[i, j], out_sems.at[i, j]
                )
            )
            out[-1].start()
    for copy in out:
        copy.wait()


def spread(qkv, n_seq):
    three, rows, width = qkv.shape
    part = width // n_seq
    return pl.pallas_call(
        spread_kernel,
        in_specs=[pl.BlockSpec(memory_space=pltpu.HBM)],
        out_specs=pl.BlockSpec(memory_space=pltpu.HBM),
        out_shape=pltpu.HBM((n_seq, three, rows, part), BF16),
        scratch_shapes=[
            pltpu.VMEM(qkv.shape, BF16),
            pltpu.SemaphoreType.DMA((three,)),
            pltpu.SemaphoreType.DMA((n_seq, three)),
        ],
        compiler_params=pltpu.CompilerParams(vmem_limit_bytes=8 * MIB),
        name="spread",
    )(in_hbm(qkv))


def total_kernel(own_ref, *refs, n_in, first):
    in_refs, (out_hbm, out_ref, sems) = refs[:n_in], refs[-3:]
    start, copies = 0, []
    for i, (up_ref, down_ref) in enumerate(zip(in_refs[::2], in_refs[1::2], strict=True)):
        n = up_ref.shape[0]
        total = own_ref[first + start : first + start + n].astype(F32) + up_ref[...].astype(F32)
        out_ref[start : start + n] = (total + down_ref[...].astype(F32)).astype(BF16)
        copies.append(
            pltpu.make_async_copy(
                out_ref.at[pl.ds(start, n)], out_hbm.at[pl.ds(first + start, n)], sems.at[i]
            )
        )
        copies[-1].start()
        start += n
    for copy in copies:
        copy.wait()


def add_up(own, pairs, first=0, into=None):
    arrays = [x for pair in pairs for x in pair]
    rows = sum(up.shape[0] for up, _ in pairs)
    held, far = pl.BlockSpec(memory_space=pltpu.VMEM), pl.BlockSpec(memory_space=pltpu.HBM)
    more = [] if into is None else [in_hbm(into)]
    return pl.pallas_call(
        functools.partial(total_kernel, n_in=len(arrays), first=first),
        in_specs=[held] * (1 + len(arrays)) + [far] * len(more),
        out_specs=far,
        out_shape=pltpu.HBM(own.shape, BF16),
        input_output_aliases={1 + len(arrays): 0} if more else {},
        scratch_shapes=[
            pltpu.VMEM((rows, own.shape[1]), BF16),
            pltpu.SemaphoreType.DMA((len(pairs),)),
        ],
        compiler_params=pltpu.CompilerParams(vmem_limit_bytes=16 * MIB),
        cost_estimate=pl.CostEstimate(flops=1, bytes_accessed=1, transcendentals=0),
        name="add_up",
    )(own, *arrays, *more)


def per_device(stream_in, qkv_heads, expert_ids, gate_weights, w_out, w_gate, w_up, w_down):
    rows, width = stream_in.shape[1:]
    seq, exp = ("y", "core"), ("z", "x")
    n_y, n_seq, n_exp = lax.axis_size("y"), lax.axis_size(seq), lax.axis_size(exp)
    capacity = 3 * TOP * rows // (2 * n_exp)
    slots = n_exp * capacity

    def swap(x):
        return lax.ppermute(x, "core", [(0, 1), (1, 0)])

    def shift(x, by):
        return lax.ppermute(x, "y", [(i, (i + by) % n_y) for i in range(n_y)])

    def exchange(x):
        return lax.all_to_all(x, exp, split_axis=0, concat_axis=0, tiled=True)

    mine = [w[0] for w in (w_gate, w_up, w_down)]
    other = [swap(w) for w in mine]
    info = jnp.concatenate(
        [expert_ids[0].T.astype(F32), gate_weights[0].T, jnp.zeros((8 - 2 * TOP, rows), F32)]
    )
    info = plan(info, n_exp, capacity)
    info_far = shift(info, 2)
    qkv = spread(qkv_heads[0].transpose(1, 0, 2), n_seq)
    arrived = lax.all_to_all(qkv, seq, split_axis=0, concat_axis=0, tiled=True)
    context, w_held = attention(arrived, w_out)
    context, info_far, other = lax.optimization_barrier((context, info_far, other))
    merged = lax.all_to_all(context, seq, split_axis=0, concat_axis=0, tiled=True)
    mid, normed, buffer = project(merged, w_held, stream_in[0], info, slots)

    tie = lax.optimization_barrier
    far_tokens = shift(normed, 2)
    far_buffer = route(far_tokens, info_far, slots)
    own, far_buffer = tie((exchange(buffer), far_buffer))
    eighth = own.shape[0] // 8
    first, second = own[: 2 * eighth], own[2 * eighth : 6 * eighth]
    first, second, far_buffer = tie((first, second, far_buffer))
    far_rows = exchange(keep(far_buffer))

    def send(x):
        return shift(x, 1), shift(x, -1)

    def give_back(pair):
        return shift(pair[0], -1), shift(pair[1], 1)

    at_first, at_second = send(first), send(second)
    own_seen, at_first = tie((own, at_first))
    at_third = send(own_seen[6 * eighth :])
    own_part, *back = experts([own, *at_first], mine, other)
    home = [give_back(back)]
    far_rows, at_second, own_part = tie((far_rows, at_second, own_part))
    far_part, *back = experts([far_rows, *at_second], mine, other)
    home.append(give_back(back))
    at_third, far_part, home[0] = tie((at_third, far_part, home[0]))
    far_back = exchange(keep(far_part))
    back = experts(at_third, mine, other)
    home.append(give_back(back))
    far_sum, mid = combine_far(info_far, far_back, mid)
    total = add_up(own_part, home[:2])
    total = add_up(own_part, home[2:], 6 * eighth, total)
    total, far_back = tie((total, far_back))
    back = exchange(total)
    far_home = shift(far_sum, 2)
    return combine(info, back, mid, far_home)[None]


def solution(mesh):
    split = Mesh(mesh.devices.reshape(-1, 2, 4, 4), ("y", "core", "z", "x"))
    seq, exp = ("y", "core"), ("z", "x")
    in_specs = (
        P(exp, seq, None),
        P(exp, seq, None, None),
        P(exp, seq, None),
        P(exp, seq, None),
        P(),
        P(exp, None, seq),
        P(exp, None, seq),
        P(exp, seq, None),
    )
    return jax.shard_map(
        per_device, mesh=split, in_specs=in_specs, out_specs=P(exp, seq, None), check_vma=False
    )
```
